128 devices in a mesh: ch: 32 (over z, y, core), img: 4 (over x).
Axes of the slice: x: 4, y: 4, z: 4, core: 2. Of those that a mesh axis runs over, the one named last changes fastest.
Arguments:
- features: bfloat16 [128, 165888], P('ch', 'img'), may hold values from -6 to 6
- size_group: int32 [128], P('img'), may hold values from 0 to 2
- cycle_offsets: int32 [2, 128], replicated, may hold values from -1 to 1
- norm_gain: bfloat16 [128], replicated, may hold values from 0.5 to 1.5
- norm_bias: bfloat16 [128], replicated, may hold values from -3 to 3
- height_weight: bfloat16 [128, 128], replicated, may hold values from -0.5 to 0.5
- height_bias: bfloat16 [128], replicated, may hold values from -3 to 3
- width_weight: bfloat16 [128, 128], replicated, may hold values from -0.5 to 0.5
- width_bias: bfloat16 [128], replicated, may hold values from -3 to 3
- channel_weight: bfloat16 [128, 128], replicated, may hold values from -0.5 to 0.5
- squeeze_weight: bfloat16 [128, 32], replicated, may hold values from -1.5 to 1.5
- squeeze_bias: bfloat16 [32], replicated, may hold values from -3 to 3
- excite_weight: bfloat16 [32, 384], replicated, may hold values from -1 to 1
- excite_bias: bfloat16 [384], replicated, may hold values from -3 to 3
- output_weight: bfloat16 [128, 128], replicated, may hold values from -0.75 to 0.75
- output_bias: bfloat16 [128], replicated, may hold values from -3 to 3
- second_gain: bfloat16 [128], replicated, may hold values from 0.5 to 1.5
- second_bias: bfloat16 [128], replicated, may hold values from -3 to 3
- expand_weight: bfloat16 [128, 512], replicated, may hold values from -0.5 to 0.5
- expand_bias: bfloat16 [512], replicated, may hold values from -3 to 3
- reduce_weight: bfloat16 [512, 128], replicated, may hold values from -0.375 to 0.375
- reduce_bias: bfloat16 [128], replicated, may hold values from -3 to 3
- stride_weight: bfloat16 [320, 9, 128], replicated, may hold values from -0.1875 to 0.1875
- stride_bias: bfloat16 [320], replicated, may hold values from -3 to 3
- cotangent: bfloat16 [320, 41472], P('ch', 'img'), may hold values from -6 to 6
Outputs:
- section_out: bfloat16 [320, 41472], P('ch', 'img')
- features_grad: float32 [128, 165888], P('ch', 'img')
- norm_gain_grad: float32 [128], replicated
- norm_bias_grad: float32 [128], replicated
- height_weight_grad: float32 [128, 128], replicated
- height_bias_grad: float32 [128], replicated
- width_weight_grad: float32 [128, 128], replicated
- width_bias_grad: float32 [128], replicated
- channel_weight_grad: float32 [128, 128], replicated
- squeeze_weight_grad: float32 [128, 32], replicated
- squeeze_bias_grad: float32 [32], replicated
- excite_weight_grad: float32 [32, 384], replicated
- excite_bias_grad: float32 [384], replicated
- output_weight_grad: float32 [128, 128], replicated
- output_bias_grad: float32 [128], replicated
- second_gain_grad: float32 [128], replicated
- second_bias_grad: float32 [128], replicated
- expand_weight_grad: float32 [128, 512], replicated
- expand_bias_grad: float32 [512], replicated
- reduce_weight_grad: float32 [512, 128], replicated
- reduce_bias_grad: float32 [128], replicated
- stride_weight_grad: float32 [320, 9, 128], replicated
- stride_bias_grad: float32 [320], replicated
The draws below stay inside these ranges and needn't reach their ends.
All inputs are finite; a program needn't handle non-finite values.
Results may differ from the reference program's by a relative error of at most 0.0078.
The reference program's roundings to bfloat16 on the way count: a program that leaves them out, or rounds other values in their place, can miss the bound.
Values may be sent and summed in bfloat16 or wider, within the bound.
No kernel may reach another device: no remote copies, remote signals or barrier semaphores. Data moves between devices by JAX's collectives and lax.ppermute only.
A program may use at most 128 MiB of HBM per device.

```python
import jax
import jax.numpy as jnp
from jax import lax

BLOCK_CHANNELS = 128
FF = 512
RED = 32
OUT = 320
CANVAS = 36
PIX = 1296
OPIX = 324
IMAGES = 128


def set_ends(entries, rng, low, top_value):
    spot = [jax.random.randint(jax.random.fold_in(rng, axis), (), 0, length) for axis, length in enumerate(entries.shape)]
    longest = entries.shape.index(max(entries.shape))
    neighbour = spot[:longest] + [(spot[longest] + 1) % entries.shape[longest]] + spot[longest + 1:]
    return entries.at[tuple(spot)].set(low).at[tuple(neighbour)].set(top_value)


def block_levels(own_key, shape, pieces, least, largest):
    level = 1.0
    for axis_at, blocks in pieces:
        steps = jax.random.uniform(jax.random.fold_in(jax.random.fold_in(own_key, 6), axis_at), (blocks,), jnp.float32, least / len(pieces), largest / len(pieces))
        level = level * jnp.repeat(jnp.exp(steps), shape[axis_at] // blocks).reshape((-1,) + (1,) * (len(shape) - 1 - axis_at))
    return level


def bell_draw(key, dims, deviation, most, cuts=(), kind=jnp.bfloat16):
    drawn = deviation * jax.random.normal(key, dims, jnp.float32)
    if cuts:
        drawn = drawn * block_levels(key, dims, cuts, -0.22, 0.18)
    return jnp.clip(drawn, -most, most).astype(kind)


def setup_inputs(seed: int = 0) -> dict:
    keys = jax.random.split(jax.random.key(seed), 26)
    features = bell_draw(keys[0], (BLOCK_CHANNELS, IMAGES * PIX), 1.0, 6.0, ((0, 32), (1, 4)))
    size_group = set_ends(jax.random.randint(keys[1], (IMAGES,), 0, 3), jax.random.fold_in(keys[1], 1), 0, 2).astype(jnp.int32)
    cycle_offsets = set_ends(jax.random.randint(keys[2], (2, BLOCK_CHANNELS), -1, 2), jax.random.fold_in(keys[2], 1), -1, 1).astype(jnp.int32)
    norm_gain = jnp.clip(1.0 + 0.1 * jax.random.normal(keys[3], (BLOCK_CHANNELS,), jnp.float32), 0.5, 1.5).astype(jnp.bfloat16)
    norm_bias = bell_draw(keys[4], (BLOCK_CHANNELS,), 0.5, 3.0)
    height_weight = bell_draw(keys[5], (BLOCK_CHANNELS, BLOCK_CHANNELS), BLOCK_CHANNELS ** -0.5, 0.5)
    height_bias = bell_draw(keys[6], (BLOCK_CHANNELS,), 0.5, 3.0)
    width_weight = bell_draw(keys[7], (BLOCK_CHANNELS, BLOCK_CHANNELS), BLOCK_CHANNELS ** -0.5, 0.5)
    width_bias = bell_draw(keys[8], (BLOCK_CHANNELS,), 0.5, 3.0)
    channel_weight = bell_draw(keys[9], (BLOCK_CHANNELS, BLOCK_CHANNELS), BLOCK_CHANNELS ** -0.5, 0.5)
    squeeze_weight = bell_draw(keys[10], (BLOCK_CHANNELS, RED), (BLOCK_CHANNELS // 8) ** -0.5, 1.5)
    squeeze_bias = bell_draw(keys[11], (RED,), 0.5, 3.0)
    excite_weight = bell_draw(keys[12], (RED, 3 * BLOCK_CHANNELS), RED ** -0.5, 1.0)
    excite_bias = bell_draw(keys[13], (3 * BLOCK_CHANNELS,), 0.5, 3.0)
    output_weight = bell_draw(keys[14], (BLOCK_CHANNELS, BLOCK_CHANNELS), (BLOCK_CHANNELS // 2) ** -0.5, 0.75)
    output_bias = bell_draw(keys[15], (BLOCK_CHANNELS,), 0.5, 3.0)
    second_gain = jnp.clip(1.0 + 0.1 * jax.random.normal(keys[16], (BLOCK_CHANNELS,), jnp.float32), 0.5, 1.5).astype(jnp.bfloat16)
    second_bias = bell_draw(keys[17], (BLOCK_CHANNELS,), 0.5, 3.0)
    expand_weight = bell_draw(keys[18], (BLOCK_CHANNELS, FF), BLOCK_CHANNELS ** -0.5, 0.5)
    expand_bias = bell_draw(keys[19], (FF,), 0.5, 3.0)
    reduce_weight = bell_draw(keys[20], (FF, BLOCK_CHANNELS), (FF // 2) ** -0.5, 0.375)
    reduce_bias = bell_draw(keys[21], (BLOCK_CHANNELS,), 0.5, 3.0)
    stride_weight = bell_draw(keys[22], (OUT, 9, BLOCK_CHANNELS), (9 * BLOCK_CHANNELS) ** -0.5, 0.1875)
    stride_bias = bell_draw(keys[23], (OUT,), 0.5, 3.0)
    cotangent = bell_draw(keys[24], (OUT, IMAGES * OPIX), 1.0, 6.0, ((0, 32), (1, 4)))
    return dict(features=features, size_group=size_group, cycle_offsets=cycle_offsets, norm_gain=norm_gain, norm_bias=norm_bias, height_weight=height_weight, height_bias=height_bias, width_weight=width_weight, width_bias=width_bias, channel_weight=channel_weight, squeeze_weight=squeeze_weight, squeeze_bias=squeeze_bias, excite_weight=excite_weight, excite_bias=excite_bias, output_weight=output_weight, output_bias=output_bias, second_gain=second_gain, second_bias=second_bias, expand_weight=expand_weight, expand_bias=expand_bias, reduce_weight=reduce_weight, reduce_bias=reduce_bias, stride_weight=stride_weight, stride_bias=stride_bias, cotangent=cotangent)


@jax.custom_vjp
def low(v):
    return lax.optimization_barrier(v.astype(jnp.bfloat16)).astype(jnp.float32)

@jax.custom_vjp
def low_back(v):
    return v

def low_keep(v):
    return (low(v), None)

def low_pass(kept, grad):
    return (grad,)

def back_keep(v):
    return (v, None)

def back_low(kept, grad):
    return (low(grad),)
low.defvjp(low_keep, low_pass)
low_back.defvjp(back_keep, back_low)
EPS = 1e-05
HIGH = lax.Precision.HIGHEST

def tdot(left, right):
    return lax.dot_general(left, right, (((0,), (0,)), ((), ())), precision=HIGH, preferred_element_type=jnp.float32)

def layer_norm(values, gain, bias):
    center = values - lax.optimization_barrier(jnp.mean(values, axis=0, keepdims=True))
    spread = lax.optimization_barrier(jnp.mean(center * center, axis=0, keepdims=True))
    return center * lax.rsqrt(spread + EPS) * gain[:, None] + bias[:, None]

def gelu_exact(values):
    return jax.nn.gelu(values, approximate=False)

def reweigh(means, squeeze_w, squeeze_b, excite_w, excite_b):
    inner = gelu_exact(tdot(squeeze_w, means) + squeeze_b[:, None])
    logits = tdot(excite_w, inner) + excite_b[:, None]
    return jax.nn.softmax(logits.reshape(3, -1, means.shape[1]), axis=0)

def pick(padded, offsets, stride, sign, count):
    result = jnp.zeros((padded.shape[0], count), padded.dtype)
    for step in (-1, 0, 1):
        begin = CANVAS + sign * step * stride
        result = jnp.where(offsets[:, None] == step, padded[:, begin:begin + count], result)
    return result

def inside(coord, offsets):
    moved = coord[None, :] + offsets[:, None]
    return (moved >= 0) & (moved < CANVAS)

def pixel_info(begin, count, sides):
    index = begin + jnp.arange(count, dtype=jnp.int32)
    image = index // (CANVAS * CANVAS)
    local = index % (CANVAS * CANVAS)
    row = local // CANVAS
    column = local % CANVAS
    onehot = (image[:, None] == jnp.arange(sides.shape[0], dtype=jnp.int32)[None, :]).astype(jnp.float32)
    side = lax.optimization_barrier(jnp.sum(onehot * sides[None, :], axis=1))
    valid = ((row < side) & (column < side)).astype(jnp.float32)
    return (valid, onehot, row, column)

def out_info(sides):
    half = CANVAS // 2
    index = jnp.arange(sides.shape[0] * half * half, dtype=jnp.int32)
    image = index // (half * half)
    local = index % (half * half)
    onehot = (image[:, None] == jnp.arange(sides.shape[0], dtype=jnp.int32)[None, :]).astype(jnp.float32)
    side = lax.optimization_barrier(jnp.sum(onehot * sides[None, :], axis=1))
    return ((2 * (local // half) < side) & (2 * (local % half) < side)).astype(jnp.float32)

def make_taps(block):
    images = block.shape[1] // (CANVAS * CANVAS)
    grid = block.reshape(block.shape[0], images, CANVAS, CANVAS)
    padded = jnp.pad(grid, ((0, 0), (0, 0), (1, 1), (1, 1)))
    half = CANVAS // 2
    taps = [padded[:, :, a:a + CANVAS:2, b:b + CANVAS:2] for a in range(3) for b in range(3)]
    return jnp.stack(taps).reshape(9 * block.shape[0], images * half * half)

def reference(features, size_group, cycle_offsets, norm_gain, norm_bias, height_weight, height_bias, width_weight, width_bias, channel_weight, squeeze_weight, squeeze_bias, excite_weight, excite_bias, output_weight, output_bias, second_gain, second_bias, expand_weight, expand_bias, reduce_weight, reduce_bias, stride_weight, stride_bias, cotangent):
    images = size_group.shape[0]
    sides = (CANVAS - 4 * (2 - size_group)).astype(jnp.float32)
    counts = sides * sides
    total = features.shape[1]
    valid, onehot, row, column = pixel_info(0, total, sides)
    out_valid = out_info(sides)
    rows_in = inside(row, cycle_offsets[0])
    cols_in = inside(column, cycle_offsets[1])

    def forward(xin, ng, nb, hw, hb, ww, wb, cw, sqw, sqb, exw, exb, ow, ob, sg, sbias, xw, xb, rw, rb, kw, kb):
        masked = xin * valid
        normed = low(layer_norm(masked, ng, nb) * valid)
        padded = jnp.pad(normed, ((0, 0), (CANVAS, CANVAS)))
        shift_rows = jnp.where(rows_in, pick(padded, cycle_offsets[0], CANVAS, 1, total), 0.0)
        shift_cols = jnp.where(cols_in, pick(padded, cycle_offsets[1], 1, 1, total), 0.0)
        branch_h = low_back(tdot(hw, shift_rows) + hb[:, None])
        branch_w = low_back(tdot(ww, shift_cols) + wb[:, None])
        branch_c = low_back(tdot(cw, normed))
        sums = lax.optimization_barrier(jnp.sum(((branch_h + branch_w + branch_c) * valid).reshape(-1, images, CANVAS * CANVAS), axis=2))
        mix_weight = reweigh(sums / counts, sqw, sqb, exw, exb)
        spread = jnp.repeat(mix_weight, CANVAS * CANVAS, axis=2)
        mixed = low(spread[0] * branch_h + spread[1] * branch_w + spread[2] * branch_c)
        resid = masked + low_back(tdot(ow, mixed) + ob[:, None])
        normed2 = low(layer_norm(resid, sg, sbias))
        hidden = low(gelu_exact(low_back(tdot(xw, normed2) + xb[:, None])))
        block = low((resid + low_back(tdot(rw, hidden) + rb[:, None])) * valid)
        taps = make_taps(block)
        conv = jnp.dot(kw.reshape(kw.shape[0], -1), taps, precision=HIGH, preferred_element_type=jnp.float32)
        return (conv + kb[:, None]) * out_valid
    params = tuple((p.astype(jnp.float32) for p in (norm_gain, norm_bias, height_weight, height_bias, width_weight, width_bias, channel_weight, squeeze_weight, squeeze_bias, excite_weight, excite_bias, output_weight, output_bias, second_gain, second_bias, expand_weight, expand_bias, reduce_weight, reduce_bias, stride_weight, stride_bias)))
    section, pull = jax.vjp(forward, features.astype(jnp.float32), *params)
    g_x, g_ng, g_nb, g_hw, g_hb, g_ww, g_wb, g_cw, g_sqw, g_sqb, g_exw, g_exb, g_ow, g_ob, g_sg, g_sb, g_xw, g_xb, g_rw, g_rb, g_kw, g_kb = pull(cotangent.astype(jnp.float32))
    return (section.astype(jnp.bfloat16), g_x, g_ng, g_nb, g_hw, g_hb, g_ww, g_wb, g_cw, g_sqw, g_sqb, g_exw, g_exb, g_ow, g_ob, g_sg, g_sb, g_xw, g_xb, g_rw, g_rb, g_kw, g_kb)
```

```python
import jax
import jax.numpy as jnp
from jax import lax
from jax.experimental import pallas as pl
from jax.experimental.pallas import tpu as pltpu
from jax.sharding import PartitionSpec as P

CH = 128
FF = 512
RED = 32
OUT = 320
SIDE = 36
PIX = SIDE * SIDE
HALF = SIDE // 2
OPIX = HALF * HALF
WIDE = 40
FLAT = SIDE * WIDE
GUARD = 48
ROWS = 288
STEPS = FLAT // ROWS
EPS = 1e-05
LANES = 128
WIN = 11
OTILE = 3
PIXROWS = 80
WROWS = 144
CHUNK = PIXROWS + WROWS
VMEM = 56 * 1024 * 1024

F32 = jnp.float32
BF16 = jnp.bfloat16

AT_CONV = 0
AT_REDUCE = 2880
AT_EXPAND = 3392
AT_HEIGHT = 3904
AT_WIDTH = 4032
AT_CHANNEL = 4160
AT_OUTPUT = 4288
AT_SQUEEZE = 4416
AT_EXCITE = 4448
AT_SQ_BIAS = 4544
AT_VECTOR = 4576


def params(**kw):
    return pltpu.CompilerParams(vmem_limit_bytes=VMEM, **kw)


def first_tile(k):
    return 10 * k + k // 8


def nn(a, b):
    return lax.dot_general(a, b, (((1,), (0,)), ((), ())), preferred_element_type=F32)


def nt(a, b):
    return lax.dot_general(a, b, (((1,), (1,)), ((), ())), preferred_element_type=F32)


def tn(a, b):
    return lax.dot_general(a, b, (((0,), (0,)), ((), ())), preferred_element_type=F32)


def lane_mean(v):
    return jnp.sum(v, axis=1, keepdims=True) * (1.0 / CH)


def col_sum(v):
    return jnp.sum(v, axis=0, keepdims=True)


def normal_parts(x):
    z = jnp.abs(x) * 0.7071067811865476
    t = 1.0 / (1.0 + 0.3275911 * z)
    bell = jnp.exp(-z * z)
    poly = 1.061405429 * t - 1.453152027
    poly = poly * t + 1.421413741
    poly = poly * t - 0.284496736
    poly = poly * t + 0.254829592
    tail = 0.5 * poly * t * bell
    return jnp.where(x < 0, tail, 1.0 - tail), bell * 0.3989422804014327


def pack_kernel(feat, cot, out, stage, cots):
    images = out.shape[0]
    cots[...] = cot[...].astype(F32)
    for k in range(images):
        base = k * PIXROWS
        begin = first_tile(k) * LANES
        for t in range(WIN):
            stage[base + 4 * t : base + 4 * t + 4, :] = feat[
                :, begin + t * LANES : begin + (t + 1) * LANES
            ].astype(F32)
        for j in range(OTILE):
            width = min(LANES, OPIX - j * LANES)
            at = k * OPIX + j * LANES
            row = base + 44 + 10 * j
            stage[row : row + 10, 0:width] = cots[:, at : at + width]
        out[k] = stage[base : base + PIXROWS, :].astype(BF16)


def main_kernel(
    info,
    recv,
    vecs,
    sqt,
    sqb,
    exw,
    kbias,
    hw,
    ww,
    cw,
    ow,
    xw,
    rw,
    kw,
    out,
    xf,
    cf,
    tall,
    canvas,
    valid,
    xhat,
    rstd,
    norm,
    rows_b,
    cols_b,
    norm_b,
    branch_h,
    branch_w,
    branch_c,
    mixed_b,
    xhat2,
    rstd2,
    norm2_b,
    hidden_b,
    slope,
    block,
    taps,
    spread,
    planes,
    gblock,
    gresid,
    gmixed,
    grows,
    gcols,
    gnorm,
    acc_r,
    acc_x,
    acc_s,
    sums,
    stage,
    gpre_b,
):
    shift = info[0]
    side = info[1]

    def vec(i):
        return vecs[i : i + 1, :]

    def put(row, value):
        value = value.astype(BF16)
        count = value.shape[0]
        done = 0
        while done < count:
            chunk, inner = divmod(row + done, WROWS)
            size = min(count - done, WROWS - inner)
            out[chunk, PIXROWS + inner : PIXROWS + inner + size, :] = value[done : done + size, :]
            done += size

    cf[...] = jnp.zeros_like(cf)
    for s in range(recv.shape[0]):
        piece = recv[s].astype(F32)
        for t in range(WIN):
            xf[4 * s : 4 * s + 4, t * LANES : (t + 1) * LANES] = piece[4 * t : 4 * t + 4, :]
        for j in range(OTILE):
            cf[10 * s : 10 * s + 10, j * LANES : (j + 1) * LANES] = piece[
                44 + 10 * j : 54 + 10 * j, :
            ]
    begin = pl.multiple_of(112 - shift, 16)
    for t in range(WIN):
        tall[pl.ds(begin + t * LANES, LANES), :] = xf[:, t * LANES : (t + 1) * LANES].T

    column = lax.broadcasted_iota(jnp.int32, (WIDE, CH), 0)
    for r in range(SIDE):
        keep = (column < side) & (r < side)
        canvas[r * WIDE : (r + 1) * WIDE, :] = jnp.where(
            keep, tall[112 + r * SIDE : 112 + r * SIDE + WIDE, :], 0.0
        )
        valid[r * WIDE : (r + 1) * WIDE, :] = jnp.where(keep, 1.0, 0.0)
    edge = jnp.zeros((GUARD, CH), F32)
    for ref in (norm, block, grows, gcols):
        ref[0:GUARD, :] = edge
        ref[GUARD + FLAT : FLAT + 2 * GUARD, :] = edge
    acc_r[...] = jnp.zeros_like(acc_r)
    acc_x[...] = jnp.zeros_like(acc_x)
    acc_s[...] = jnp.zeros_like(acc_s)
    sums[...] = jnp.zeros_like(sums)

    def rows_at(i):
        return pl.ds(pl.multiple_of(i * ROWS, 16), ROWS)

    def guarded(i, extra=0, size=ROWS):
        return pl.ds(pl.multiple_of(i * ROWS + GUARD + extra, 8), size)

    def first_norm(i, carry):
        here = rows_at(i)
        x = canvas[here, :]
        center = x - lane_mean(x)
        scale = lax.rsqrt(lane_mean(center * center) + EPS)
        unit = center * scale
        xhat[here, :] = unit
        rstd[here, :] = jnp.broadcast_to(scale, unit.shape)
        value = jnp.where(valid[here, :] > 0, unit * vec(0) + vec(1), 0.0)
        norm[guarded(i), :] = value.astype(BF16).astype(F32)
        return carry

    lax.fori_loop(0, STEPS, first_norm, 0)

    def near(ref, i):
        wide = ref[guarded(i, -8, ROWS + 16), :]
        back = pltpu.roll(wide, 1, 0)[8 : 8 + ROWS, :]
        ahead = pltpu.roll(wide, ROWS + 15, 0)[8 : 8 + ROWS, :]
        return back, ahead

    def branches(i, total):
        here = rows_at(i)
        plain = norm[guarded(i), :]
        above = norm[guarded(i, -WIDE), :]
        below = norm[guarded(i, WIDE), :]
        left, right = near(norm, i)
        by_row = vec(15)
        by_col = vec(16)
        sr = jnp.where(by_row < 0, above, jnp.where(by_row > 0, below, plain)).astype(BF16)
        sc = jnp.where(by_col < 0, left, jnp.where(by_col > 0, right, plain)).astype(BF16)
        nb = plain.astype(BF16)
        rows_b[here, :] = sr
        cols_b[here, :] = sc
        norm_b[here, :] = nb
        bh = nn(sr, hw[...]) + vec(2)
        bw = nn(sc, ww[...]) + vec(3)
        bc = nn(nb, cw[...])
        branch_h[here, :] = bh
        branch_w[here, :] = bw
        branch_c[here, :] = bc
        return total + col_sum(valid[here, :] * (bh + bw + bc))

    total = lax.fori_loop(0, STEPS, branches, jnp.zeros((1, CH), F32))

    count = jnp.full((1, CH), side * side, jnp.int32).astype(F32)
    means = total / count
    inner_pre = jnp.sum(sqt[...] * means, axis=1, keepdims=True) + sqb[...]
    inner_cdf, inner_density = normal_parts(inner_pre)
    inner = inner_pre * inner_cdf
    inner_slope = inner_cdf + inner_pre * inner_density
    logit = [col_sum(exw[:, j * CH : (j + 1) * CH] * inner) + vec(12 + j) for j in range(3)]
    top = jnp.maximum(jnp.maximum(logit[0], logit[1]), logit[2])
    grown = [jnp.exp(v - top) for v in logit]
    whole = grown[0] + grown[1] + grown[2]
    mix = [v / whole for v in grown]

    def forward(i, carry):
        here = rows_at(i)
        mixed = mix[0] * branch_h[here, :] + mix[1] * branch_w[here, :] + mix[2] * branch_c[here, :]
        mixed = mixed.astype(BF16)
        mixed_b[here, :] = mixed
        resid = canvas[here, :] + nn(mixed, ow[...]) + vec(4)
        center = resid - lane_mean(resid)
        scale = lax.rsqrt(lane_mean(center * center) + EPS)
        unit = center * scale
        xhat2[here, :] = unit
        rstd2[here, :] = jnp.broadcast_to(scale, unit.shape)
        n2 = (unit * vec(5) + vec(6)).astype(BF16)
        norm2_b[here, :] = n2
        total2 = resid + vec(7)
        for j in range(FF // CH):
            lanes = slice(j * CH, (j + 1) * CH)
            pre = nn(n2, xw[:, lanes]) + vec(8 + j)
            cdf, density = normal_parts(pre)
            hid = (pre * cdf).astype(BF16)
            hidden_b[here, lanes] = hid
            slope[here, lanes] = cdf + pre * density
        total2 = total2 + nn(hidden_b[here, :], rw[...])
        value = jnp.where(valid[here, :] > 0, total2, 0.0)
        block[guarded(i), :] = value.astype(BF16).astype(F32)
        return carry

    lax.fori_loop(0, STEPS, forward, 0)

    taps[OPIX:, :] = jnp.zeros((taps.shape[0] - OPIX, taps.shape[1]), F32)
    for a in range(3):
        for b in range(3):
            lanes = slice((3 * a + b) * CH, (3 * a + b + 1) * CH)
            for i in range(HALF):
                at = GUARD + (2 * i + a - 1) * WIDE + b - 1
                taps[i * HALF : (i + 1) * HALF, lanes] = block[pl.ds(at, HALF, stride=2), :]
    tap_b = taps[...].astype(BF16)
    index = lax.broadcasted_iota(jnp.int32, (1, OTILE * LANES), 1)
    out_row = ((index.astype(F32) + 0.5) * (1.0 / HALF)).astype(jnp.int32)
    out_col = index - out_row * HALF
    out_keep = (2 * out_row < side) & (2 * out_col < side)
    cot = jnp.where(out_keep, cf[...], 0.0)
    cot_b = cot[0:OUT, :].astype(BF16)
    cot_t = cot.T.astype(BF16)[:, 0:OUT]
    section = nt(kw[...], tap_b) + kbias[...]
    section = jnp.where(out_keep, section, 0.0)
    conv = nn(cot_b, tap_b)
    for t in range(9):
        put(AT_CONV + t * OUT, conv[:, t * CH : (t + 1) * CH])
    kb_rows = jnp.sum(cot, axis=1, keepdims=True)
    spread[...] = nn(cot_t, kw[...])
    row_id = lax.broadcasted_iota(jnp.int32, (OPIX, CH), 0)
    row_of = ((row_id.astype(F32) + 0.5) * (1.0 / HALF)).astype(jnp.int32)
    inside = row_id - row_of * HALF < HALF - 1

    def part(tap, ahead, masked):
        value = spread[ahead : ahead + OPIX, tap * CH : (tap + 1) * CH]
        return jnp.where(inside, value, 0.0) if masked else value

    found = (
        part(4, 0, False),
        part(5, 0, False) + part(3, 1, True),
        part(7, 0, False) + part(1, HALF, False),
        (part(8, 0, False) + part(6, 1, True)) + (part(2, HALF, False) + part(0, HALF + 1, True)),
    )
    for p in range(4):
        planes[p, 0:OPIX, :] = found[p]
        for i in range(HALF):
            at = (2 * i + p // 2) * WIDE + p % 2
            gblock[pl.ds(at, HALF, stride=2), :] = planes[p, i * HALF : (i + 1) * HALF, :]

    def add(row, value):
        sums[row : row + 1, :] += value

    def backward(i, carry):
        here = rows_at(i)
        gb = jnp.where(valid[here, :] > 0, gblock[here, :], 0.0)
        gred = gb.astype(BF16)
        add(7, col_sum(gred.astype(F32)))
        acc_r[...] += tn(gred, hidden_b[here, :])
        n2 = norm2_b[here, :]
        for j in range(FF // CH):
            lanes = slice(j * CH, (j + 1) * CH)
            gpre = (nt(gred, rw[lanes, :]) * slope[here, lanes]).astype(BF16)
            add(8 + j, col_sum(gpre.astype(F32)))
            gpre_b[:, lanes] = gpre
        acc_x[...] += tn(n2, gpre_b[...])
        gn2 = nt(gpre_b[...], xw[...])
        unit = xhat2[here, :]
        add(5, col_sum(gn2 * unit))
        add(6, col_sum(gn2))
        gy = gn2 * vec(5)
        gr = gb + rstd2[here, :] * (gy - lane_mean(gy) - unit * lane_mean(gy * unit))
        gresid[here, :] = gr
        gproj = gr.astype(BF16)
        add(4, col_sum(gproj.astype(F32)))
        acc_s[3] += tn(mixed_b[here, :], gproj)
        gm = nt(gproj, ow[...])
        gmixed[here, :] = gm
        add(20, col_sum(gm * branch_h[here, :]))
        add(21, col_sum(gm * branch_w[here, :]))
        add(22, col_sum(gm * branch_c[here, :]))
        return carry

    lax.fori_loop(0, STEPS, backward, 0)

    gmix = [sums[20 + j : 21 + j, :] for j in range(3)]
    inner_dot = mix[0] * gmix[0] + mix[1] * gmix[1] + mix[2] * gmix[2]
    glogit = [mix[j] * (gmix[j] - inner_dot) for j in range(3)]
    ginner = jnp.zeros((RED, 1), F32)
    for j in range(3):
        ginner += jnp.sum(exw[:, j * CH : (j + 1) * CH] * glogit[j], axis=1, keepdims=True)
        put(AT_EXCITE + RED * j, inner * glogit[j])
        sums[12 + j : 13 + j, :] = glogit[j]
    ginner = ginner * inner_slope
    put(AT_SQUEEZE, ginner * means)
    put(AT_SQ_BIAS, jnp.broadcast_to(ginner, (RED, CH)))
    gmeans = col_sum(sqt[...] * ginner) / count

    def branch_back(i, carry):
        here = rows_at(i)
        gm = gmixed[here, :]
        level = valid[here, :] * gmeans
        gh = (mix[0] * gm + level).astype(BF16)
        gw = (mix[1] * gm + level).astype(BF16)
        gc = (mix[2] * gm + level).astype(BF16)
        add(2, col_sum(gh.astype(F32)))
        add(3, col_sum(gw.astype(F32)))
        acc_s[0] += tn(rows_b[here, :], gh)
        acc_s[1] += tn(cols_b[here, :], gw)
        acc_s[2] += tn(norm_b[here, :], gc)
        grows[guarded(i), :] = nt(gh, hw[...])
        gcols[guarded(i), :] = nt(gw, ww[...])
        gnorm[here, :] = nt(gc, cw[...])
        return carry

    lax.fori_loop(0, STEPS, branch_back, 0)

    def last(i, carry):
        here = rows_at(i)
        by_row = vec(15)
        by_col = vec(16)
        plain = grows[guarded(i), :]
        above = grows[guarded(i, -WIDE), :]
        below = grows[guarded(i, WIDE), :]
        left, right = near(gcols, i)
        level = gcols[guarded(i), :]
        value = (
            gnorm[here, :]
            + jnp.where(by_row < 0, below, jnp.where(by_row > 0, above, plain))
            + jnp.where(by_col < 0, right, jnp.where(by_col > 0, left, level))
        )
        keep = valid[here, :] > 0
        value = jnp.where(keep, value, 0.0)
        unit = xhat[here, :]
        add(0, col_sum(value * unit))
        add(1, col_sum(value))
        gy = value * vec(0)
        back = rstd[here, :] * (gy - lane_mean(gy) - unit * lane_mean(gy * unit))
        canvas[here, :] = jnp.where(keep, gresid[here, :] + back, 0.0)
        return carry

    lax.fori_loop(0, STEPS, last, 0)

    tall[0:112, :] = jnp.zeros((112, CH), F32)
    tall[112 + PIX :, :] = jnp.zeros((tall.shape[0] - 112 - PIX, CH), F32)
    for r in range(SIDE):
        tall[112 + r * SIDE : 112 + (r + 1) * SIDE, :] = canvas[r * WIDE : r * WIDE + SIDE, :]
    for t in range(WIN):
        xf[:, t * LANES : (t + 1) * LANES] = tall[pl.ds(begin + t * LANES, LANES), :].T
    cf[0:OUT, :] = section
    for s in range(recv.shape[0]):
        for t in range(WIN):
            stage[4 * t : 4 * t + 4, :] = xf[4 * s : 4 * s + 4, t * LANES : (t + 1) * LANES]
        for j in range(OTILE):
            stage[44 + 10 * j : 54 + 10 * j, :] = cf[
                10 * s : 10 * s + 10, j * LANES : (j + 1) * LANES
            ]
        out[s, 0:PIXROWS, :] = stage[...].astype(BF16)

    for j in range(FF // CH):
        put(AT_REDUCE + j * CH, acc_r[:, j * CH : (j + 1) * CH].T)
        put(AT_EXPAND + j * CH, acc_x[:, j * CH : (j + 1) * CH])
    for j, at in enumerate((AT_HEIGHT, AT_WIDTH, AT_CHANNEL, AT_OUTPUT)):
        put(at, acc_s[j])
    same = lax.broadcasted_iota(jnp.int32, (LANES, LANES), 0) == lax.broadcasted_iota(
        jnp.int32, (LANES, LANES), 1
    )
    for j in range(OTILE):
        add(15 + j, col_sum(jnp.where(same, kb_rows[j * LANES : (j + 1) * LANES, :], 0.0)))
    put(AT_VECTOR, sums[...])


def add_kernel(recv, out):
    total = recv[0, PIXROWS:, :].astype(F32)
    for s in range(1, recv.shape[0]):
        total += recv[s, PIXROWS:, :].astype(F32)
    out[...] = total.astype(BF16)


def pixel_kernel(recv, feat, section, stage):
    images = recv.shape[0]
    for k in range(images):
        piece = recv[k, 0:PIXROWS, :].astype(F32)
        tile = first_tile(k)
        for t in range(WIN):
            lanes = slice((tile + t) * LANES, (tile + t + 1) * LANES)
            value = piece[4 * t : 4 * t + 4, :]
            if t == 0 and k % 8:
                feat[:, lanes] += value
            else:
                feat[:, lanes] = value
        for j in range(OTILE):
            width = min(LANES, OPIX - j * LANES)
            at = k * OPIX + j * LANES
            stage[:, at : at + width] = piece[44 + 10 * j : 54 + 10 * j, 0:width]
    section[...] = stage[...].astype(BF16)


def weight_kernel(
    recv, conv, red, exp, height, width, chan, outw, squeeze, excite, sq_bias, vectors
):
    def rows(at, count):
        return recv[at : at + count, :].astype(F32)

    for t in range(9):
        conv[:, t, :] = rows(AT_CONV + t * OUT, OUT)
    red[...] = rows(AT_REDUCE, FF)
    for j in range(FF // CH):
        exp[:, j * CH : (j + 1) * CH] = rows(AT_EXPAND + j * CH, CH)
    for at, ref in (
        (AT_HEIGHT, height),
        (AT_WIDTH, width),
        (AT_CHANNEL, chan),
        (AT_OUTPUT, outw),
    ):
        ref[...] = rows(at, CH)
    squeeze[...] = rows(AT_SQUEEZE, RED).T
    for j in range(3):
        excite[:, j * CH : (j + 1) * CH] = rows(AT_EXCITE + j * RED, RED)
    sq_bias[...] = rows(AT_SQ_BIAS, RED).T[0:8, :]
    vectors[...] = rows(AT_VECTOR, RED)


def body(
    features,
    size_group,
    cycle_offsets,
    norm_gain,
    norm_bias,
    height_weight,
    height_bias,
    width_weight,
    width_bias,
    channel_weight,
    squeeze_weight,
    squeeze_bias,
    excite_weight,
    excite_bias,
    output_weight,
    output_bias,
    second_gain,
    second_bias,
    expand_weight,
    expand_bias,
    reduce_weight,
    reduce_bias,
    stride_weight,
    stride_bias,
    cotangent,
):
    shards = lax.axis_size("ch")
    rank = lax.axis_index("ch")
    side = SIDE - 4 * (2 - lax.dynamic_index_in_dim(size_group, rank, keepdims=False))
    info = jnp.stack([16 * (rank % 8), side]).astype(jnp.int32)
    vecs = jnp.concatenate(
        [
            v.astype(F32)
            for v in (
                norm_gain,
                norm_bias,
                height_bias,
                width_bias,
                output_bias,
                second_gain,
                second_bias,
                reduce_bias,
                expand_bias,
                excite_bias,
                cycle_offsets[0],
                cycle_offsets[1],
            )
        ]
    ).reshape(17, CH)

    chunks = pl.pallas_call(
        pack_kernel,
        out_shape=jax.ShapeDtypeStruct((shards, PIXROWS, LANES), BF16),
        scratch_shapes=[
            pltpu.VMEM((shards * PIXROWS, LANES), F32),
            pltpu.VMEM(cotangent.shape, F32),
        ],
        compiler_params=params(),
    )(features, cotangent)
    arrived = lax.all_to_all(chunks, "ch", split_axis=0, concat_axis=0, tiled=True)

    canvas = pltpu.VMEM((FLAT, CH), F32)
    guarded = pltpu.VMEM((FLAT + 2 * GUARD, CH), F32)
    narrow = pltpu.VMEM((FLAT, CH), BF16)
    whole = pl.BlockSpec(memory_space=pltpu.VMEM)
    made = pl.pallas_call(
        main_kernel,
        out_shape=jax.ShapeDtypeStruct((shards, CHUNK, LANES), BF16),
        in_specs=[pl.BlockSpec(memory_space=pltpu.SMEM)] + [whole] * 13,
        out_specs=whole,
        scratch_shapes=[
            pltpu.VMEM((CH, WIN * LANES), F32),
            pltpu.VMEM((3 * LANES, OTILE * LANES), F32),
            pltpu.VMEM((112 + WIN * LANES, CH), F32),
            canvas,
            canvas,
            canvas,
            canvas,
            guarded,
            narrow,
            narrow,
            narrow,
            canvas,
            canvas,
            canvas,
            narrow,
            canvas,
            canvas,
            narrow,
            pltpu.VMEM((FLAT, FF), BF16),
            pltpu.VMEM((FLAT, FF), F32),
            guarded,
            pltpu.VMEM((OTILE * LANES, 9 * CH), F32),
            pltpu.VMEM((OTILE * LANES, 9 * CH), F32),
            pltpu.VMEM((4, 328, CH), F32),
            canvas,
            canvas,
            canvas,
            guarded,
            guarded,
            canvas,
            pltpu.VMEM((CH, FF), F32),
            pltpu.VMEM((CH, FF), F32),
            pltpu.VMEM((4, CH, CH), F32),
            pltpu.VMEM((RED, CH), F32),
            pltpu.VMEM((PIXROWS, LANES), F32),
            pltpu.VMEM((ROWS, FF), BF16),
        ],
        compiler_params=params(),
    )(
        info,
        arrived,
        vecs,
        squeeze_weight.astype(F32).T,
        squeeze_bias.astype(F32)[:, None],
        excite_weight.astype(F32),
        stride_bias.astype(F32)[:, None],
        height_weight,
        width_weight,
        channel_weight,
        output_weight,
        expand_weight,
        reduce_weight,
        stride_weight.reshape(OUT, 9 * CH),
    )
    back = lax.all_to_all(made, "ch", split_axis=0, concat_axis=0, tiled=True)

    mine = pl.pallas_call(
        add_kernel,
        out_shape=jax.ShapeDtypeStruct((WROWS, LANES), BF16),
        compiler_params=params(),
    )(back)
    groups = lax.axis_size("img")
    other = [
        lax.ppermute(mine, "img", [(i, (i + d) % groups) for i in range(groups)]).astype(F32)
        for d in (1, 2, 3)
    ]
    owned = ((mine.astype(F32) + other[1]) + (other[0] + other[2])).astype(BF16)
    copies = jnp.broadcast_to(owned, (shards, WROWS, LANES))
    summed = lax.all_to_all(copies, "ch", split_axis=0, concat_axis=0, tiled=True)

    features_grad, section = pl.pallas_call(
        pixel_kernel,
        out_shape=(
            jax.ShapeDtypeStruct(features.shape, F32),
            jax.ShapeDtypeStruct(cotangent.shape, BF16),
        ),
        scratch_shapes=[pltpu.VMEM(cotangent.shape, F32)],
        compiler_params=params(),
    )(back)

    def like(*shape):
        return jax.ShapeDtypeStruct(shape, F32)

    (
        conv_grad,
        reduce_grad,
        expand_grad,
        height_grad,
        width_grad,
        channel_grad,
        output_grad,
        squeeze_grad,
        excite_grad,
        squeeze_rows,
        vectors,
    ) = pl.pallas_call(
        weight_kernel,
        out_shape=(
            like(OUT, 9, CH),
            like(FF, CH),
            like(CH, FF),
            like(CH, CH),
            like(CH, CH),
            like(CH, CH),
            like(CH, CH),
            like(CH, RED),
            like(RED, 3 * CH),
            like(8, RED),
            like(RED, CH),
        ),
        compiler_params=params(),
    )(summed.reshape(shards * WROWS, LANES))
    flat = vectors.reshape(RED * CH)

    def vector(row, count=CH):
        return flat[row * CH : row * CH + count]

    return (
        section,
        features_grad,
        vector(0),
        vector(1),
        height_grad,
        vector(2),
        width_grad,
        vector(3),
        channel_grad,
        squeeze_grad,
        squeeze_rows[0],
        excite_grad,
        vector(12, 3 * CH),
        output_grad,
        vector(4),
        vector(5),
        vector(6),
        expand_grad,
        vector(8, FF),
        reduce_grad,
        vector(7),
        conv_grad,
        vector(15, OUT),
    )


def solution(mesh):
    split = P("ch", "img")
    return jax.shard_map(
        body,
        mesh=mesh,
        in_specs=(split, P("img")) + (P(),) * 22 + (split,),
        out_specs=(split, split) + (P(),) * 21,
        check_vma=False,
    )
```

```python
import jax
import jax.numpy as jnp
from jax import lax
from jax.experimental import pallas as pl
from jax.experimental.pallas import tpu as pltpu
from jax.sharding import PartitionSpec as P

CH = 128
FF = 512
RED = 32
OUT = 320
SIDE = 36
PIX = SIDE * SIDE
HALF = SIDE // 2
OPIX = HALF * HALF
WIDE = 40
FLAT = SIDE * WIDE
GUARD = 48
ROWS = 288
STEPS = FLAT // ROWS
EPS = 1e-05
LANES = 128
WIN = 11
OTILE = 3
PIXROWS = 80
WROWS = 144
VMEM = 56 * 1024 * 1024

F32 = jnp.float32
BF16 = jnp.bfloat16

AT_CONV = 0
AT_REDUCE = 2880
AT_EXPAND = 3392
AT_HEIGHT = 3904
AT_WIDTH = 4032
AT_CHANNEL = 4160
AT_OUTPUT = 4288
AT_SQUEEZE = 4416
AT_EXCITE = 4448
AT_SQ_BIAS = 4544
AT_VECTOR = 4576
VECTOR_ROWS = (0, 1, 2, 3, 4, 5, 6, 7, 8, 12, 15)
VECTOR_SIZES = (CH,) * 8 + (FF, 3 * CH, OUT)


def params(**kw):
    return pltpu.CompilerParams(vmem_limit_bytes=VMEM, **kw)


def cost(micros):
    return pl.CostEstimate(flops=0, bytes_accessed=int(micros * 3.69e6), transcendentals=0)


def first_tile(k):
    return 10 * k + k // 8


def nn(a, b):
    return lax.dot_general(a, b, (((1,), (0,)), ((), ())), preferred_element_type=F32)


def nt(a, b):
    return lax.dot_general(a, b, (((1,), (1,)), ((), ())), preferred_element_type=F32)


def tn(a, b):
    return lax.dot_general(a, b, (((0,), (0,)), ((), ())), preferred_element_type=F32)


def lane_mean(v):
    return jnp.sum(v, axis=1, keepdims=True) * (1.0 / CH)


def col_sum(v):
    return jnp.sum(v, axis=0, keepdims=True)


def normal_parts(x):
    z = jnp.abs(x) * 0.7071067811865476
    t = 1.0 / (1.0 + 0.3275911 * z)
    bell = jnp.exp(-z * z)
    poly = 1.061405429 * t - 1.453152027
    poly = poly * t + 1.421413741
    poly = poly * t - 0.284496736
    poly = poly * t + 0.254829592
    tail = 0.5 * poly * t * bell
    return jnp.where(x < 0, tail, 1.0 - tail), bell * 0.3989422804014327


def pack_kernel(feat, cot, out, stage, cots):
    images = out.shape[0]
    cots[...] = cot[...].astype(F32)
    for k in range(images):
        base = k * PIXROWS
        begin = first_tile(k) * LANES
        for t in range(WIN):
            stage[base + 4 * t : base + 4 * t + 4, :] = feat[
                :, begin + t * LANES : begin + (t + 1) * LANES
            ].astype(F32)
        for j in range(OTILE):
            width = min(LANES, OPIX - j * LANES)
            at = k * OPIX + j * LANES
            row = base + 44 + 10 * j
            stage[row : row + 10, 0:width] = cots[:, at : at + width]
        out[k] = stage[base : base + PIXROWS, :].astype(BF16)


def main_kernel(
    info,
    recv,
    vecs,
    sqt,
    sqb,
    exw,
    kbias,
    hw,
    ww,
    cw,
    ow,
    xw,
    rw,
    kw,
    keep_out,
    send_out,
    grad,
    section_out,
    xf,
    cf,
    tall,
    canvas,
    valid,
    xhat,
    rstd,
    norm,
    rows_b,
    cols_b,
    norm_b,
    branch_h,
    branch_w,
    branch_c,
    mixed_b,
    xhat2,
    rstd2,
    norm2_b,
    hidden_b,
    slope,
    block,
    taps,
    spread,
    planes,
    gblock,
    gresid,
    gmixed,
    grows,
    gcols,
    gnorm,
    acc_r,
    acc_x,
    acc_s,
    sums,
    gpre_b,
    rows_out,
):
    shift = info[0]
    side = info[1]
    core = info[2]

    def vec(i):
        return vecs[i : i + 1, :]

    def put(row, value):
        count = value.shape[0]
        done = 0
        while done < count:
            chunk, inner = divmod(row + done, WROWS)
            size = min(count - done, WROWS - inner)
            slot = core if chunk % 2 == 0 else 1 - core
            rows_out[slot, chunk // 2, inner : inner + size, :] = value[done : done + size, :]
            done += size

    cf[...] = jnp.zeros_like(cf)
    for s in range(recv.shape[0]):
        piece = recv[s].astype(F32)
        for t in range(WIN):
            xf[4 * s : 4 * s + 4, t * LANES : (t + 1) * LANES] = piece[4 * t : 4 * t + 4, :]
        for j in range(OTILE):
            cf[10 * s : 10 * s + 10, j * LANES : (j + 1) * LANES] = piece[
                44 + 10 * j : 54 + 10 * j, :
            ]
    begin = pl.multiple_of(112 - shift, 16)
    for t in range(WIN):
        tall[pl.ds(begin + t * LANES, LANES), :] = xf[:, t * LANES : (t + 1) * LANES].T

    column = lax.broadcasted_iota(jnp.int32, (WIDE, CH), 0)
    for r in range(SIDE):
        keep = (column < side) & (r < side)
        canvas[r * WIDE : (r + 1) * WIDE, :] = jnp.where(
            keep, tall[112 + r * SIDE : 112 + r * SIDE + WIDE, :], 0.0
        )
        valid[r * WIDE : (r + 1) * WIDE, :] = jnp.where(keep, 1.0, 0.0)
    edge = jnp.zeros((GUARD, CH), F32)
    for ref in (norm, block, grows, gcols):
        ref[0:GUARD, :] = edge
        ref[GUARD + FLAT : FLAT + 2 * GUARD, :] = edge
    acc_r[...] = jnp.zeros_like(acc_r)
    acc_x[...] = jnp.zeros_like(acc_x)
    acc_s[...] = jnp.zeros_like(acc_s)
    sums[...] = jnp.zeros_like(sums)

    def rows_at(i):
        return pl.ds(pl.multiple_of(i * ROWS, 16), ROWS)

    def guarded(i, extra=0, size=ROWS):
        return pl.ds(pl.multiple_of(i * ROWS + GUARD + extra, 8), size)

    def first_norm(i, carry):
        here = rows_at(i)
        x = canvas[here, :]
        center = x - lane_mean(x)
        scale = lax.rsqrt(lane_mean(center * center) + EPS)
        unit = center * scale
        xhat[here, :] = unit
        rstd[here, :] = jnp.broadcast_to(scale, unit.shape)
        value = jnp.where(valid[here, :] > 0, unit * vec(0) + vec(1), 0.0)
        norm[guarded(i), :] = value.astype(BF16).astype(F32)
        return carry

    lax.fori_loop(0, STEPS, first_norm, 0)

    def near(ref, i):
        wide = ref[guarded(i, -8, ROWS + 16), :]
        back = pltpu.roll(wide, 1, 0)[8 : 8 + ROWS, :]
        ahead = pltpu.roll(wide, ROWS + 15, 0)[8 : 8 + ROWS, :]
        return back, ahead

    def branches(i, total):
        here = rows_at(i)
        plain = norm[guarded(i), :]
        above = norm[guarded(i, -WIDE), :]
        below = norm[guarded(i, WIDE), :]
        left, right = near(norm, i)
        by_row = vec(15)
        by_col = vec(16)
        sr = jnp.where(by_row < 0, above, jnp.where(by_row > 0, below, plain)).astype(BF16)
        sc = jnp.where(by_col < 0, left, jnp.where(by_col > 0, right, plain)).astype(BF16)
        nb = plain.astype(BF16)
        rows_b[here, :] = sr
        cols_b[here, :] = sc
        norm_b[here, :] = nb
        bh = nn(sr, hw[...]) + vec(2)
        bw = nn(sc, ww[...]) + vec(3)
        bc = nn(nb, cw[...])
        branch_h[here, :] = bh
        branch_w[here, :] = bw
        branch_c[here, :] = bc
        return total + col_sum(valid[here, :] * (bh + bw + bc))

    total = lax.fori_loop(0, STEPS, branches, jnp.zeros((1, CH), F32))

    count = jnp.full((1, CH), side * side, jnp.int32).astype(F32)
    means = total / count
    inner_pre = jnp.sum(sqt[...] * means, axis=1, keepdims=True) + sqb[...]
    inner_cdf, inner_density = normal_parts(inner_pre)
    inner = inner_pre * inner_cdf
    inner_slope = inner_cdf + inner_pre * inner_density
    logit = [col_sum(exw[:, j * CH : (j + 1) * CH] * inner) + vec(12 + j) for j in range(3)]
    top = jnp.maximum(jnp.maximum(logit[0], logit[1]), logit[2])
    grown = [jnp.exp(v - top) for v in logit]
    whole = grown[0] + grown[1] + grown[2]
    mix = [v / whole for v in grown]

    def forward(i, carry):
        here = rows_at(i)
        mixed = mix[0] * branch_h[here, :] + mix[1] * branch_w[here, :] + mix[2] * branch_c[here, :]
        mixed = mixed.astype(BF16)
        mixed_b[here, :] = mixed
        resid = canvas[here, :] + nn(mixed, ow[...]) + vec(4)
        center = resid - lane_mean(resid)
        scale = lax.rsqrt(lane_mean(center * center) + EPS)
        unit = center * scale
        xhat2[here, :] = unit
        rstd2[here, :] = jnp.broadcast_to(scale, unit.shape)
        n2 = (unit * vec(5) + vec(6)).astype(BF16)
        norm2_b[here, :] = n2
        total2 = resid + vec(7)
        for j in range(FF // CH):
            lanes = slice(j * CH, (j + 1) * CH)
            pre = nn(n2, xw[:, lanes]) + vec(8 + j)
            cdf, density = normal_parts(pre)
            hid = (pre * cdf).astype(BF16)
            hidden_b[here, lanes] = hid
            slope[here, lanes] = cdf + pre * density
        total2 = total2 + nn(hidden_b[here, :], rw[...])
        value = jnp.where(valid[here, :] > 0, total2, 0.0)
        block[guarded(i), :] = value.astype(BF16).astype(F32)
        return carry

    lax.fori_loop(0, STEPS, forward, 0)

    taps[OPIX:, :] = jnp.zeros((taps.shape[0] - OPIX, taps.shape[1]), F32)
    for a in range(3):
        for b in range(3):
            lanes = slice((3 * a + b) * CH, (3 * a + b + 1) * CH)
            for i in range(HALF):
                at = GUARD + (2 * i + a - 1) * WIDE + b - 1
                taps[i * HALF : (i + 1) * HALF, lanes] = block[pl.ds(at, HALF, stride=2), :]
    tap_b = taps[...].astype(BF16)
    index = lax.broadcasted_iota(jnp.int32, (1, OTILE * LANES), 1)
    out_row = ((index.astype(F32) + 0.5) * (1.0 / HALF)).astype(jnp.int32)
    out_col = index - out_row * HALF
    out_keep = (2 * out_row < side) & (2 * out_col < side)
    cot = jnp.where(out_keep, cf[...], 0.0)
    cot_b = cot[0:OUT, :].astype(BF16)
    cot_t = cot.T.astype(BF16)[:, 0:OUT]
    section = nt(kw[...], tap_b) + kbias[...]
    section_out[...] = jnp.where(out_keep, section, 0.0)
    conv = nn(cot_b, tap_b)
    for t in range(9):
        put(AT_CONV + t * OUT, conv[:, t * CH : (t + 1) * CH])
    kb_rows = jnp.sum(cot, axis=1, keepdims=True)
    spread[...] = nn(cot_t, kw[...])
    row_id = lax.broadcasted_iota(jnp.int32, (OPIX, CH), 0)
    row_of = ((row_id.astype(F32) + 0.5) * (1.0 / HALF)).astype(jnp.int32)
    inside = row_id - row_of * HALF < HALF - 1

    def part(tap, ahead, masked):
        value = spread[ahead : ahead + OPIX, tap * CH : (tap + 1) * CH]
        return jnp.where(inside, value, 0.0) if masked else value

    found = (
        part(4, 0, False),
        part(5, 0, False) + part(3, 1, True),
        part(7, 0, False) + part(1, HALF, False),
        (part(8, 0, False) + part(6, 1, True)) + (part(2, HALF, False) + part(0, HALF + 1, True)),
    )
    for p in range(4):
        planes[p, 0:OPIX, :] = found[p]
        for i in range(HALF):
            at = (2 * i + p // 2) * WIDE + p % 2
            gblock[pl.ds(at, HALF, stride=2), :] = planes[p, i * HALF : (i + 1) * HALF, :]

    def add(row, value):
        sums[row : row + 1, :] += value

    def backward(i, carry):
        here = rows_at(i)
        gb = jnp.where(valid[here, :] > 0, gblock[here, :], 0.0)
        gred = gb.astype(BF16)
        add(7, col_sum(gred.astype(F32)))
        acc_r[...] += tn(gred, hidden_b[here, :])
        n2 = norm2_b[here, :]
        for j in range(FF // CH):
            lanes = slice(j * CH, (j + 1) * CH)
            gpre = (nt(gred, rw[lanes, :]) * slope[here, lanes]).astype(BF16)
            add(8 + j, col_sum(gpre.astype(F32)))
            gpre_b[:, lanes] = gpre
        acc_x[...] += tn(n2, gpre_b[...])
        gn2 = nt(gpre_b[...], xw[...])
        unit = xhat2[here, :]
        add(5, col_sum(gn2 * unit))
        add(6, col_sum(gn2))
        gy = gn2 * vec(5)
        gr = gb + rstd2[here, :] * (gy - lane_mean(gy) - unit * lane_mean(gy * unit))
        gresid[here, :] = gr
        gproj = gr.astype(BF16)
        add(4, col_sum(gproj.astype(F32)))
        acc_s[3] += tn(mixed_b[here, :], gproj)
        gm = nt(gproj, ow[...])
        gmixed[here, :] = gm
        add(20, col_sum(gm * branch_h[here, :]))
        add(21, col_sum(gm * branch_w[here, :]))
        add(22, col_sum(gm * branch_c[here, :]))
        return carry

    lax.fori_loop(0, STEPS, backward, 0)

    gmix = [sums[20 + j : 21 + j, :] for j in range(3)]
    inner_dot = mix[0] * gmix[0] + mix[1] * gmix[1] + mix[2] * gmix[2]
    glogit = [mix[j] * (gmix[j] - inner_dot) for j in range(3)]
    ginner = jnp.zeros((RED, 1), F32)
    for j in range(3):
        ginner += jnp.sum(exw[:, j * CH : (j + 1) * CH] * glogit[j], axis=1, keepdims=True)
        put(AT_EXCITE + RED * j, inner * glogit[j])
        sums[12 + j : 13 + j, :] = glogit[j]
    ginner = ginner * inner_slope
    put(AT_SQUEEZE, ginner * means)
    put(AT_SQ_BIAS, jnp.broadcast_to(ginner, (RED, CH)))
    gmeans = col_sum(sqt[...] * ginner) / count

    def branch_back(i, carry):
        here = rows_at(i)
        gm = gmixed[here, :]
        level = valid[here, :] * gmeans
        gh = (mix[0] * gm + level).astype(BF16)
        gw = (mix[1] * gm + level).astype(BF16)
        gc = (mix[2] * gm + level).astype(BF16)
        add(2, col_sum(gh.astype(F32)))
        add(3, col_sum(gw.astype(F32)))
        acc_s[0] += tn(rows_b[here, :], gh)
        acc_s[1] += tn(cols_b[here, :], gw)
        acc_s[2] += tn(norm_b[here, :], gc)
        grows[guarded(i), :] = nt(gh, hw[...])
        gcols[guarded(i), :] = nt(gw, ww[...])
        gnorm[here, :] = nt(gc, cw[...])
        return carry

    lax.fori_loop(0, STEPS, branch_back, 0)

    def last(i, carry):
        here = rows_at(i)
        by_row = vec(15)
        by_col = vec(16)
        plain = grows[guarded(i), :]
        above = grows[guarded(i, -WIDE), :]
        below = grows[guarded(i, WIDE), :]
        left, right = near(gcols, i)
        level = gcols[guarded(i), :]
        value = (
            gnorm[here, :]
            + jnp.where(by_row < 0, below, jnp.where(by_row > 0, above, plain))
            + jnp.where(by_col < 0, right, jnp.where(by_col > 0, left, level))
        )
        keep = valid[here, :] > 0
        value = jnp.where(keep, value, 0.0)
        unit = xhat[here, :]
        add(0, col_sum(value * unit))
        add(1, col_sum(value))
        gy = value * vec(0)
        back = rstd[here, :] * (gy - lane_mean(gy) - unit * lane_mean(gy * unit))
        grad[here, :] = jnp.where(keep, gresid[here, :] + back, 0.0)
        return carry

    lax.fori_loop(0, STEPS, last, 0)

    for j in range(FF // CH):
        put(AT_REDUCE + j * CH, acc_r[:, j * CH : (j + 1) * CH].T)
        put(AT_EXPAND + j * CH, acc_x[:, j * CH : (j + 1) * CH])
    for j, at in enumerate((AT_HEIGHT, AT_WIDTH, AT_CHANNEL, AT_OUTPUT)):
        put(at, acc_s[j])
    same = lax.broadcasted_iota(jnp.int32, (LANES, LANES), 0) == lax.broadcasted_iota(
        jnp.int32, (LANES, LANES), 1
    )
    for j in range(OTILE):
        add(15 + j, col_sum(jnp.where(same, kb_rows[j * LANES : (j + 1) * LANES, :], 0.0)))
    put(AT_VECTOR, sums[...])
    keep_out[...] = rows_out[0]
    send_out[...] = rows_out[1].astype(BF16)


def send_kernel(info, grad, section, out, tall, turned, stage):
    begin = pl.multiple_of(112 - info[0], 16)
    tall[0:112, :] = jnp.zeros((112, CH), F32)
    tall[112 + PIX :, :] = jnp.zeros((tall.shape[0] - 112 - PIX, CH), F32)
    for r in range(SIDE):
        tall[112 + r * SIDE : 112 + (r + 1) * SIDE, :] = grad[r * WIDE : r * WIDE + SIDE, :]
    for t in range(WIN):
        turned[:, t * LANES : (t + 1) * LANES] = tall[pl.ds(begin + t * LANES, LANES), :].T
    for s in range(out.shape[0]):
        base = s * PIXROWS
        for t in range(WIN):
            stage[base + 4 * t : base + 4 * t + 4, :] = turned[
                4 * s : 4 * s + 4, t * LANES : (t + 1) * LANES
            ]
        for j in range(OTILE):
            stage[base + 44 + 10 * j : base + 54 + 10 * j, :] = section[
                10 * s : 10 * s + 10, j * LANES : (j + 1) * LANES
            ]
        out[s] = stage[base : base + PIXROWS, :].astype(BF16)


def pair_kernel(kept, met, out):
    out[...] = (kept[...] + met[...].astype(F32)).astype(BF16)


def add_kernel(recv, out):
    total = recv[0].astype(F32)
    for s in range(1, recv.shape[0]):
        total += recv[s].astype(F32)
    out[...] = total.astype(BF16)


def copies_kernel(mine, one, two, three, out):
    total = (mine[...].astype(F32) + two[...].astype(F32)) + (
        one[...].astype(F32) + three[...].astype(F32)
    )
    total = total.astype(BF16)
    for s in range(out.shape[0]):
        out[s] = total


def pixel_kernel(info, near, far, feat, section, stage, recv):
    core = info[2]
    for i in range(near.shape[0]):
        recv[2 * i + core] = near[i]
        recv[2 * i + 1 - core] = far[i]
    for k in range(recv.shape[0]):
        piece = recv[k].astype(F32)
        tile = first_tile(k)
        for t in range(WIN):
            lanes = slice((tile + t) * LANES, (tile + t + 1) * LANES)
            value = piece[4 * t : 4 * t + 4, :]
            if t == 0 and k % 8:
                feat[:, lanes] += value
            else:
                feat[:, lanes] = value
        for j in range(OTILE):
            width = min(LANES, OPIX - j * LANES)
            at = k * OPIX + j * LANES
            stage[:, at : at + width] = piece[44 + 10 * j : 54 + 10 * j, 0:width]
    section[...] = stage[...].astype(BF16)


def weight_kernel(info, own, other, *refs):
    outs = refs[:-1]
    both = refs[-1]
    core = info[2]
    for i in range(own.shape[0]):
        both[2 * i + core] = own[i]
        both[2 * i + 1 - core] = other[i]

    def rows(at, count):
        found = []
        done = 0
        while done < count:
            chunk, inner = divmod(at + done, WROWS)
            size = min(count - done, WROWS - inner)
            found.append(both[chunk, inner : inner + size, :])
            done += size
        return jnp.concatenate(found).astype(F32)

    conv, red, exp, height, width, chan, outw, squeeze, excite, sq_bias = outs[:10]
    for t in range(9):
        conv[t] = rows(AT_CONV + t * OUT, OUT)
    red[...] = rows(AT_REDUCE, FF)
    for j in range(FF // CH):
        exp[:, j * CH : (j + 1) * CH] = rows(AT_EXPAND + j * CH, CH)
    for at, ref in (
        (AT_HEIGHT, height),
        (AT_WIDTH, width),
        (AT_CHANNEL, chan),
        (AT_OUTPUT, outw),
    ):
        ref[...] = rows(at, CH)
    squeeze[...] = rows(AT_SQUEEZE, RED)
    for j in range(3):
        excite[:, j * CH : (j + 1) * CH] = rows(AT_EXCITE + j * RED, RED)
    same = lax.broadcasted_iota(jnp.int32, (RED, CH), 0) == lax.broadcasted_iota(
        jnp.int32, (RED, CH), 1
    )
    sq_bias[...] = jnp.sum(jnp.where(same, rows(AT_SQ_BIAS, RED), 0.0), axis=0)[0:RED]
    vectors = rows(AT_VECTOR, RED)
    for ref, row in zip(outs[10:], VECTOR_ROWS):
        size = ref.shape[0]
        for j in range(-(-size // CH)):
            width = min(CH, size - j * CH)
            ref[j * CH : j * CH + width] = vectors[row + j, 0:width]


def body(
    features,
    size_group,
    cycle_offsets,
    norm_gain,
    norm_bias,
    height_weight,
    height_bias,
    width_weight,
    width_bias,
    channel_weight,
    squeeze_weight,
    squeeze_bias,
    excite_weight,
    excite_bias,
    output_weight,
    output_bias,
    second_gain,
    second_bias,
    expand_weight,
    expand_bias,
    reduce_weight,
    reduce_bias,
    stride_weight,
    stride_bias,
    cotangent,
):
    shards = lax.axis_size("ch")
    rank = lax.axis_index("ch")
    side = SIDE - 4 * (2 - lax.dynamic_index_in_dim(size_group, rank, keepdims=False))
    info = jnp.stack([16 * (rank % 8), side, rank % 2]).astype(jnp.int32)
    vecs = jnp.concatenate(
        [
            v.astype(F32)
            for v in (
                norm_gain,
                norm_bias,
                height_bias,
                width_bias,
                output_bias,
                second_gain,
                second_bias,
                reduce_bias,
                expand_bias,
                excite_bias,
                cycle_offsets[0],
                cycle_offsets[1],
            )
        ]
    ).reshape(17, CH)

    chunks = pl.pallas_call(
        pack_kernel,
        cost_estimate=cost(2.5),
        out_shape=jax.ShapeDtypeStruct((shards, PIXROWS, LANES), BF16),
        scratch_shapes=[
            pltpu.VMEM((shards * PIXROWS, LANES), F32),
            pltpu.VMEM(cotangent.shape, F32),
        ],
        compiler_params=params(),
    )(features, cotangent)
    arrived = lax.all_to_all(chunks, "ch", split_axis=0, concat_axis=0, tiled=True)

    canvas = pltpu.VMEM((FLAT, CH), F32)
    guarded = pltpu.VMEM((FLAT + 2 * GUARD, CH), F32)
    narrow = pltpu.VMEM((FLAT, CH), BF16)
    whole = pl.BlockSpec(memory_space=pltpu.VMEM)
    kept, sent, grad, section_part = pl.pallas_call(
        main_kernel,
        cost_estimate=cost(22),
        out_shape=(
            jax.ShapeDtypeStruct((shards // 2, WROWS, LANES), F32),
            jax.ShapeDtypeStruct((shards // 2, WROWS, LANES), BF16),
            jax.ShapeDtypeStruct((FLAT, CH), F32),
            jax.ShapeDtypeStruct((OUT, OTILE * LANES), F32),
        ),
        in_specs=[pl.BlockSpec(memory_space=pltpu.SMEM)] + [whole] * 13,
        out_specs=(whole,) * 4,
        scratch_shapes=[
            pltpu.VMEM((CH, WIN * LANES), F32),
            pltpu.VMEM((3 * LANES, OTILE * LANES), F32),
            pltpu.VMEM((112 + WIN * LANES, CH), F32),
            canvas,
            canvas,
            canvas,
            canvas,
            guarded,
            narrow,
            narrow,
            narrow,
            canvas,
            canvas,
            canvas,
            narrow,
            canvas,
            canvas,
            narrow,
            pltpu.VMEM((FLAT, FF), BF16),
            pltpu.VMEM((FLAT, FF), F32),
            guarded,
            pltpu.VMEM((OTILE * LANES, 9 * CH), F32),
            pltpu.VMEM((OTILE * LANES, 9 * CH), F32),
            pltpu.VMEM((4, 328, CH), F32),
            canvas,
            canvas,
            canvas,
            guarded,
            guarded,
            canvas,
            pltpu.VMEM((CH, FF), F32),
            pltpu.VMEM((CH, FF), F32),
            pltpu.VMEM((4, CH, CH), F32),
            pltpu.VMEM((RED, CH), F32),
            pltpu.VMEM((ROWS, FF), BF16),
            pltpu.VMEM((2, shards // 2, WROWS, LANES), F32),
        ],
        compiler_params=params(),
    )(
        info,
        arrived,
        vecs,
        squeeze_weight.astype(F32).T,
        squeeze_bias.astype(F32)[:, None],
        excite_weight.astype(F32),
        stride_bias.astype(F32)[:, None],
        height_weight,
        width_weight,
        channel_weight,
        output_weight,
        expand_weight,
        reduce_weight,
        stride_weight.reshape(OUT, 9 * CH),
    )
    other_core = [(i, i ^ 1) for i in range(shards)]
    same_core = [[2 * i + c for i in range(shards // 2)] for c in range(2)]
    met = lax.ppermute(sent, "ch", other_core)
    pixels = pl.pallas_call(
        send_kernel,
        cost_estimate=cost(2.5),
        out_shape=jax.ShapeDtypeStruct((shards, PIXROWS, LANES), BF16),
        in_specs=[pl.BlockSpec(memory_space=pltpu.SMEM)] + [whole] * 2,
        out_specs=whole,
        scratch_shapes=[
            pltpu.VMEM((112 + WIN * LANES, CH), F32),
            pltpu.VMEM((CH, WIN * LANES), F32),
            pltpu.VMEM((shards * PIXROWS, LANES), F32),
        ],
        compiler_params=params(),
    )(info, grad, section_part)
    kept, pixels = lax.optimization_barrier((kept, pixels))
    partial = pl.pallas_call(
        pair_kernel,
        cost_estimate=cost(2.3),
        out_shape=jax.ShapeDtypeStruct(kept.shape, BF16),
        compiler_params=params(),
    )(kept, met)

    def exchange(v):
        return lax.all_to_all(
            v, "ch", split_axis=0, concat_axis=0, tiled=True, axis_index_groups=same_core
        )

    parts = exchange(partial)
    parts, pixels = lax.optimization_barrier((parts, pixels))
    back = exchange(pixels.reshape(shards // 2, 2, PIXROWS, LANES))

    mine = pl.pallas_call(
        add_kernel,
        cost_estimate=cost(1.7),
        out_shape=jax.ShapeDtypeStruct((WROWS, LANES), BF16),
        compiler_params=params(),
    )(parts)
    groups = lax.axis_size("img")
    other = [
        lax.ppermute(mine, "img", [(i, (i + d) % groups) for i in range(groups)])
        for d in (1, 2, 3)
    ]
    copies = pl.pallas_call(
        copies_kernel,
        cost_estimate=cost(1.7),
        out_shape=jax.ShapeDtypeStruct((shards // 2, WROWS, LANES), BF16),
        compiler_params=params(),
    )(mine, *other)
    copies, back = lax.optimization_barrier((copies, back))
    own_half = exchange(copies)
    core = rank % 2
    near = lax.dynamic_index_in_dim(back, core, axis=1, keepdims=False)
    far = lax.dynamic_index_in_dim(back, 1 - core, axis=1, keepdims=False)
    far = lax.ppermute(far, "ch", other_core)

    features_grad, section = pl.pallas_call(
        pixel_kernel,
        cost_estimate=cost(2.5),
        out_shape=(
            jax.ShapeDtypeStruct(features.shape, F32),
            jax.ShapeDtypeStruct(cotangent.shape, BF16),
        ),
        in_specs=[pl.BlockSpec(memory_space=pltpu.SMEM)] + [whole] * 2,
        out_specs=(whole,) * 2,
        scratch_shapes=[
            pltpu.VMEM(cotangent.shape, F32),
            pltpu.VMEM((shards, PIXROWS, LANES), BF16),
        ],
        compiler_params=params(),
    )(info, near, far)

    own_half, features_grad, section = lax.optimization_barrier((own_half, features_grad, section))
    other_half = lax.ppermute(own_half, "ch", other_core)

    def like(*shape):
        return jax.ShapeDtypeStruct(shape, F32)

    (
        conv_grad,
        reduce_grad,
        expand_grad,
        height_grad,
        width_grad,
        channel_grad,
        output_grad,
        squeeze_grad,
        excite_grad,
        squeeze_bias_grad,
        norm_gain_grad,
        norm_bias_grad,
        height_bias_grad,
        width_bias_grad,
        output_bias_grad,
        second_gain_grad,
        second_bias_grad,
        reduce_bias_grad,
        expand_bias_grad,
        excite_bias_grad,
        conv_bias_grad,
    ) = pl.pallas_call(
        weight_kernel,
        cost_estimate=cost(2.8),
        out_shape=(
            like(9, OUT, CH),
            like(FF, CH),
            like(CH, FF),
            like(CH, CH),
            like(CH, CH),
            like(CH, CH),
            like(CH, CH),
            like(RED, CH),
            like(RED, 3 * CH),
            like(RED),
        )
        + tuple(like(size) for size in VECTOR_SIZES),
        in_specs=[pl.BlockSpec(memory_space=pltpu.SMEM)] + [whole] * 2,
        out_specs=(whole,) * 21,
        scratch_shapes=[pltpu.VMEM((shards, WROWS, LANES), BF16)],
        compiler_params=params(),
    )(info, own_half, other_half)
    return (
        section,
        features_grad,
        norm_gain_grad,
        norm_bias_grad,
        height_grad,
        height_bias_grad,
        width_grad,
        width_bias_grad,
        channel_grad,
        squeeze_grad.T,
        squeeze_bias_grad,
        excite_grad,
        excite_bias_grad,
        output_grad,
        output_bias_grad,
        second_gain_grad,
        second_bias_grad,
        expand_grad,
        expand_bias_grad,
        reduce_grad,
        reduce_bias_grad,
        jnp.transpose(conv_grad, (1, 0, 2)),
        conv_bias_grad,
    )


def solution(mesh):
    split = P("ch", "img")
    return jax.shard_map(
        body,
        mesh=mesh,
        in_specs=(split, P("img")) + (P(),) * 22 + (split,),
        out_specs=(split, split) + (P(),) * 21,
        check_vma=False,
    )
```

```python
import jax
import jax.numpy as jnp
from jax import lax
from jax.experimental import pallas as pl
from jax.experimental.pallas import tpu as pltpu
from jax.sharding import PartitionSpec as P

CH = 128
FF = 512
RED = 32
OUT = 320
SIDE = 36
PIX = SIDE * SIDE
HALF = SIDE // 2
OPIX = HALF * HALF
WIDE = 40
FLAT = SIDE * WIDE
GUARD = 48
ROWS = 288
STEPS = FLAT // ROWS
EPS = 1e-05
LANES = 128
WIN = 11
OTILE = 3
PIXROWS = 80
WROWS = 144

F32 = jnp.float32
BF16 = jnp.bfloat16

AT_CONV = 0
AT_REDUCE = 2880
AT_EXPAND = 3392
AT_HEIGHT = 3904
AT_WIDTH = 4032
AT_CHANNEL = 4160
AT_OUTPUT = 4288
AT_SQUEEZE = 4416
AT_EXCITE = 4448
AT_SQ_BIAS = 4544
AT_VECTOR = 4576
VECTOR_ROWS = (0, 1, 2, 3, 4, 5, 6, 7, 8, 12, 15)
VECTOR_SIZES = (CH,) * 8 + (FF, 3 * CH, OUT)


def params(mebibytes):
    return pltpu.CompilerParams(vmem_limit_bytes=mebibytes * 1024 * 1024)


def cost(micros):
    return pl.CostEstimate(flops=0, bytes_accessed=int(micros * 3.69e6), transcendentals=0)


def first_tile(k):
    return 10 * k + k // 8


def nn(a, b):
    return lax.dot_general(a, b, (((1,), (0,)), ((), ())), preferred_element_type=F32)


def nt(a, b):
    return lax.dot_general(a, b, (((1,), (1,)), ((), ())), preferred_element_type=F32)


def tn(a, b):
    return lax.dot_general(a, b, (((0,), (0,)), ((), ())), preferred_element_type=F32)


def lane_mean(v):
    return jnp.sum(v, axis=1, keepdims=True) * (1.0 / CH)


def col_sum(v):
    return jnp.sum(v, axis=0, keepdims=True)


def normal_parts(x):
    z = jnp.abs(x) * 0.7071067811865476
    t = 1.0 / (1.0 + 0.3275911 * z)
    bell = jnp.exp(-z * z)
    poly = 1.061405429 * t - 1.453152027
    poly = poly * t + 1.421413741
    poly = poly * t - 0.284496736
    poly = poly * t + 0.254829592
    tail = 0.5 * poly * t * bell
    return jnp.where(x < 0, tail, 1.0 - tail), bell * 0.3989422804014327


def pack_kernel(feat, cot, out, stage, cots):
    images = out.shape[0]
    cots[...] = cot[...].astype(F32)
    for k in range(images):
        base = k * PIXROWS
        begin = first_tile(k) * LANES
        for t in range(WIN):
            stage[base + 4 * t : base + 4 * t + 4, :] = feat[
                :, begin + t * LANES : begin + (t + 1) * LANES
            ].astype(F32)
        for j in range(OTILE):
            width = min(LANES, OPIX - j * LANES)
            at = k * OPIX + j * LANES
            row = base + 44 + 10 * j
            stage[row : row + 10, 0:width] = cots[:, at : at + width]
        out[k] = stage[base : base + PIXROWS, :].astype(BF16)


def main_kernel(
    info,
    recv,
    vecs,
    sqt,
    sqb,
    exw,
    kbias,
    hw,
    ww,
    cw,
    ow,
    xw,
    rw,
    kw,
    keep_out,
    send_out,
    grad,
    section_out,
    xf,
    cf,
    tall,
    canvas,
    valid,
    xhat,
    rstd,
    norm,
    rows_b,
    cols_b,
    norm_b,
    branch_h,
    branch_w,
    branch_c,
    mixed_b,
    xhat2,
    rstd2,
    norm2_b,
    hidden_b,
    slope,
    block,
    taps,
    spread,
    planes,
    gblock,
    gresid,
    gmixed,
    grows,
    gcols,
    gnorm,
    acc_r,
    acc_x,
    acc_s,
    sums,
    gpre_b,
    rows_out,
):
    shift = info[0]
    side = info[1]
    core = info[2]

    def vec(i):
        return vecs[i : i + 1, :]

    def put(row, value):
        count = value.shape[0]
        done = 0
        while done < count:
            chunk, inner = divmod(row + done, WROWS)
            size = min(count - done, WROWS - inner)
            slot = core if chunk % 2 == 0 else 1 - core
            rows_out[slot, chunk // 2, inner : inner + size, :] = value[done : done + size, :]
            done += size

    cf[...] = jnp.zeros_like(cf)
    for s in range(recv.shape[0]):
        piece = recv[s].astype(F32)
        for t in range(WIN):
            xf[4 * s : 4 * s + 4, t * LANES : (t + 1) * LANES] = piece[4 * t : 4 * t + 4, :]
        for j in range(OTILE):
            cf[10 * s : 10 * s + 10, j * LANES : (j + 1) * LANES] = piece[
                44 + 10 * j : 54 + 10 * j, :
            ]
    begin = pl.multiple_of(112 - shift, 16)
    for t in range(WIN):
        tall[pl.ds(begin + t * LANES, LANES), :] = xf[:, t * LANES : (t + 1) * LANES].T

    column = lax.broadcasted_iota(jnp.int32, (WIDE, CH), 0)
    for r in range(SIDE):
        keep = (column < side) & (r < side)
        canvas[r * WIDE : (r + 1) * WIDE, :] = jnp.where(
            keep, tall[112 + r * SIDE : 112 + r * SIDE + WIDE, :], 0.0
        )
        valid[r * WIDE : (r + 1) * WIDE, :] = jnp.where(keep, 1.0, 0.0)
    edge = jnp.zeros((GUARD, CH), F32)
    for ref in (norm, block, grows, gcols):
        ref[0:GUARD, :] = edge
        ref[GUARD + FLAT : FLAT + 2 * GUARD, :] = edge
    acc_r[...] = jnp.zeros_like(acc_r)
    acc_x[...] = jnp.zeros_like(acc_x)
    acc_s[...] = jnp.zeros_like(acc_s)
    sums[...] = jnp.zeros_like(sums)

    def rows_at(i):
        return pl.ds(pl.multiple_of(i * ROWS, 16), ROWS)

    def guarded(i, extra=0, size=ROWS):
        return pl.ds(pl.multiple_of(i * ROWS + GUARD + extra, 8), size)

    def first_norm(i, carry):
        here = rows_at(i)
        x = canvas[here, :]
        center = x - lane_mean(x)
        scale = lax.rsqrt(lane_mean(center * center) + EPS)
        unit = center * scale
        xhat[here, :] = unit
        rstd[here, :] = jnp.broadcast_to(scale, unit.shape)
        value = jnp.where(valid[here, :] > 0, unit * vec(0) + vec(1), 0.0)
        norm[guarded(i), :] = value.astype(BF16).astype(F32)
        return carry

    lax.fori_loop(0, STEPS, first_norm, 0)

    def near(ref, i):
        wide = ref[guarded(i, -8, ROWS + 16), :]
        back = pltpu.roll(wide, 1, 0)[8 : 8 + ROWS, :]
        ahead = pltpu.roll(wide, ROWS + 15, 0)[8 : 8 + ROWS, :]
        return back, ahead

    def branches(i, total):
        here = rows_at(i)
        plain = norm[guarded(i), :]
        above = norm[guarded(i, -WIDE), :]
        below = norm[guarded(i, WIDE), :]
        left, right = near(norm, i)
        by_row = vec(15)
        by_col = vec(16)
        sr = jnp.where(by_row < 0, above, jnp.where(by_row > 0, below, plain)).astype(BF16)
        sc = jnp.where(by_col < 0, left, jnp.where(by_col > 0, right, plain)).astype(BF16)
        nb = plain.astype(BF16)
        rows_b[here, :] = sr
        cols_b[here, :] = sc
        norm_b[here, :] = nb
        bh = nn(sr, hw[...]) + vec(2)
        bw = nn(sc, ww[...]) + vec(3)
        bc = nn(nb, cw[...])
        branch_h[here, :] = bh
        branch_w[here, :] = bw
        branch_c[here, :] = bc
        return total + col_sum(valid[here, :] * (bh + bw + bc))

    total = lax.fori_loop(0, STEPS, branches, jnp.zeros((1, CH), F32))

    count = jnp.full((1, CH), side * side, jnp.int32).astype(F32)
    means = total / count
    inner_pre = jnp.sum(sqt[...] * means, axis=1, keepdims=True) + sqb[...]
    inner_cdf, inner_density = normal_parts(inner_pre)
    inner = inner_pre * inner_cdf
    inner_slope = inner_cdf + inner_pre * inner_density
    logit = [col_sum(exw[:, j * CH : (j + 1) * CH] * inner) + vec(12 + j) for j in range(3)]
    top = jnp.maximum(jnp.maximum(logit[0], logit[1]), logit[2])
    grown = [jnp.exp(v - top) for v in logit]
    whole = grown[0] + grown[1] + grown[2]
    mix = [v / whole for v in grown]

    def forward(i, carry):
        here = rows_at(i)
        mixed = mix[0] * branch_h[here, :] + mix[1] * branch_w[here, :] + mix[2] * branch_c[here, :]
        mixed = mixed.astype(BF16)
        mixed_b[here, :] = mixed
        resid = canvas[here, :] + nn(mixed, ow[...]) + vec(4)
        center = resid - lane_mean(resid)
        scale = lax.rsqrt(lane_mean(center * center) + EPS)
        unit = center * scale
        xhat2[here, :] = unit
        rstd2[here, :] = jnp.broadcast_to(scale, unit.shape)
        n2 = (unit * vec(5) + vec(6)).astype(BF16)
        norm2_b[here, :] = n2
        total2 = resid + vec(7)
        for j in range(FF // CH):
            lanes = slice(j * CH, (j + 1) * CH)
            pre = nn(n2, xw[:, lanes]) + vec(8 + j)
            cdf, density = normal_parts(pre)
            hid = (pre * cdf).astype(BF16)
            hidden_b[here, lanes] = hid
            slope[here, lanes] = cdf + pre * density
        total2 = total2 + nn(hidden_b[here, :], rw[...])
        value = jnp.where(valid[here, :] > 0, total2, 0.0)
        block[guarded(i), :] = value.astype(BF16).astype(F32)
        return carry

    lax.fori_loop(0, STEPS, forward, 0)

    taps[OPIX:, :] = jnp.zeros((taps.shape[0] - OPIX, taps.shape[1]), F32)
    for a in range(3):
        for b in range(3):
            lanes = slice((3 * a + b) * CH, (3 * a + b + 1) * CH)
            for i in range(HALF):
                at = GUARD + (2 * i + a - 1) * WIDE + b - 1
                taps[i * HALF : (i + 1) * HALF, lanes] = block[pl.ds(at, HALF, stride=2), :]
    tap_b = taps[...].astype(BF16)
    index = lax.broadcasted_iota(jnp.int32, (1, OTILE * LANES), 1)
    out_row = ((index.astype(F32) + 0.5) * (1.0 / HALF)).astype(jnp.int32)
    out_col = index - out_row * HALF
    out_keep = (2 * out_row < side) & (2 * out_col < side)
    cot = jnp.where(out_keep, cf[...], 0.0)
    cot_b = cot[0:OUT, :].astype(BF16)
    cot_t = cot.T.astype(BF16)[:, 0:OUT]
    section = nt(kw[...], tap_b) + kbias[...]
    section_out[...] = jnp.where(out_keep, section, 0.0)
    conv = nn(cot_b, tap_b)
    for t in range(9):
        put(AT_CONV + t * OUT, conv[:, t * CH : (t + 1) * CH])
    kb_rows = jnp.sum(cot, axis=1, keepdims=True)
    spread[...] = nn(cot_t, kw[...])
    row_id = lax.broadcasted_iota(jnp.int32, (OPIX, CH), 0)
    row_of = ((row_id.astype(F32) + 0.5) * (1.0 / HALF)).astype(jnp.int32)
    inside = row_id - row_of * HALF < HALF - 1

    def part(tap, ahead, masked):
        value = spread[ahead : ahead + OPIX, tap * CH : (tap + 1) * CH]
        return jnp.where(inside, value, 0.0) if masked else value

    found = (
        part(4, 0, False),
        part(5, 0, False) + part(3, 1, True),
        part(7, 0, False) + part(1, HALF, False),
        (part(8, 0, False) + part(6, 1, True)) + (part(2, HALF, False) + part(0, HALF + 1, True)),
    )
    for p in range(4):
        planes[p, 0:OPIX, :] = found[p]
        for i in range(HALF):
            at = (2 * i + p // 2) * WIDE + p % 2
            gblock[pl.ds(at, HALF, stride=2), :] = planes[p, i * HALF : (i + 1) * HALF, :]

    def add(row, value):
        sums[row : row + 1, :] += value

    def backward(i, carry):
        here = rows_at(i)
        gb = jnp.where(valid[here, :] > 0, gblock[here, :], 0.0)
        gred = gb.astype(BF16)
        add(7, col_sum(gred.astype(F32)))
        acc_r[...] += tn(gred, hidden_b[here, :])
        n2 = norm2_b[here, :]
        for j in range(FF // CH):
            lanes = slice(j * CH, (j + 1) * CH)
            gpre = (nt(gred, rw[lanes, :]) * slope[here, lanes]).astype(BF16)
            add(8 + j, col_sum(gpre.astype(F32)))
            gpre_b[:, lanes] = gpre
        acc_x[...] += tn(n2, gpre_b[...])
        gn2 = nt(gpre_b[...], xw[...])
        unit = xhat2[here, :]
        add(5, col_sum(gn2 * unit))
        add(6, col_sum(gn2))
        gy = gn2 * vec(5)
        gr = gb + rstd2[here, :] * (gy - lane_mean(gy) - unit * lane_mean(gy * unit))
        gresid[here, :] = gr
        gproj = gr.astype(BF16)
        add(4, col_sum(gproj.astype(F32)))
        acc_s[3] += tn(mixed_b[here, :], gproj)
        gm = nt(gproj, ow[...])
        gmixed[here, :] = gm
        add(20, col_sum(gm * branch_h[here, :]))
        add(21, col_sum(gm * branch_w[here, :]))
        add(22, col_sum(gm * branch_c[here, :]))
        return carry

    lax.fori_loop(0, STEPS, backward, 0)

    gmix = [sums[20 + j : 21 + j, :] for j in range(3)]
    inner_dot = mix[0] * gmix[0] + mix[1] * gmix[1] + mix[2] * gmix[2]
    glogit = [mix[j] * (gmix[j] - inner_dot) for j in range(3)]
    ginner = jnp.zeros((RED, 1), F32)
    for j in range(3):
        ginner += jnp.sum(exw[:, j * CH : (j + 1) * CH] * glogit[j], axis=1, keepdims=True)
        put(AT_EXCITE + RED * j, inner * glogit[j])
        sums[12 + j : 13 + j, :] = glogit[j]
    ginner = ginner * inner_slope
    put(AT_SQUEEZE, ginner * means)
    put(AT_SQ_BIAS, jnp.broadcast_to(ginner, (RED, CH)))
    gmeans = col_sum(sqt[...] * ginner) / count

    def branch_back(i, carry):
        here = rows_at(i)
        gm = gmixed[here, :]
        level = valid[here, :] * gmeans
        gh = (mix[0] * gm + level).astype(BF16)
        gw = (mix[1] * gm + level).astype(BF16)
        gc = (mix[2] * gm + level).astype(BF16)
        add(2, col_sum(gh.astype(F32)))
        add(3, col_sum(gw.astype(F32)))
        acc_s[0] += tn(rows_b[here, :], gh)
        acc_s[1] += tn(cols_b[here, :], gw)
        acc_s[2] += tn(norm_b[here, :], gc)
        grows[guarded(i), :] = nt(gh, hw[...])
        gcols[guarded(i), :] = nt(gw, ww[...])
        gnorm[here, :] = nt(gc, cw[...])
        return carry

    lax.fori_loop(0, STEPS, branch_back, 0)

    def last(i, carry):
        here = rows_at(i)
        by_row = vec(15)
        by_col = vec(16)
        plain = grows[guarded(i), :]
        above = grows[guarded(i, -WIDE), :]
        below = grows[guarded(i, WIDE), :]
        left, right = near(gcols, i)
        level = gcols[guarded(i), :]
        value = (
            gnorm[here, :]
            + jnp.where(by_row < 0, below, jnp.where(by_row > 0, above, plain))
            + jnp.where(by_col < 0, right, jnp.where(by_col > 0, left, level))
        )
        keep = valid[here, :] > 0
        value = jnp.where(keep, value, 0.0)
        unit = xhat[here, :]
        add(0, col_sum(value * unit))
        add(1, col_sum(value))
        gy = value * vec(0)
        back = rstd[here, :] * (gy - lane_mean(gy) - unit * lane_mean(gy * unit))
        grad[here, :] = jnp.where(keep, gresid[here, :] + back, 0.0)
        return carry

    lax.fori_loop(0, STEPS, last, 0)

    for j in range(FF // CH):
        put(AT_REDUCE + j * CH, acc_r[:, j * CH : (j + 1) * CH].T)
        put(AT_EXPAND + j * CH, acc_x[:, j * CH : (j + 1) * CH])
    for j, at in enumerate((AT_HEIGHT, AT_WIDTH, AT_CHANNEL, AT_OUTPUT)):
        put(at, acc_s[j])
    same = lax.broadcasted_iota(jnp.int32, (LANES, LANES), 0) == lax.broadcasted_iota(
        jnp.int32, (LANES, LANES), 1
    )
    for j in range(OTILE):
        add(15 + j, col_sum(jnp.where(same, kb_rows[j * LANES : (j + 1) * LANES, :], 0.0)))
    put(AT_VECTOR, sums[...])
    keep_out[...] = rows_out[0]
    send_out[...] = rows_out[1].astype(BF16)


def send_kernel(info, grad, section, out, tall, turned, stage):
    begin = pl.multiple_of(112 - info[0], 16)
    tall[0:112, :] = jnp.zeros((112, CH), F32)
    tall[112 + PIX :, :] = jnp.zeros((tall.shape[0] - 112 - PIX, CH), F32)
    for r in range(SIDE):
        tall[112 + r * SIDE : 112 + (r + 1) * SIDE, :] = grad[r * WIDE : r * WIDE + SIDE, :]
    for t in range(WIN):
        turned[:, t * LANES : (t + 1) * LANES] = tall[pl.ds(begin + t * LANES, LANES), :].T
    for s in range(out.shape[0]):
        base = s * PIXROWS
        for t in range(WIN):
            stage[base + 4 * t : base + 4 * t + 4, :] = turned[
                4 * s : 4 * s + 4, t * LANES : (t + 1) * LANES
            ]
        for j in range(OTILE):
            stage[base + 44 + 10 * j : base + 54 + 10 * j, :] = section[
                10 * s : 10 * s + 10, j * LANES : (j + 1) * LANES
            ]
        out[s] = stage[base : base + PIXROWS, :].astype(BF16)


def pair_kernel(kept, met, out):
    out[...] = (kept[...] + met[...].astype(F32)).astype(BF16)


def add_kernel(recv, out):
    total = recv[0].astype(F32)
    for s in range(1, recv.shape[0]):
        total += recv[s].astype(F32)
    out[...] = total.astype(BF16)


def copies_kernel(mine, one, two, three, out):
    total = (mine[...].astype(F32) + two[...].astype(F32)) + (
        one[...].astype(F32) + three[...].astype(F32)
    )
    total = total.astype(BF16)
    for s in range(out.shape[0]):
        out[s] = total


def pixel_kernel(info, near, far, feat, section, stage, recv):
    core = info[2]
    for i in range(near.shape[0]):
        recv[2 * i + core] = near[i]
        recv[2 * i + 1 - core] = far[i]
    for k in range(recv.shape[0]):
        piece = recv[k].astype(F32)
        tile = first_tile(k)
        for t in range(WIN):
            lanes = slice((tile + t) * LANES, (tile + t + 1) * LANES)
            value = piece[4 * t : 4 * t + 4, :]
            if t == 0 and k % 8:
                feat[:, lanes] += value
            else:
                feat[:, lanes] = value
        for j in range(OTILE):
            width = min(LANES, OPIX - j * LANES)
            at = k * OPIX + j * LANES
            stage[:, at : at + width] = piece[44 + 10 * j : 54 + 10 * j, 0:width]
    section[...] = stage[...].astype(BF16)


def weight_kernel(info, own, other, *refs):
    outs = refs[:-1]
    both = refs[-1]
    core = info[2]
    for i in range(own.shape[0]):
        both[2 * i + core] = own[i]
        both[2 * i + 1 - core] = other[i]

    def rows(at, count):
        found = []
        done = 0
        while done < count:
            chunk, inner = divmod(at + done, WROWS)
            size = min(count - done, WROWS - inner)
            found.append(both[chunk, inner : inner + size, :])
            done += size
        return jnp.concatenate(found).astype(F32)

    conv, red, exp, height, width, chan, outw, squeeze, excite, sq_bias = outs[:10]
    for t in range(9):
        conv[t] = rows(AT_CONV + t * OUT, OUT)
    red[...] = rows(AT_REDUCE, FF)
    for j in range(FF // CH):
        exp[:, j * CH : (j + 1) * CH] = rows(AT_EXPAND + j * CH, CH)
    for at, ref in (
        (AT_HEIGHT, height),
        (AT_WIDTH, width),
        (AT_CHANNEL, chan),
        (AT_OUTPUT, outw),
    ):
        ref[...] = rows(at, CH)
    squeeze[...] = rows(AT_SQUEEZE, RED)
    for j in range(3):
        excite[:, j * CH : (j + 1) * CH] = rows(AT_EXCITE + j * RED, RED)
    same = lax.broadcasted_iota(jnp.int32, (RED, CH), 0) == lax.broadcasted_iota(
        jnp.int32, (RED, CH), 1
    )
    sq_bias[...] = jnp.sum(jnp.where(same, rows(AT_SQ_BIAS, RED), 0.0), axis=0)[0:RED]
    vectors = rows(AT_VECTOR, RED)
    for ref, row in zip(outs[10:], VECTOR_ROWS):
        size = ref.shape[0]
        for j in range(-(-size // CH)):
            width = min(CH, size - j * CH)
            ref[j * CH : j * CH + width] = vectors[row + j, 0:width]


def body(
    features,
    size_group,
    cycle_offsets,
    norm_gain,
    norm_bias,
    height_weight,
    height_bias,
    width_weight,
    width_bias,
    channel_weight,
    squeeze_weight,
    squeeze_bias,
    excite_weight,
    excite_bias,
    output_weight,
    output_bias,
    second_gain,
    second_bias,
    expand_weight,
    expand_bias,
    reduce_weight,
    reduce_bias,
    stride_weight,
    stride_bias,
    cotangent,
):
    shards = lax.axis_size("ch")
    rank = lax.axis_index("ch")
    side = SIDE - 4 * (2 - lax.dynamic_index_in_dim(size_group, rank, keepdims=False))
    info = jnp.stack([16 * (rank % 8), side, rank % 2]).astype(jnp.int32)
    vecs = jnp.concatenate(
        [
            v.astype(F32)
            for v in (
                norm_gain,
                norm_bias,
                height_bias,
                width_bias,
                output_bias,
                second_gain,
                second_bias,
                reduce_bias,
                expand_bias,
                excite_bias,
                cycle_offsets[0],
                cycle_offsets[1],
            )
        ]
    ).reshape(17, CH)

    chunks = pl.pallas_call(
        pack_kernel,
        cost_estimate=cost(2.5),
        out_shape=jax.ShapeDtypeStruct((shards, PIXROWS, LANES), BF16),
        scratch_shapes=[
            pltpu.VMEM((shards * PIXROWS, LANES), F32),
            pltpu.VMEM(cotangent.shape, F32),
        ],
        compiler_params=params(8),
    )(features, cotangent)
    arrived = lax.all_to_all(chunks, "ch", split_axis=0, concat_axis=0, tiled=True)

    canvas = pltpu.VMEM((FLAT, CH), F32)
    guarded = pltpu.VMEM((FLAT + 2 * GUARD, CH), F32)
    narrow = pltpu.VMEM((FLAT, CH), BF16)
    whole = pl.BlockSpec(memory_space=pltpu.VMEM)
    kept, sent, grad, section_part = pl.pallas_call(
        main_kernel,
        cost_estimate=cost(22),
        out_shape=(
            jax.ShapeDtypeStruct((shards // 2, WROWS, LANES), F32),
            jax.ShapeDtypeStruct((shards // 2, WROWS, LANES), BF16),
            jax.ShapeDtypeStruct((FLAT, CH), F32),
            jax.ShapeDtypeStruct((OUT, OTILE * LANES), F32),
        ),
        in_specs=[pl.BlockSpec(memory_space=pltpu.SMEM)] + [whole] * 13,
        out_specs=(whole,) * 4,
        scratch_shapes=[
            pltpu.VMEM((CH, WIN * LANES), F32),
            pltpu.VMEM((3 * LANES, OTILE * LANES), F32),
            pltpu.VMEM((112 + WIN * LANES, CH), F32),
            canvas,
            canvas,
            canvas,
            canvas,
            guarded,
            narrow,
            narrow,
            narrow,
            canvas,
            canvas,
            canvas,
            narrow,
            canvas,
            canvas,
            narrow,
            pltpu.VMEM((FLAT, FF), BF16),
            pltpu.VMEM((FLAT, FF), F32),
            guarded,
            pltpu.VMEM((OTILE * LANES, 9 * CH), F32),
            pltpu.VMEM((OTILE * LANES, 9 * CH), F32),
            pltpu.VMEM((4, 328, CH), F32),
            canvas,
            canvas,
            canvas,
            guarded,
            guarded,
            canvas,
            pltpu.VMEM((CH, FF), F32),
            pltpu.VMEM((CH, FF), F32),
            pltpu.VMEM((4, CH, CH), F32),
            pltpu.VMEM((RED, CH), F32),
            pltpu.VMEM((ROWS, FF), BF16),
            pltpu.VMEM((2, shards // 2, WROWS, LANES), F32),
        ],
        compiler_params=params(42),
    )(
        info,
        arrived,
        vecs,
        squeeze_weight.astype(F32).T,
        squeeze_bias.astype(F32)[:, None],
        excite_weight.astype(F32),
        stride_bias.astype(F32)[:, None],
        height_weight,
        width_weight,
        channel_weight,
        output_weight,
        expand_weight,
        reduce_weight,
        stride_weight.reshape(OUT, 9 * CH),
    )
    other_core = [(i, i ^ 1) for i in range(shards)]
    same_core = [[2 * i + c for i in range(shards // 2)] for c in range(2)]
    met = lax.ppermute(sent, "ch", other_core)
    pixels = pl.pallas_call(
        send_kernel,
        cost_estimate=cost(2.5),
        out_shape=jax.ShapeDtypeStruct((shards, PIXROWS, LANES), BF16),
        in_specs=[pl.BlockSpec(memory_space=pltpu.SMEM)] + [whole] * 2,
        out_specs=whole,
        scratch_shapes=[
            pltpu.VMEM((112 + WIN * LANES, CH), F32),
            pltpu.VMEM((CH, WIN * LANES), F32),
            pltpu.VMEM((shards * PIXROWS, LANES), F32),
        ],
        compiler_params=params(10),
    )(info, grad, section_part)
    kept, pixels = lax.optimization_barrier((kept, pixels))
    partial = pl.pallas_call(
        pair_kernel,
        cost_estimate=cost(2.3),
        out_shape=jax.ShapeDtypeStruct(kept.shape, BF16),
        compiler_params=params(8),
    )(kept, met)

    def exchange(v):
        return lax.all_to_all(
            v, "ch", split_axis=0, concat_axis=0, tiled=True, axis_index_groups=same_core
        )

    parts = exchange(partial)
    parts, pixels = lax.optimization_barrier((parts, pixels))
    back = exchange(pixels.reshape(shards // 2, 2, PIXROWS, LANES))

    mine = pl.pallas_call(
        add_kernel,
        cost_estimate=cost(1.7),
        out_shape=jax.ShapeDtypeStruct((WROWS, LANES), BF16),
        compiler_params=params(4),
    )(parts)
    groups = lax.axis_size("img")
    other = [
        lax.ppermute(mine, "img", [(i, (i + d) % groups) for i in range(groups)])
        for d in (1, 2, 3)
    ]
    copies = pl.pallas_call(
        copies_kernel,
        cost_estimate=cost(1.7),
        out_shape=jax.ShapeDtypeStruct((shards // 2, WROWS, LANES), BF16),
        compiler_params=params(4),
    )(mine, *other)
    copies, back = lax.optimization_barrier((copies, back))
    own_half = exchange(copies)
    core = rank % 2
    near = lax.dynamic_index_in_dim(back, core, axis=1, keepdims=False)
    far = lax.dynamic_index_in_dim(back, 1 - core, axis=1, keepdims=False)
    far = lax.ppermute(far, "ch", other_core)

    features_grad, section = pl.pallas_call(
        pixel_kernel,
        cost_estimate=cost(2.5),
        out_shape=(
            jax.ShapeDtypeStruct(features.shape, F32),
            jax.ShapeDtypeStruct(cotangent.shape, BF16),
        ),
        in_specs=[pl.BlockSpec(memory_space=pltpu.SMEM)] + [whole] * 2,
        out_specs=(whole,) * 2,
        scratch_shapes=[
            pltpu.VMEM(cotangent.shape, F32),
            pltpu.VMEM((shards, PIXROWS, LANES), BF16),
        ],
        compiler_params=params(8),
    )(info, near, far)

    own_half, features_grad, section = lax.optimization_barrier((own_half, features_grad, section))
    other_half = lax.ppermute(own_half, "ch", other_core)

    def like(*shape):
        return jax.ShapeDtypeStruct(shape, F32)

    (
        conv_grad,
        reduce_grad,
        expand_grad,
        height_grad,
        width_grad,
        channel_grad,
        output_grad,
        squeeze_grad,
        excite_grad,
        squeeze_bias_grad,
        norm_gain_grad,
        norm_bias_grad,
        height_bias_grad,
        width_bias_grad,
        output_bias_grad,
        second_gain_grad,
        second_bias_grad,
        reduce_bias_grad,
        expand_bias_grad,
        excite_bias_grad,
        conv_bias_grad,
    ) = pl.pallas_call(
        weight_kernel,
        cost_estimate=cost(2.8),
        out_shape=(
            like(9, OUT, CH),
            like(FF, CH),
            like(CH, FF),
            like(CH, CH),
            like(CH, CH),
            like(CH, CH),
            like(CH, CH),
            like(RED, CH),
            like(RED, 3 * CH),
            like(RED),
        )
        + tuple(like(size) for size in VECTOR_SIZES),
        in_specs=[pl.BlockSpec(memory_space=pltpu.SMEM)] + [whole] * 2,
        out_specs=(whole,) * 21,
        scratch_shapes=[pltpu.VMEM((shards, WROWS, LANES), BF16)],
        compiler_params=params(12),
    )(info, own_half, other_half)
    return (
        section,
        features_grad,
        norm_gain_grad,
        norm_bias_grad,
        height_grad,
        height_bias_grad,
        width_grad,
        width_bias_grad,
        channel_grad,
        squeeze_grad.T,
        squeeze_bias_grad,
        excite_grad,
        excite_bias_grad,
        output_grad,
        output_bias_grad,
        second_gain_grad,
        second_bias_grad,
        expand_grad,
        expand_bias_grad,
        reduce_grad,
        reduce_bias_grad,
        jnp.transpose(conv_grad, (1, 0, 2)),
        conv_bias_grad,
    )


def solution(mesh):
    split = P("ch", "img")
    return jax.shard_map(
        body,
        mesh=mesh,
        in_specs=(split, P("img")) + (P(),) * 22 + (split,),
        out_specs=(split, split) + (P(),) * 21,
        check_vma=False,
    )
```

```python
import jax
import jax.numpy as jnp
from jax import lax
from jax.experimental import pallas as pl
from jax.experimental.pallas import tpu as pltpu
from jax.sharding import PartitionSpec as P

CH = 128
FF = 512
RED = 32
OUT = 320
SIDE = 36
PIX = SIDE * SIDE
HALF = SIDE // 2
OPIX = HALF * HALF
WIDE = 40
FLAT = SIDE * WIDE
GUARD = 48
ROWS = 1440
STEPS = FLAT // ROWS
EPS = 1e-05
LANES = 128
WIN = 11
OTILE = 3
PIXROWS = 80
WROWS = 144

F32 = jnp.float32
BF16 = jnp.bfloat16

AT_CONV = 0
AT_REDUCE = 2880
AT_EXPAND = 3392
AT_HEIGHT = 3904
AT_WIDTH = 4032
AT_CHANNEL = 4160
AT_OUTPUT = 4288
AT_SQUEEZE = 4416
AT_EXCITE = 4448
AT_SQ_BIAS = 4544
AT_VECTOR = 4576
VECTOR_ROWS = (0, 1, 2, 3, 4, 5, 6, 7, 8, 12, 15)
VECTOR_SIZES = (CH,) * 8 + (FF, 3 * CH, OUT)


def params(mebibytes):
    return pltpu.CompilerParams(vmem_limit_bytes=mebibytes * 1024 * 1024)


def cost(micros):
    return pl.CostEstimate(flops=0, bytes_accessed=int(micros * 3.69e6), transcendentals=0)


def first_tile(k):
    return 10 * k + k // 8


def nn(a, b):
    return lax.dot_general(a, b, (((1,), (0,)), ((), ())), preferred_element_type=F32)


def nt(a, b):
    return lax.dot_general(a, b, (((1,), (1,)), ((), ())), preferred_element_type=F32)


def tn(a, b):
    return lax.dot_general(a, b, (((0,), (0,)), ((), ())), preferred_element_type=F32)


def lane_mean(v):
    return jnp.sum(v, axis=1, keepdims=True) * (1.0 / CH)


def col_sum(v):
    return jnp.sum(v, axis=0, keepdims=True)


def normal_parts(x):
    cdf = 0.5 + 0.5 * lax.erf(x * 0.7071067811865476)
    return cdf, (x * 0.3989422804014327) * jnp.exp(x * (x * -0.5))


def pack_kernel(feat_hbm, cot_hbm, out, stage, cots, feat, cot, ready):
    images = out.shape[0]
    first = pltpu.make_async_copy(feat_hbm, feat, ready.at[0])
    second = pltpu.make_async_copy(cot_hbm, cot, ready.at[1])
    first.start()
    second.start()
    first.wait()
    for k in range(images):
        base = k * PIXROWS
        begin = first_tile(k) * LANES
        for t in range(WIN):
            stage[base + 4 * t : base + 4 * t + 4, :] = feat[
                :, begin + t * LANES : begin + (t + 1) * LANES
            ].astype(F32)
    second.wait()
    cots[...] = cot[...].astype(F32)
    for k in range(images):
        base = k * PIXROWS
        for j in range(OTILE):
            width = min(LANES, OPIX - j * LANES)
            at = k * OPIX + j * LANES
            row = base + 44 + 10 * j
            stage[row : row + 10, 0:width] = cots[:, at : at + width]
        out[k] = stage[base : base + PIXROWS, :].astype(BF16)


def main_kernel(
    info,
    recv,
    vecs,
    sqt,
    sqb,
    exw,
    kbias,
    hw,
    ww,
    cw,
    ow,
    xw,
    rw,
    kw,
    keep_out,
    send_out,
    grad,
    section_out,
    xf,
    cf,
    tall,
    canvas,
    valid,
    xhat,
    rstd,
    norm,
    rows_b,
    cols_b,
    norm_b,
    branch_h,
    branch_w,
    branch_c,
    mixed_b,
    xhat2,
    rstd2,
    norm2_b,
    hidden_b,
    slope,
    block,
    taps,
    spread,
    planes,
    gblock,
    gresid,
    gmixed,
    grows,
    gcols,
    gnorm,
    acc_r,
    acc_x,
    acc_s,
    sums,
    gpre_b,
    rows_out,
):
    shift = info[0]
    side = info[1]
    core = info[2]

    def vec(i):
        return vecs[i : i + 1, :]

    def put(row, value):
        count = value.shape[0]
        done = 0
        while done < count:
            chunk, inner = divmod(row + done, WROWS)
            size = min(count - done, WROWS - inner)
            slot = core if chunk % 2 == 0 else 1 - core
            rows_out[slot, chunk // 2, inner : inner + size, :] = value[done : done + size, :]
            done += size

    cf[...] = jnp.zeros_like(cf)
    for s in range(recv.shape[0]):
        piece = recv[s].astype(F32)
        for t in range(WIN):
            xf[4 * s : 4 * s + 4, t * LANES : (t + 1) * LANES] = piece[4 * t : 4 * t + 4, :]
        for j in range(OTILE):
            cf[10 * s : 10 * s + 10, j * LANES : (j + 1) * LANES] = piece[
                44 + 10 * j : 54 + 10 * j, :
            ]
    begin = pl.multiple_of(112 - shift, 16)
    for t in range(WIN):
        tall[pl.ds(begin + t * LANES, LANES), :] = xf[:, t * LANES : (t + 1) * LANES].T

    column = lax.broadcasted_iota(jnp.int32, (WIDE, CH), 0)
    for r in range(SIDE):
        keep = (column < side) & (r < side)
        canvas[r * WIDE : (r + 1) * WIDE, :] = jnp.where(
            keep, tall[112 + r * SIDE : 112 + r * SIDE + WIDE, :], 0.0
        )
        valid[r * WIDE : (r + 1) * WIDE, :] = jnp.where(keep, 1.0, 0.0)
    edge = jnp.zeros((GUARD, CH), F32)
    for ref in (norm, block, grows, gcols):
        ref[0:GUARD, :] = edge
        ref[GUARD + FLAT : FLAT + 2 * GUARD, :] = edge
    acc_r[...] = jnp.zeros_like(acc_r)
    acc_x[...] = jnp.zeros_like(acc_x)
    acc_s[...] = jnp.zeros_like(acc_s)
    sums[...] = jnp.zeros_like(sums)

    def rows_at(i):
        return pl.ds(pl.multiple_of(i * ROWS, 16), ROWS)

    def guarded(i, extra=0, size=ROWS):
        return pl.ds(pl.multiple_of(i * ROWS + GUARD + extra, 8), size)

    def first_norm(i, carry):
        here = rows_at(i)
        x = canvas[here, :]
        center = x - lane_mean(x)
        scale = lax.rsqrt(lane_mean(center * center) + EPS)
        unit = center * scale
        xhat[here, :] = unit
        rstd[here, :] = jnp.broadcast_to(scale, unit.shape)
        value = jnp.where(valid[here, :] > 0, unit * vec(0) + vec(1), 0.0)
        norm[guarded(i), :] = value.astype(BF16).astype(F32)
        return carry

    lax.fori_loop(0, STEPS, first_norm, 0)

    def near(ref, i):
        wide = ref[guarded(i, -8, ROWS + 16), :]
        back = pltpu.roll(wide, 1, 0)[8 : 8 + ROWS, :]
        ahead = pltpu.roll(wide, ROWS + 15, 0)[8 : 8 + ROWS, :]
        return back, ahead

    def branches(i, total):
        here = rows_at(i)
        plain = norm[guarded(i), :]
        above = norm[guarded(i, -WIDE), :]
        below = norm[guarded(i, WIDE), :]
        left, right = near(norm, i)
        by_row = vec(15)
        by_col = vec(16)
        sr = jnp.where(by_row < 0, above, jnp.where(by_row > 0, below, plain)).astype(BF16)
        sc = jnp.where(by_col < 0, left, jnp.where(by_col > 0, right, plain)).astype(BF16)
        nb = plain.astype(BF16)
        rows_b[here, :] = sr
        cols_b[here, :] = sc
        norm_b[here, :] = nb
        bh = nn(sr, hw[...]) + vec(2)
        bw = nn(sc, ww[...]) + vec(3)
        bc = nn(nb, cw[...])
        branch_h[here, :] = bh
        branch_w[here, :] = bw
        branch_c[here, :] = bc
        return total + col_sum(valid[here, :] * (bh + bw + bc))

    total = lax.fori_loop(0, STEPS, branches, jnp.zeros((1, CH), F32))

    count = jnp.full((1, CH), side * side, jnp.int32).astype(F32)
    means = total / count
    inner_pre = jnp.sum(sqt[...] * means, axis=1, keepdims=True) + sqb[...]
    inner_cdf, inner_density = normal_parts(inner_pre)
    inner = inner_pre * inner_cdf
    inner_slope = inner_cdf + inner_density
    logit = [col_sum(exw[:, j * CH : (j + 1) * CH] * inner) + vec(12 + j) for j in range(3)]
    top = jnp.maximum(jnp.maximum(logit[0], logit[1]), logit[2])
    grown = [jnp.exp(v - top) for v in logit]
    whole = grown[0] + grown[1] + grown[2]
    mix = [v / whole for v in grown]

    def forward(i, carry):
        here = rows_at(i)
        mixed = mix[0] * branch_h[here, :] + mix[1] * branch_w[here, :] + mix[2] * branch_c[here, :]
        mixed = mixed.astype(BF16)
        mixed_b[here, :] = mixed
        resid = canvas[here, :] + nn(mixed, ow[...]) + vec(4)
        center = resid - lane_mean(resid)
        scale = lax.rsqrt(lane_mean(center * center) + EPS)
        unit = center * scale
        xhat2[here, :] = unit
        rstd2[here, :] = jnp.broadcast_to(scale, unit.shape)
        n2 = (unit * vec(5) + vec(6)).astype(BF16)
        norm2_b[here, :] = n2
        total2 = resid + vec(7)
        for j in range(FF // CH):
            lanes = slice(j * CH, (j + 1) * CH)
            pre = nn(n2, xw[:, lanes]) + vec(8 + j)
            cdf, density = normal_parts(pre)
            hid = (pre * cdf).astype(BF16)
            hidden_b[here, lanes] = hid
            slope[here, lanes] = cdf + density
        total2 = total2 + nn(hidden_b[here, :], rw[...])
        value = jnp.where(valid[here, :] > 0, total2, 0.0)
        block[guarded(i), :] = value.astype(BF16).astype(F32)
        return carry

    lax.fori_loop(0, STEPS, forward, 0)

    taps[OPIX:, :] = jnp.zeros((taps.shape[0] - OPIX, taps.shape[1]), F32)
    for a in range(3):
        for b in range(3):
            lanes = slice((3 * a + b) * CH, (3 * a + b + 1) * CH)
            for i in range(HALF):
                at = GUARD + (2 * i + a - 1) * WIDE + b - 1
                taps[i * HALF : (i + 1) * HALF, lanes] = block[pl.ds(at, HALF, stride=2), :]
    tap_b = taps[...].astype(BF16)
    index = lax.broadcasted_iota(jnp.int32, (1, OTILE * LANES), 1)
    out_row = ((index.astype(F32) + 0.5) * (1.0 / HALF)).astype(jnp.int32)
    out_col = index - out_row * HALF
    out_keep = (2 * out_row < side) & (2 * out_col < side)
    cot = jnp.where(out_keep, cf[...], 0.0)
    cot_b = cot[0:OUT, :].astype(BF16)
    cot_t = cot.T.astype(BF16)[:, 0:OUT]
    section = nt(kw[...], tap_b) + kbias[...]
    section_out[...] = jnp.where(out_keep, section, 0.0)
    conv = nn(cot_b, tap_b)
    for t in range(9):
        put(AT_CONV + t * OUT, conv[:, t * CH : (t + 1) * CH])
    kb_rows = jnp.sum(cot, axis=1, keepdims=True)
    spread[...] = nn(cot_t, kw[...])
    row_id = lax.broadcasted_iota(jnp.int32, (OPIX, CH), 0)
    row_of = ((row_id.astype(F32) + 0.5) * (1.0 / HALF)).astype(jnp.int32)
    inside = row_id - row_of * HALF < HALF - 1

    def part(tap, ahead, masked):
        value = spread[ahead : ahead + OPIX, tap * CH : (tap + 1) * CH]
        return jnp.where(inside, value, 0.0) if masked else value

    found = (
        part(4, 0, False),
        part(5, 0, False) + part(3, 1, True),
        part(7, 0, False) + part(1, HALF, False),
        (part(8, 0, False) + part(6, 1, True)) + (part(2, HALF, False) + part(0, HALF + 1, True)),
    )
    for p in range(4):
        planes[p, 0:OPIX, :] = found[p]
        for i in range(HALF):
            at = (2 * i + p // 2) * WIDE + p % 2
            gblock[pl.ds(at, HALF, stride=2), :] = planes[p, i * HALF : (i + 1) * HALF, :]

    def add(row, value):
        sums[row : row + 1, :] += value

    def backward(i, carry):
        here = rows_at(i)
        gb = jnp.where(valid[here, :] > 0, gblock[here, :], 0.0)
        gred = gb.astype(BF16)
        add(7, col_sum(gred.astype(F32)))
        acc_r[...] += tn(gred, hidden_b[here, :])
        n2 = norm2_b[here, :]
        for j in range(FF // CH):
            lanes = slice(j * CH, (j + 1) * CH)
            gpre = (nt(gred, rw[lanes, :]) * slope[here, lanes]).astype(BF16)
            add(8 + j, col_sum(gpre.astype(F32)))
            gpre_b[:, lanes] = gpre
        acc_x[...] += tn(n2, gpre_b[...])
        gn2 = nt(gpre_b[...], xw[...])
        unit = xhat2[here, :]
        add(5, col_sum(gn2 * unit))
        add(6, col_sum(gn2))
        gy = gn2 * vec(5)
        gr = gb + rstd2[here, :] * (gy - lane_mean(gy) - unit * lane_mean(gy * unit))
        gresid[here, :] = gr
        gproj = gr.astype(BF16)
        add(4, col_sum(gproj.astype(F32)))
        acc_s[3] += tn(mixed_b[here, :], gproj)
        gm = nt(gproj, ow[...])
        gmixed[here, :] = gm
        add(20, col_sum(gm * branch_h[here, :]))
        add(21, col_sum(gm * branch_w[here, :]))
        add(22, col_sum(gm * branch_c[here, :]))
        return carry

    lax.fori_loop(0, STEPS, backward, 0)

    gmix = [sums[20 + j : 21 + j, :] for j in range(3)]
    inner_dot = mix[0] * gmix[0] + mix[1] * gmix[1] + mix[2] * gmix[2]
    glogit = [mix[j] * (gmix[j] - inner_dot) for j in range(3)]
    ginner = jnp.zeros((RED, 1), F32)
    for j in range(3):
        ginner += jnp.sum(exw[:, j * CH : (j + 1) * CH] * glogit[j], axis=1, keepdims=True)
        put(AT_EXCITE + RED * j, inner * glogit[j])
        sums[12 + j : 13 + j, :] = glogit[j]
    ginner = ginner * inner_slope
    put(AT_SQUEEZE, ginner * means)
    put(AT_SQ_BIAS, jnp.broadcast_to(ginner, (RED, CH)))
    gmeans = col_sum(sqt[...] * ginner) / count

    def branch_back(i, carry):
        here = rows_at(i)
        gm = gmixed[here, :]
        level = valid[here, :] * gmeans
        gh = (mix[0] * gm + level).astype(BF16)
        gw = (mix[1] * gm + level).astype(BF16)
        gc = (mix[2] * gm + level).astype(BF16)
        add(2, col_sum(gh.astype(F32)))
        add(3, col_sum(gw.astype(F32)))
        acc_s[0] += tn(rows_b[here, :], gh)
        acc_s[1] += tn(cols_b[here, :], gw)
        acc_s[2] += tn(norm_b[here, :], gc)
        grows[guarded(i), :] = nt(gh, hw[...])
        gcols[guarded(i), :] = nt(gw, ww[...])
        gnorm[here, :] = nt(gc, cw[...])
        return carry

    lax.fori_loop(0, STEPS, branch_back, 0)

    def last(i, carry):
        here = rows_at(i)
        by_row = vec(15)
        by_col = vec(16)
        plain = grows[guarded(i), :]
        above = grows[guarded(i, -WIDE), :]
        below = grows[guarded(i, WIDE), :]
        left, right = near(gcols, i)
        level = gcols[guarded(i), :]
        value = (
            gnorm[here, :]
            + jnp.where(by_row < 0, below, jnp.where(by_row > 0, above, plain))
            + jnp.where(by_col < 0, right, jnp.where(by_col > 0, left, level))
        )
        keep = valid[here, :] > 0
        value = jnp.where(keep, value, 0.0)
        unit = xhat[here, :]
        add(0, col_sum(value * unit))
        add(1, col_sum(value))
        gy = value * vec(0)
        back = rstd[here, :] * (gy - lane_mean(gy) - unit * lane_mean(gy * unit))
        grad[here, :] = jnp.where(keep, gresid[here, :] + back, 0.0)
        return carry

    lax.fori_loop(0, STEPS, last, 0)

    for j in range(FF // CH):
        put(AT_REDUCE + j * CH, acc_r[:, j * CH : (j + 1) * CH].T)
        put(AT_EXPAND + j * CH, acc_x[:, j * CH : (j + 1) * CH])
    for j, at in enumerate((AT_HEIGHT, AT_WIDTH, AT_CHANNEL, AT_OUTPUT)):
        put(at, acc_s[j])
    same = lax.broadcasted_iota(jnp.int32, (LANES, LANES), 0) == lax.broadcasted_iota(
        jnp.int32, (LANES, LANES), 1
    )
    for j in range(OTILE):
        add(15 + j, col_sum(jnp.where(same, kb_rows[j * LANES : (j + 1) * LANES, :], 0.0)))
    put(AT_VECTOR, sums[...])
    keep_out[...] = rows_out[0]
    send_out[...] = rows_out[1].astype(BF16)


def send_kernel(info, grad, section, out, tall, turned, stage):
    begin = pl.multiple_of(112 - info[0], 16)
    tall[0:112, :] = jnp.zeros((112, CH), F32)
    tall[112 + PIX :, :] = jnp.zeros((tall.shape[0] - 112 - PIX, CH), F32)
    for r in range(SIDE):
        tall[112 + r * SIDE : 112 + (r + 1) * SIDE, :] = grad[r * WIDE : r * WIDE + SIDE, :]
    for t in range(WIN):
        turned[:, t * LANES : (t + 1) * LANES] = tall[pl.ds(begin + t * LANES, LANES), :].T
    for s in range(out.shape[0]):
        base = s * PIXROWS
        for t in range(WIN):
            stage[base + 4 * t : base + 4 * t + 4, :] = turned[
                4 * s : 4 * s + 4, t * LANES : (t + 1) * LANES
            ]
        for j in range(OTILE):
            stage[base + 44 + 10 * j : base + 54 + 10 * j, :] = section[
                10 * s : 10 * s + 10, j * LANES : (j + 1) * LANES
            ]
        out[s] = stage[base : base + PIXROWS, :].astype(BF16)


def pair_kernel(kept, met, out):
    out[...] = (kept[...] + met[...].astype(F32)).astype(BF16)


def add_kernel(recv, out):
    total = recv[0].astype(F32)
    for s in range(1, recv.shape[0]):
        total += recv[s].astype(F32)
    out[...] = total.astype(BF16)


def copies_kernel(mine, one, two, three, out):
    total = (mine[...].astype(F32) + two[...].astype(F32)) + (
        one[...].astype(F32) + three[...].astype(F32)
    )
    total = total.astype(BF16)
    for s in range(out.shape[0]):
        out[s] = total


def pixel_kernel(info, near, far, feat, section, stage, recv):
    core = info[2]
    for i in range(near.shape[0]):
        recv[2 * i + core] = near[i]
        recv[2 * i + 1 - core] = far[i]
    for k in range(recv.shape[0]):
        piece = recv[k].astype(F32)
        tile = first_tile(k)
        for t in range(WIN):
            lanes = slice((tile + t) * LANES, (tile + t + 1) * LANES)
            value = piece[4 * t : 4 * t + 4, :]
            if t == 0 and k % 8:
                feat[:, lanes] += value
            else:
                feat[:, lanes] = value
        for j in range(OTILE):
            width = min(LANES, OPIX - j * LANES)
            at = k * OPIX + j * LANES
            stage[:, at : at + width] = piece[44 + 10 * j : 54 + 10 * j, 0:width]
    section[...] = stage[...].astype(BF16)


def weight_kernel(info, own, other, *refs):
    outs = refs[:-1]
    both = refs[-1]
    core = info[2]
    for i in range(own.shape[0]):
        both[2 * i + core] = own[i]
        both[2 * i + 1 - core] = other[i]

    def rows(at, count):
        found = []
        done = 0
        while done < count:
            chunk, inner = divmod(at + done, WROWS)
            size = min(count - done, WROWS - inner)
            found.append(both[chunk, inner : inner + size, :])
            done += size
        return jnp.concatenate(found).astype(F32)

    conv, red, exp, height, width, chan, outw, squeeze, excite, sq_bias = outs[:10]
    for t in range(9):
        conv[t] = rows(AT_CONV + t * OUT, OUT)
    red[...] = rows(AT_REDUCE, FF)
    for j in range(FF // CH):
        exp[:, j * CH : (j + 1) * CH] = rows(AT_EXPAND + j * CH, CH)
    for at, ref in (
        (AT_HEIGHT, height),
        (AT_WIDTH, width),
        (AT_CHANNEL, chan),
        (AT_OUTPUT, outw),
    ):
        ref[...] = rows(at, CH)
    squeeze[...] = rows(AT_SQUEEZE, RED)
    for j in range(3):
        excite[:, j * CH : (j + 1) * CH] = rows(AT_EXCITE + j * RED, RED)
    same = lax.broadcasted_iota(jnp.int32, (RED, CH), 0) == lax.broadcasted_iota(
        jnp.int32, (RED, CH), 1
    )
    sq_bias[...] = jnp.sum(jnp.where(same, rows(AT_SQ_BIAS, RED), 0.0), axis=0)[0:RED]
    vectors = rows(AT_VECTOR, RED)
    for ref, row in zip(outs[10:], VECTOR_ROWS):
        size = ref.shape[0]
        for j in range(-(-size // CH)):
            width = min(CH, size - j * CH)
            ref[j * CH : j * CH + width] = vectors[row + j, 0:width]


def body(
    features,
    size_group,
    cycle_offsets,
    norm_gain,
    norm_bias,
    height_weight,
    height_bias,
    width_weight,
    width_bias,
    channel_weight,
    squeeze_weight,
    squeeze_bias,
    excite_weight,
    excite_bias,
    output_weight,
    output_bias,
    second_gain,
    second_bias,
    expand_weight,
    expand_bias,
    reduce_weight,
    reduce_bias,
    stride_weight,
    stride_bias,
    cotangent,
):
    shards = lax.axis_size("ch")
    rank = lax.axis_index("ch")
    side = SIDE - 4 * (2 - lax.dynamic_index_in_dim(size_group, rank, keepdims=False))
    info = jnp.stack([16 * (rank % 8), side, rank % 2]).astype(jnp.int32)
    vecs = jnp.concatenate(
        [
            v.astype(F32)
            for v in (
                norm_gain,
                norm_bias,
                height_bias,
                width_bias,
                output_bias,
                second_gain,
                second_bias,
                reduce_bias,
                expand_bias,
                excite_bias,
                cycle_offsets[0],
                cycle_offsets[1],
            )
        ]
    ).reshape(17, CH)

    whole = pl.BlockSpec(memory_space=pltpu.VMEM)
    chunks = pl.pallas_call(
        pack_kernel,
        cost_estimate=cost(2.5),
        out_shape=jax.ShapeDtypeStruct((shards, PIXROWS, LANES), BF16),
        in_specs=[pl.BlockSpec(memory_space=pltpu.HBM)] * 2,
        out_specs=whole,
        scratch_shapes=[
            pltpu.VMEM((shards * PIXROWS, LANES), F32),
            pltpu.VMEM(cotangent.shape, F32),
            pltpu.VMEM(features.shape, BF16),
            pltpu.VMEM(cotangent.shape, BF16),
            pltpu.SemaphoreType.DMA((2,)),
        ],
        compiler_params=params(56),
    )(features, cotangent)
    arrived = lax.all_to_all(chunks, "ch", split_axis=0, concat_axis=0, tiled=True)

    canvas = pltpu.VMEM((FLAT, CH), F32)
    guarded = pltpu.VMEM((FLAT + 2 * GUARD, CH), F32)
    narrow = pltpu.VMEM((FLAT, CH), BF16)
    kept, sent, grad, section_part = pl.pallas_call(
        main_kernel,
        cost_estimate=cost(22),
        out_shape=(
            jax.ShapeDtypeStruct((shards // 2, WROWS, LANES), F32),
            jax.ShapeDtypeStruct((shards // 2, WROWS, LANES), BF16),
            jax.ShapeDtypeStruct((FLAT, CH), F32),
            jax.ShapeDtypeStruct((OUT, OTILE * LANES), F32),
        ),
        in_specs=[pl.BlockSpec(memory_space=pltpu.SMEM)] + [whole] * 13,
        out_specs=(whole,) * 4,
        scratch_shapes=[
            pltpu.VMEM((CH, WIN * LANES), F32),
            pltpu.VMEM((3 * LANES, OTILE * LANES), F32),
            pltpu.VMEM((112 + WIN * LANES, CH), F32),
            canvas,
            canvas,
            canvas,
            canvas,
            guarded,
            narrow,
            narrow,
            narrow,
            canvas,
            canvas,
            canvas,
            narrow,
            canvas,
            canvas,
            narrow,
            pltpu.VMEM((FLAT, FF), BF16),
            pltpu.VMEM((FLAT, FF), F32),
            guarded,
            pltpu.VMEM((OTILE * LANES, 9 * CH), F32),
            pltpu.VMEM((OTILE * LANES, 9 * CH), F32),
            pltpu.VMEM((4, 328, CH), F32),
            canvas,
            canvas,
            canvas,
            guarded,
            guarded,
            canvas,
            pltpu.VMEM((CH, FF), F32),
            pltpu.VMEM((CH, FF), F32),
            pltpu.VMEM((4, CH, CH), F32),
            pltpu.VMEM((RED, CH), F32),
            pltpu.VMEM((ROWS, FF), BF16),
            pltpu.VMEM((2, shards // 2, WROWS, LANES), F32),
        ],
        compiler_params=params(42),
    )(
        info,
        arrived,
        vecs,
        squeeze_weight.astype(F32).T,
        squeeze_bias.astype(F32)[:, None],
        excite_weight.astype(F32),
        stride_bias.astype(F32)[:, None],
        height_weight,
        width_weight,
        channel_weight,
        output_weight,
        expand_weight,
        reduce_weight,
        stride_weight.reshape(OUT, 9 * CH),
    )
    other_core = [(i, i ^ 1) for i in range(shards)]
    same_core = [[2 * i + c for i in range(shards // 2)] for c in range(2)]
    met = lax.ppermute(sent, "ch", other_core)
    pixels = pl.pallas_call(
        send_kernel,
        cost_estimate=cost(2.5),
        out_shape=jax.ShapeDtypeStruct((shards, PIXROWS, LANES), BF16),
        in_specs=[pl.BlockSpec(memory_space=pltpu.SMEM)] + [whole] * 2,
        out_specs=whole,
        scratch_shapes=[
            pltpu.VMEM((112 + WIN * LANES, CH), F32),
            pltpu.VMEM((CH, WIN * LANES), F32),
            pltpu.VMEM((shards * PIXROWS, LANES), F32),
        ],
        compiler_params=params(8),
    )(info, grad, section_part)
    kept, pixels = lax.optimization_barrier((kept, pixels))
    partial = pl.pallas_call(
        pair_kernel,
        cost_estimate=cost(2.3),
        out_shape=jax.ShapeDtypeStruct(kept.shape, BF16),
        compiler_params=params(3),
    )(kept, met)

    def exchange(v):
        return lax.all_to_all(
            v, "ch", split_axis=0, concat_axis=0, tiled=True, axis_index_groups=same_core
        )

    parts = exchange(partial)
    parts, pixels = lax.optimization_barrier((parts, pixels))
    back = exchange(pixels.reshape(shards // 2, 2, PIXROWS, LANES))

    mine = pl.pallas_call(
        add_kernel,
        cost_estimate=cost(1.7),
        out_shape=jax.ShapeDtypeStruct((WROWS, LANES), BF16),
        compiler_params=params(2),
    )(parts)
    groups = lax.axis_size("img")
    other = [
        lax.ppermute(mine, "img", [(i, (i + d) % groups) for i in range(groups)])
        for d in (1, 2, 3)
    ]
    copies = pl.pallas_call(
        copies_kernel,
        cost_estimate=cost(1.7),
        out_shape=jax.ShapeDtypeStruct((shards // 2, WROWS, LANES), BF16),
        compiler_params=params(2),
    )(mine, *other)
    copies, back = lax.optimization_barrier((copies, back))
    own_half = exchange(copies)
    core = rank % 2
    near = lax.dynamic_index_in_dim(back, core, axis=1, keepdims=False)
    far = lax.dynamic_index_in_dim(back, 1 - core, axis=1, keepdims=False)
    far = lax.ppermute(far, "ch", other_core)

    features_grad, section = pl.pallas_call(
        pixel_kernel,
        cost_estimate=cost(2.5),
        out_shape=(
            jax.ShapeDtypeStruct(features.shape, F32),
            jax.ShapeDtypeStruct(cotangent.shape, BF16),
        ),
        in_specs=[pl.BlockSpec(memory_space=pltpu.SMEM)] + [whole] * 2,
        out_specs=(whole,) * 2,
        scratch_shapes=[
            pltpu.VMEM(cotangent.shape, F32),
            pltpu.VMEM((shards, PIXROWS, LANES), BF16),
        ],
        compiler_params=params(5),
    )(info, near, far)

    own_half, features_grad, section = lax.optimization_barrier((own_half, features_grad, section))
    other_half = lax.ppermute(own_half, "ch", other_core)

    def like(*shape):
        return jax.ShapeDtypeStruct(shape, F32)

    (
        conv_grad,
        reduce_grad,
        expand_grad,
        height_grad,
        width_grad,
        channel_grad,
        output_grad,
        squeeze_grad,
        excite_grad,
        squeeze_bias_grad,
        norm_gain_grad,
        norm_bias_grad,
        height_bias_grad,
        width_bias_grad,
        output_bias_grad,
        second_gain_grad,
        second_bias_grad,
        reduce_bias_grad,
        expand_bias_grad,
        excite_bias_grad,
        conv_bias_grad,
    ) = pl.pallas_call(
        weight_kernel,
        cost_estimate=cost(2.8),
        out_shape=(
            like(9, OUT, CH),
            like(FF, CH),
            like(CH, FF),
            like(CH, CH),
            like(CH, CH),
            like(CH, CH),
            like(CH, CH),
            like(RED, CH),
            like(RED, 3 * CH),
            like(RED),
        )
        + tuple(like(size) for size in VECTOR_SIZES),
        in_specs=[pl.BlockSpec(memory_space=pltpu.SMEM)] + [whole] * 2,
        out_specs=(whole,) * 21,
        scratch_shapes=[pltpu.VMEM((shards, WROWS, LANES), BF16)],
        compiler_params=params(6),
    )(info, own_half, other_half)
    return (
        section,
        features_grad,
        norm_gain_grad,
        norm_bias_grad,
        height_grad,
        height_bias_grad,
        width_grad,
        width_bias_grad,
        channel_grad,
        squeeze_grad.T,
        squeeze_bias_grad,
        excite_grad,
        excite_bias_grad,
        output_grad,
        output_bias_grad,
        second_gain_grad,
        second_bias_grad,
        expand_grad,
        expand_bias_grad,
        reduce_grad,
        reduce_bias_grad,
        jnp.transpose(conv_grad, (1, 0, 2)),
        conv_bias_grad,
    )


def solution(mesh):
    split = P("ch", "img")
    return jax.shard_map(
        body,
        mesh=mesh,
        in_specs=(split, P("img")) + (P(),) * 22 + (split,),
        out_specs=(split, split) + (P(),) * 21,
        check_vma=False,
    )
```

```python
import jax
import jax.numpy as jnp
from jax import lax
from jax.experimental import pallas as pl
from jax.experimental.pallas import tpu as pltpu
from jax.sharding import PartitionSpec as P

CH = 128
FF = 512
RED = 32
OUT = 320
SIDE = 36
PIX = SIDE * SIDE
HALF = SIDE // 2
OPIX = HALF * HALF
WIDE = 40
FLAT = SIDE * WIDE
GUARD = 48
EPS = 1e-05
LANES = 128
WIN = 11
OTILE = 3
PIXROWS = 80
WROWS = 144

F32 = jnp.float32
BF16 = jnp.bfloat16

AT_CONV = 0
AT_REDUCE = 2880
AT_EXPAND = 3392
AT_HEIGHT = 3904
AT_WIDTH = 4032
AT_CHANNEL = 4160
AT_OUTPUT = 4288
AT_SQUEEZE = 4416
AT_EXCITE = 4448
AT_SQ_BIAS = 4544
AT_VECTOR = 4576
VECTOR_ROWS = (0, 1, 2, 3, 4, 5, 6, 7, 8, 12, 15)
VECTOR_SIZES = (CH,) * 8 + (FF, 3 * CH, OUT)


def params(mebibytes):
    return pltpu.CompilerParams(vmem_limit_bytes=mebibytes * 1024 * 1024)


def cost(micros):
    return pl.CostEstimate(flops=0, bytes_accessed=int(micros * 3.69e6), transcendentals=0)


def first_tile(k):
    return 10 * k + k // 8


def nn(a, b):
    return lax.dot_general(a, b, (((1,), (0,)), ((), ())), preferred_element_type=F32)


def nt(a, b):
    return lax.dot_general(a, b, (((1,), (1,)), ((), ())), preferred_element_type=F32)


def tn(a, b):
    return lax.dot_general(a, b, (((0,), (0,)), ((), ())), preferred_element_type=F32)


def lane_mean(v):
    return jnp.sum(v, axis=1, keepdims=True) * (1.0 / CH)


def col_sum(v):
    return jnp.sum(v, axis=0, keepdims=True)


def normal_parts(x):
    cdf = 0.5 + 0.5 * lax.erf(x * 0.7071067811865476)
    return cdf, (x * 0.3989422804014327) * jnp.exp(x * (x * -0.5))


def pack_kernel(feat_hbm, cot_hbm, out, stage, cots, feat, cot, ready):
    images = out.shape[0]
    first = pltpu.make_async_copy(feat_hbm, feat, ready.at[0])
    second = pltpu.make_async_copy(cot_hbm, cot, ready.at[1])
    first.start()
    second.start()
    first.wait()
    for k in range(images):
        base = k * PIXROWS
        begin = first_tile(k) * LANES
        for t in range(WIN):
            stage[base + 4 * t : base + 4 * t + 4, :] = feat[
                :, begin + t * LANES : begin + (t + 1) * LANES
            ].astype(F32)
    second.wait()
    cots[...] = cot[...].astype(F32)
    for k in range(images):
        base = k * PIXROWS
        for j in range(OTILE):
            width = min(LANES, OPIX - j * LANES)
            at = k * OPIX + j * LANES
            row = base + 44 + 10 * j
            stage[row : row + 10, 0:width] = cots[:, at : at + width]
        out[k] = stage[base : base + PIXROWS, :].astype(BF16)


def main_kernel(
    info,
    recv,
    vecs,
    sqt,
    sqb,
    exw,
    kbias,
    hw,
    ww,
    cw,
    ow,
    xw,
    rw,
    kw,
    keep_out,
    send_out,
    grad,
    section_out,
    xf,
    cf,
    tall,
    canvas,
    valid,
    xhat,
    rstd,
    norm,
    rows_b,
    cols_b,
    norm_b,
    branch_h,
    branch_w,
    branch_c,
    mixed_b,
    xhat2,
    rstd2,
    norm2_b,
    hidden_b,
    slope,
    block,
    planes,
    taps,
    spread,
    gblock,
    gresid,
    gmixed,
    grows,
    gcols,
    gpre_b,
    sums,
    rows_out,
):
    shift = info[0]
    side = info[1]
    core = info[2]

    def vec(i):
        return vecs[i : i + 1, :]

    def put(row, value):
        count = value.shape[0]
        done = 0
        while done < count:
            chunk, inner = divmod(row + done, WROWS)
            size = min(count - done, WROWS - inner)
            slot = core if chunk % 2 == 0 else 1 - core
            rows_out[slot, chunk // 2, inner : inner + size, :] = value[done : done + size, :]
            done += size

    def total_of(row, value):
        sums[row : row + 1, :] = col_sum(value)

    cf[OUT:, :] = jnp.zeros((cf.shape[0] - OUT, cf.shape[1]), F32)
    for s in range(recv.shape[0]):
        piece = recv[s].astype(F32)
        for t in range(WIN):
            xf[4 * s : 4 * s + 4, t * LANES : (t + 1) * LANES] = piece[4 * t : 4 * t + 4, :]
        for j in range(OTILE):
            cf[10 * s : 10 * s + 10, j * LANES : (j + 1) * LANES] = piece[
                44 + 10 * j : 54 + 10 * j, :
            ]
    begin = pl.multiple_of(112 - shift, 16)
    for t in range(WIN):
        tall[pl.ds(begin + t * LANES, LANES), :] = xf[:, t * LANES : (t + 1) * LANES].T

    column = lax.broadcasted_iota(jnp.int32, (WIDE, CH), 0)
    for r in range(SIDE):
        keep = (column < side) & (r < side)
        canvas[r * WIDE : (r + 1) * WIDE, :] = jnp.where(
            keep, tall[112 + r * SIDE : 112 + r * SIDE + WIDE, :], 0.0
        )
        valid[r * WIDE : (r + 1) * WIDE, :] = jnp.where(keep, 1.0, 0.0)
    edge = jnp.zeros((GUARD, CH), F32)
    for ref in (norm, block, grows, gcols):
        ref[0:GUARD, :] = edge
        ref[GUARD + FLAT : FLAT + 2 * GUARD, :] = edge
    sums[...] = jnp.zeros_like(sums)

    def moved(ref, by):
        return ref[GUARD + by : GUARD + by + FLAT, :]

    x = canvas[...]
    center = x - lane_mean(x)
    scale = lax.rsqrt(lane_mean(center * center) + EPS)
    unit = center * scale
    xhat[...] = unit
    rstd[...] = jnp.broadcast_to(scale, unit.shape)
    value = jnp.where(valid[...] > 0, unit * vec(0) + vec(1), 0.0)
    norm[GUARD : GUARD + FLAT, :] = value.astype(BF16).astype(F32)

    by_row = vec(15)
    by_col = vec(16)
    plain = moved(norm, 0)
    rows_b[...] = jnp.where(
        by_row < 0, moved(norm, -WIDE), jnp.where(by_row > 0, moved(norm, WIDE), plain)
    ).astype(BF16)
    cols_b[...] = jnp.where(
        by_col < 0, moved(norm, -1), jnp.where(by_col > 0, moved(norm, 1), plain)
    ).astype(BF16)
    norm_b[...] = plain.astype(BF16)
    bh = nn(rows_b[...], hw[...]) + vec(2)
    bw = nn(cols_b[...], ww[...]) + vec(3)
    bc = nn(norm_b[...], cw[...])
    branch_h[...] = bh
    branch_w[...] = bw
    branch_c[...] = bc
    total = col_sum(valid[...] * (bh + bw + bc))

    count = jnp.full((1, CH), side * side, jnp.int32).astype(F32)
    means = total / count
    inner_pre = jnp.sum(sqt[...] * means, axis=1, keepdims=True) + sqb[...]
    inner_cdf, inner_density = normal_parts(inner_pre)
    inner = inner_pre * inner_cdf
    inner_slope = inner_cdf + inner_density
    logit = [col_sum(exw[:, j * CH : (j + 1) * CH] * inner) + vec(12 + j) for j in range(3)]
    top = jnp.maximum(jnp.maximum(logit[0], logit[1]), logit[2])
    grown = [jnp.exp(v - top) for v in logit]
    whole = grown[0] + grown[1] + grown[2]
    mix = [v / whole for v in grown]

    mixed = mix[0] * branch_h[...] + mix[1] * branch_w[...] + mix[2] * branch_c[...]
    mixed_b[...] = mixed.astype(BF16)
    resid = canvas[...] + nn(mixed_b[...], ow[...]) + vec(4)
    center = resid - lane_mean(resid)
    scale = lax.rsqrt(lane_mean(center * center) + EPS)
    unit = center * scale
    xhat2[...] = unit
    rstd2[...] = jnp.broadcast_to(scale, unit.shape)
    norm2_b[...] = (unit * vec(5) + vec(6)).astype(BF16)
    through = resid + vec(7)
    for j in range(FF // CH):
        lanes = slice(j * CH, (j + 1) * CH)
        pre = nn(norm2_b[...], xw[:, lanes]) + vec(8 + j)
        cdf, density = normal_parts(pre)
        hidden_b[:, lanes] = (pre * cdf).astype(BF16)
        slope[:, lanes] = cdf + density
    through = through + nn(hidden_b[...], rw[...])
    value = jnp.where(valid[...] > 0, through, 0.0)
    block[GUARD : GUARD + FLAT, :] = value.astype(BF16).astype(F32)

    top_rows = 24
    for p in range(4):
        planes[p, 0:top_rows, :] = jnp.zeros((top_rows, CH), F32)
        planes[p, top_rows + OPIX :, :] = jnp.zeros((planes.shape[1] - top_rows - OPIX, CH), F32)
        for i in range(HALF):
            at = GUARD + (2 * i + p // 2) * WIDE + p % 2
            row = top_rows + i * HALF
            planes[p, row : row + HALF, :] = block[pl.ds(at, HALF, stride=2), :]
    used = 336
    row_id = lax.broadcasted_iota(jnp.int32, (used, CH), 0)
    row_of = ((row_id.astype(F32) + 0.5) * (1.0 / HALF)).astype(jnp.int32)
    out_column = row_id - row_of * HALF
    for a in range(3):
        for b in range(3):
            plane = 2 * ((a + 1) % 2) + (b + 1) % 2
            row = top_rows - HALF * (a == 0) - (b == 0)
            value = planes[plane, row : row + used, :]
            if b == 0:
                value = jnp.where(out_column > 0, value, 0.0)
            taps[0:used, (3 * a + b) * CH : (3 * a + b + 1) * CH] = value.astype(BF16)
    taps[used:, :] = jnp.zeros((taps.shape[0] - used, taps.shape[1]), BF16)
    index = lax.broadcasted_iota(jnp.int32, (1, OTILE * LANES), 1)
    lane_row = ((index.astype(F32) + 0.5) * (1.0 / HALF)).astype(jnp.int32)
    lane_col = index - lane_row * HALF
    out_keep = (2 * lane_row < side) & (2 * lane_col < side)
    cot = jnp.where(out_keep, cf[...], 0.0)
    cot_b = cot[0:OUT, :].astype(BF16)
    cot_t = cot.T.astype(BF16)[:, 0:OUT]
    kb_rows = jnp.sum(cot, axis=1, keepdims=True)
    spread[...] = nn(cot_t, kw[...])
    inside = out_column[0:OPIX, :] < HALF - 1

    def part(tap, ahead, masked):
        value = spread[ahead : ahead + OPIX, tap * CH : (tap + 1) * CH]
        return jnp.where(inside, value, 0.0) if masked else value

    found = (
        part(4, 0, False),
        part(5, 0, False) + part(3, 1, True),
        part(7, 0, False) + part(1, HALF, False),
        (part(8, 0, False) + part(6, 1, True)) + (part(2, HALF, False) + part(0, HALF + 1, True)),
    )
    for p in range(4):
        planes[p, 0:OPIX, :] = found[p]
        for i in range(HALF):
            at = (2 * i + p // 2) * WIDE + p % 2
            gblock[pl.ds(at, HALF, stride=2), :] = planes[p, i * HALF : (i + 1) * HALF, :]

    gb = jnp.where(valid[...] > 0, gblock[...], 0.0)
    gred = gb.astype(BF16)
    total_of(7, gred.astype(F32))
    for j in range(FF // (2 * CH)):
        lanes = slice(2 * j * CH, 2 * (j + 1) * CH)
        gpre = (nt(gred, rw[lanes, :]) * slope[:, lanes]).astype(BF16)
        total_of(8 + 2 * j, gpre[:, 0:CH].astype(F32))
        total_of(9 + 2 * j, gpre[:, CH:].astype(F32))
        gpre_b[:, lanes] = gpre
    gn2 = nt(gpre_b[...], xw[...])
    conv = nn(cot_b, taps[...])
    for t in range(9):
        put(AT_CONV + t * OUT, conv[:, t * CH : (t + 1) * CH])
    unit = xhat2[...]
    total_of(5, gn2 * unit)
    total_of(6, gn2)
    gy = gn2 * vec(5)
    gr = gb + rstd2[...] * (gy - lane_mean(gy) - unit * lane_mean(gy * unit))
    gresid[...] = gr
    gproj = gr.astype(BF16)
    total_of(4, gproj.astype(F32))
    grown = tn(gred, hidden_b[...])
    for j in range(FF // CH):
        put(AT_REDUCE + j * CH, grown[:, j * CH : (j + 1) * CH].T)
    gm = nt(gproj, ow[...])
    gmixed[...] = gm
    section = nt(kw[...], taps[...]) + kbias[...]
    section_out[...] = jnp.where(out_keep, section, 0.0)
    gmix = [col_sum(gm * branch[...]) for branch in (branch_h, branch_w, branch_c)]
    put(AT_OUTPUT, tn(mixed_b[...], gproj))
    inner_dot = mix[0] * gmix[0] + mix[1] * gmix[1] + mix[2] * gmix[2]
    glogit = [mix[j] * (gmix[j] - inner_dot) for j in range(3)]
    ginner = jnp.zeros((RED, 1), F32)
    for j in range(3):
        ginner += jnp.sum(exw[:, j * CH : (j + 1) * CH] * glogit[j], axis=1, keepdims=True)
        put(AT_EXCITE + RED * j, inner * glogit[j])
        sums[12 + j : 13 + j, :] = glogit[j]
    ginner = ginner * inner_slope
    put(AT_SQUEEZE, ginner * means)
    put(AT_SQ_BIAS, jnp.broadcast_to(ginner, (RED, CH)))
    gmeans = col_sum(sqt[...] * ginner) / count

    gm = gmixed[...]
    level = valid[...] * gmeans
    gh = (mix[0] * gm + level).astype(BF16)
    gw = (mix[1] * gm + level).astype(BF16)
    gc = (mix[2] * gm + level).astype(BF16)
    total_of(2, gh.astype(F32))
    total_of(3, gw.astype(F32))
    grown = tn(norm2_b[...], gpre_b[...])
    for j in range(FF // CH):
        put(AT_EXPAND + j * CH, grown[:, j * CH : (j + 1) * CH])
    grows[GUARD : GUARD + FLAT, :] = nt(gh, hw[...])
    gcols[GUARD : GUARD + FLAT, :] = nt(gw, ww[...])
    value = nt(gc, cw[...])
    put(AT_HEIGHT, tn(rows_b[...], gh))
    put(AT_WIDTH, tn(cols_b[...], gw))
    put(AT_CHANNEL, tn(norm_b[...], gc))
    value = value + jnp.where(
        by_row < 0,
        moved(grows, WIDE),
        jnp.where(by_row > 0, moved(grows, -WIDE), moved(grows, 0)),
    )
    value = value + jnp.where(
        by_col < 0, moved(gcols, 1), jnp.where(by_col > 0, moved(gcols, -1), moved(gcols, 0))
    )
    keep = valid[...] > 0
    value = jnp.where(keep, value, 0.0)
    unit = xhat[...]
    total_of(0, value * unit)
    total_of(1, value)
    gy = value * vec(0)
    back = rstd[...] * (gy - lane_mean(gy) - unit * lane_mean(gy * unit))
    grad[...] = jnp.where(keep, gresid[...] + back, 0.0)

    same = lax.broadcasted_iota(jnp.int32, (LANES, LANES), 0) == lax.broadcasted_iota(
        jnp.int32, (LANES, LANES), 1
    )
    for j in range(OTILE):
        total_of(15 + j, jnp.where(same, kb_rows[j * LANES : (j + 1) * LANES, :], 0.0))
    put(AT_VECTOR, sums[...])
    keep_out[...] = rows_out[0]
    send_out[...] = rows_out[1].astype(BF16)


def send_kernel(info, grad, section, out, tall, turned, stage):
    begin = pl.multiple_of(112 - info[0], 16)
    tall[0:112, :] = jnp.zeros((112, CH), F32)
    tall[112 + PIX :, :] = jnp.zeros((tall.shape[0] - 112 - PIX, CH), F32)
    for r in range(SIDE):
        tall[112 + r * SIDE : 112 + (r + 1) * SIDE, :] = grad[r * WIDE : r * WIDE + SIDE, :]
    for t in range(WIN):
        turned[:, t * LANES : (t + 1) * LANES] = tall[pl.ds(begin + t * LANES, LANES), :].T
    for s in range(out.shape[0]):
        base = s * PIXROWS
        for t in range(WIN):
            stage[base + 4 * t : base + 4 * t + 4, :] = turned[
                4 * s : 4 * s + 4, t * LANES : (t + 1) * LANES
            ]
        for j in range(OTILE):
            stage[base + 44 + 10 * j : base + 54 + 10 * j, :] = section[
                10 * s : 10 * s + 10, j * LANES : (j + 1) * LANES
            ]
        out[s] = stage[base : base + PIXROWS, :].astype(BF16)


def pair_kernel(kept, met, out):
    out[...] = (kept[...] + met[...].astype(F32)).astype(BF16)


def add_kernel(recv, out):
    total = recv[0].astype(F32)
    for s in range(1, recv.shape[0]):
        total += recv[s].astype(F32)
    out[...] = total.astype(BF16)


def copies_kernel(mine, one, two, three, out):
    total = (mine[...].astype(F32) + two[...].astype(F32)) + (
        one[...].astype(F32) + three[...].astype(F32)
    )
    total = total.astype(BF16)
    for s in range(out.shape[0]):
        out[s] = total


def pixel_kernel(info, near, far, feat, section, stage, recv):
    core = info[2]
    for i in range(near.shape[0]):
        recv[2 * i + core] = near[i]
        recv[2 * i + 1 - core] = far[i]
    for k in range(recv.shape[0]):
        piece = recv[k].astype(F32)
        tile = first_tile(k)
        for t in range(WIN):
            lanes = slice((tile + t) * LANES, (tile + t + 1) * LANES)
            value = piece[4 * t : 4 * t + 4, :]
            if t == 0 and k % 8:
                feat[:, lanes] += value
            else:
                feat[:, lanes] = value
        for j in range(OTILE):
            width = min(LANES, OPIX - j * LANES)
            at = k * OPIX + j * LANES
            stage[:, at : at + width] = piece[44 + 10 * j : 54 + 10 * j, 0:width]
    section[...] = stage[...].astype(BF16)


def weight_kernel(info, own, other, *refs):
    outs = refs[:-1]
    both = refs[-1]
    core = info[2]
    for i in range(own.shape[0]):
        both[2 * i + core] = own[i]
        both[2 * i + 1 - core] = other[i]

    def rows(at, count):
        found = []
        done = 0
        while done < count:
            chunk, inner = divmod(at + done, WROWS)
            size = min(count - done, WROWS - inner)
            found.append(both[chunk, inner : inner + size, :])
            done += size
        return jnp.concatenate(found).astype(F32)

    conv, red, exp, height, width, chan, outw, squeeze, excite, sq_bias = outs[:10]
    for t in range(9):
        conv[t] = rows(AT_CONV + t * OUT, OUT)
    red[...] = rows(AT_REDUCE, FF)
    for j in range(FF // CH):
        exp[:, j * CH : (j + 1) * CH] = rows(AT_EXPAND + j * CH, CH)
    for at, ref in (
        (AT_HEIGHT, height),
        (AT_WIDTH, width),
        (AT_CHANNEL, chan),
        (AT_OUTPUT, outw),
    ):
        ref[...] = rows(at, CH)
    squeeze[...] = rows(AT_SQUEEZE, RED)
    for j in range(3):
        excite[:, j * CH : (j + 1) * CH] = rows(AT_EXCITE + j * RED, RED)
    same = lax.broadcasted_iota(jnp.int32, (RED, CH), 0) == lax.broadcasted_iota(
        jnp.int32, (RED, CH), 1
    )
    sq_bias[...] = jnp.sum(jnp.where(same, rows(AT_SQ_BIAS, RED), 0.0), axis=0)[0:RED]
    vectors = rows(AT_VECTOR, RED)
    for ref, row in zip(outs[10:], VECTOR_ROWS):
        size = ref.shape[0]
        for j in range(-(-size // CH)):
            width = min(CH, size - j * CH)
            ref[j * CH : j * CH + width] = vectors[row + j, 0:width]


def body(
    features,
    size_group,
    cycle_offsets,
    norm_gain,
    norm_bias,
    height_weight,
    height_bias,
    width_weight,
    width_bias,
    channel_weight,
    squeeze_weight,
    squeeze_bias,
    excite_weight,
    excite_bias,
    output_weight,
    output_bias,
    second_gain,
    second_bias,
    expand_weight,
    expand_bias,
    reduce_weight,
    reduce_bias,
    stride_weight,
    stride_bias,
    cotangent,
):
    shards = lax.axis_size("ch")
    rank = lax.axis_index("ch")
    side = SIDE - 4 * (2 - lax.dynamic_index_in_dim(size_group, rank, keepdims=False))
    info = jnp.stack([16 * (rank % 8), side, rank % 2]).astype(jnp.int32)
    vecs = jnp.concatenate(
        [
            v.astype(F32)
            for v in (
                norm_gain,
                norm_bias,
                height_bias,
                width_bias,
                output_bias,
                second_gain,
                second_bias,
                reduce_bias,
                expand_bias,
                excite_bias,
                cycle_offsets[0],
                cycle_offsets[1],
            )
        ]
    ).reshape(17, CH)

    whole = pl.BlockSpec(memory_space=pltpu.VMEM)
    chunks = pl.pallas_call(
        pack_kernel,
        cost_estimate=cost(2.5),
        out_shape=jax.ShapeDtypeStruct((shards, PIXROWS, LANES), BF16),
        in_specs=[pl.BlockSpec(memory_space=pltpu.HBM)] * 2,
        out_specs=whole,
        scratch_shapes=[
            pltpu.VMEM((shards * PIXROWS, LANES), F32),
            pltpu.VMEM(cotangent.shape, F32),
            pltpu.VMEM(features.shape, BF16),
            pltpu.VMEM(cotangent.shape, BF16),
            pltpu.SemaphoreType.DMA((2,)),
        ],
        compiler_params=params(56),
    )(features, cotangent)
    arrived = lax.all_to_all(chunks, "ch", split_axis=0, concat_axis=0, tiled=True)

    canvas = pltpu.VMEM((FLAT, CH), F32)
    guarded = pltpu.VMEM((FLAT + 2 * GUARD, CH), F32)
    narrow = pltpu.VMEM((FLAT, CH), BF16)
    kept, sent, grad, section_part = pl.pallas_call(
        main_kernel,
        cost_estimate=cost(22),
        out_shape=(
            jax.ShapeDtypeStruct((shards // 2, WROWS, LANES), F32),
            jax.ShapeDtypeStruct((shards // 2, WROWS, LANES), BF16),
            jax.ShapeDtypeStruct((FLAT, CH), F32),
            jax.ShapeDtypeStruct((OUT, OTILE * LANES), F32),
        ),
        in_specs=[pl.BlockSpec(memory_space=pltpu.SMEM)] + [whole] * 13,
        out_specs=(whole,) * 4,
        scratch_shapes=[
            pltpu.VMEM((CH, WIN * LANES), F32),
            pltpu.VMEM((3 * LANES, OTILE * LANES), F32),
            pltpu.VMEM((112 + WIN * LANES, CH), F32),
            canvas,
            canvas,
            canvas,
            canvas,
            guarded,
            narrow,
            narrow,
            narrow,
            canvas,
            canvas,
            canvas,
            narrow,
            canvas,
            canvas,
            narrow,
            pltpu.VMEM((FLAT, FF), BF16),
            pltpu.VMEM((FLAT, FF), F32),
            guarded,
            pltpu.VMEM((4, 360, CH), F32),
            pltpu.VMEM((OTILE * LANES, 9 * CH), BF16),
            pltpu.VMEM((OTILE * LANES, 9 * CH), F32),
            canvas,
            canvas,
            canvas,
            guarded,
            guarded,
            pltpu.VMEM((FLAT, FF), BF16),
            pltpu.VMEM((RED, CH), F32),
            pltpu.VMEM((2, shards // 2, WROWS, LANES), F32),
        ],
        compiler_params=params(42),
    )(
        info,
        arrived,
        vecs,
        squeeze_weight.astype(F32).T,
        squeeze_bias.astype(F32)[:, None],
        excite_weight.astype(F32),
        stride_bias.astype(F32)[:, None],
        height_weight,
        width_weight,
        channel_weight,
        output_weight,
        expand_weight,
        reduce_weight,
        stride_weight.reshape(OUT, 9 * CH),
    )
    other_core = [(i, i ^ 1) for i in range(shards)]
    same_core = [[2 * i + c for i in range(shards // 2)] for c in range(2)]
    met = lax.ppermute(sent, "ch", other_core)
    pixels = pl.pallas_call(
        send_kernel,
        cost_estimate=cost(2.5),
        out_shape=jax.ShapeDtypeStruct((shards, PIXROWS, LANES), BF16),
        in_specs=[pl.BlockSpec(memory_space=pltpu.SMEM)] + [whole] * 2,
        out_specs=whole,
        scratch_shapes=[
            pltpu.VMEM((112 + WIN * LANES, CH), F32),
            pltpu.VMEM((CH, WIN * LANES), F32),
            pltpu.VMEM((shards * PIXROWS, LANES), F32),
        ],
        compiler_params=params(8),
    )(info, grad, section_part)
    kept, pixels = lax.optimization_barrier((kept, pixels))
    partial = pl.pallas_call(
        pair_kernel,
        cost_estimate=cost(2.3),
        out_shape=jax.ShapeDtypeStruct(kept.shape, BF16),
        in_specs=[whole] * 2,
        out_specs=whole,
        compiler_params=params(3),
    )(kept, met)

    def exchange(v):
        return lax.all_to_all(
            v, "ch", split_axis=0, concat_axis=0, tiled=True, axis_index_groups=same_core
        )

    parts = exchange(partial)
    parts, pixels = lax.optimization_barrier((parts, pixels))
    back = exchange(pixels.reshape(shards // 2, 2, PIXROWS, LANES))

    mine = pl.pallas_call(
        add_kernel,
        cost_estimate=cost(1.7),
        out_shape=jax.ShapeDtypeStruct((WROWS, LANES), BF16),
        compiler_params=params(2),
    )(parts)
    groups = lax.axis_size("img")
    other = [
        lax.ppermute(mine, "img", [(i, (i + d) % groups) for i in range(groups)])
        for d in (1, 2, 3)
    ]
    copies = pl.pallas_call(
        copies_kernel,
        cost_estimate=cost(1.7),
        in_specs=[whole] * 4,
        out_specs=whole,
        out_shape=jax.ShapeDtypeStruct((shards // 2, WROWS, LANES), BF16),
        compiler_params=params(2),
    )(mine, *other)
    copies, back = lax.optimization_barrier((copies, back))
    own_half = exchange(copies)
    core = rank % 2
    near = lax.dynamic_index_in_dim(back, core, axis=1, keepdims=False)
    far = lax.dynamic_index_in_dim(back, 1 - core, axis=1, keepdims=False)
    far = lax.ppermute(far, "ch", other_core)

    features_grad, section = pl.pallas_call(
        pixel_kernel,
        cost_estimate=cost(2.5),
        out_shape=(
            jax.ShapeDtypeStruct(features.shape, F32),
            jax.ShapeDtypeStruct(cotangent.shape, BF16),
        ),
        in_specs=[pl.BlockSpec(memory_space=pltpu.SMEM)] + [whole] * 2,
        out_specs=(whole,) * 2,
        scratch_shapes=[
            pltpu.VMEM(cotangent.shape, F32),
            pltpu.VMEM((shards, PIXROWS, LANES), BF16),
        ],
        compiler_params=params(5),
    )(info, near, far)

    own_half, features_grad, section = lax.optimization_barrier((own_half, features_grad, section))
    other_half = lax.ppermute(own_half, "ch", other_core)

    def like(*shape):
        return jax.ShapeDtypeStruct(shape, F32)

    (
        conv_grad,
        reduce_grad,
        expand_grad,
        height_grad,
        width_grad,
        channel_grad,
        output_grad,
        squeeze_grad,
        excite_grad,
        squeeze_bias_grad,
        norm_gain_grad,
        norm_bias_grad,
        height_bias_grad,
        width_bias_grad,
        output_bias_grad,
        second_gain_grad,
        second_bias_grad,
        reduce_bias_grad,
        expand_bias_grad,
        excite_bias_grad,
        conv_bias_grad,
    ) = pl.pallas_call(
        weight_kernel,
        cost_estimate=cost(2.8),
        out_shape=(
            like(9, OUT, CH),
            like(FF, CH),
            like(CH, FF),
            like(CH, CH),
            like(CH, CH),
            like(CH, CH),
            like(CH, CH),
            like(RED, CH),
            like(RED, 3 * CH),
            like(RED),
        )
        + tuple(like(size) for size in VECTOR_SIZES),
        in_specs=[pl.BlockSpec(memory_space=pltpu.SMEM)] + [whole] * 2,
        out_specs=(whole,) * 21,
        scratch_shapes=[pltpu.VMEM((shards, WROWS, LANES), BF16)],
        compiler_params=params(6),
    )(info, own_half, other_half)
    return (
        section,
        features_grad,
        norm_gain_grad,
        norm_bias_grad,
        height_grad,
        height_bias_grad,
        width_grad,
        width_bias_grad,
        channel_grad,
        squeeze_grad.T,
        squeeze_bias_grad,
        excite_grad,
        excite_bias_grad,
        output_grad,
        output_bias_grad,
        second_gain_grad,
        second_bias_grad,
        expand_grad,
        expand_bias_grad,
        reduce_grad,
        reduce_bias_grad,
        jnp.transpose(conv_grad, (1, 0, 2)),
        conv_bias_grad,
    )


def solution(mesh):
    split = P("ch", "img")
    return jax.shard_map(
        body,
        mesh=mesh,
        in_specs=(split, P("img")) + (P(),) * 22 + (split,),
        out_specs=(split, split) + (P(),) * 21,
        check_vma=False,
    )
```

```python
import jax
import jax.numpy as jnp
from jax import lax
from jax.experimental import pallas as pl
from jax.experimental.pallas import tpu as pltpu
from jax.sharding import PartitionSpec as P

CH = 128
FF = 512
RED = 32
OUT = 320
SIDE = 36
PIX = SIDE * SIDE
HALF = SIDE // 2
OPIX = HALF * HALF
WIDE = 40
FLAT = SIDE * WIDE
GUARD = 48
EPS = 1e-05
LANES = 128
WIN = 11
OTILE = 3
PIXROWS = 80
WROWS = 144

F32 = jnp.float32
BF16 = jnp.bfloat16

AT_CONV = 0
AT_REDUCE = 2880
AT_EXPAND = 3392
AT_HEIGHT = 3904
AT_WIDTH = 4032
AT_CHANNEL = 4160
AT_OUTPUT = 4288
AT_SQUEEZE = 4416
AT_EXCITE = 4448
AT_SQ_BIAS = 4544
AT_VECTOR = 4576
VECTOR_ROWS = (0, 1, 2, 3, 4, 5, 6, 7, 8, 12, 15)
VECTOR_SIZES = (CH,) * 8 + (FF, 3 * CH, OUT)


def params(mebibytes):
    return pltpu.CompilerParams(vmem_limit_bytes=mebibytes * 1024 * 1024)


def cost(micros):
    return pl.CostEstimate(flops=0, bytes_accessed=int(micros * 3.69e6), transcendentals=0)


def first_tile(k):
    return 10 * k + k // 8


def nn(a, b):
    return lax.dot_general(a, b, (((1,), (0,)), ((), ())), preferred_element_type=F32)


def nt(a, b):
    return lax.dot_general(a, b, (((1,), (1,)), ((), ())), preferred_element_type=F32)


def tn(a, b):
    return lax.dot_general(a, b, (((0,), (0,)), ((), ())), preferred_element_type=F32)


def lane_mean(v):
    return jnp.sum(v, axis=1, keepdims=True) * (1.0 / CH)


def col_sum(v):
    return jnp.sum(v, axis=0, keepdims=True)


def normal_parts(x):
    cdf = 0.5 + 0.5 * lax.erf(x * 0.7071067811865476)
    return cdf, (x * 0.3989422804014327) * jnp.exp(x * (x * -0.5))


def pack_kernel(feat_hbm, cot_hbm, out, stage, cots, feat, cot, ready):
    images = out.shape[0]
    first = pltpu.make_async_copy(feat_hbm, feat, ready.at[0])
    second = pltpu.make_async_copy(cot_hbm, cot, ready.at[1])
    first.start()
    second.start()
    first.wait()
    for k in range(images):
        base = k * PIXROWS
        begin = first_tile(k) * LANES
        for t in range(WIN):
            stage[base + 4 * t : base + 4 * t + 4, :] = feat[
                :, begin + t * LANES : begin + (t + 1) * LANES
            ].astype(F32)
    second.wait()
    cots[...] = cot[...].astype(F32)
    for k in range(images):
        base = k * PIXROWS
        for j in range(OTILE):
            width = min(LANES, OPIX - j * LANES)
            at = k * OPIX + j * LANES
            row = base + 44 + 10 * j
            stage[row : row + 10, 0:width] = cots[:, at : at + width]
        out[k] = stage[base : base + PIXROWS, :].astype(BF16)


def main_kernel(
    info,
    recv,
    vecs,
    sqt,
    sqb,
    exw,
    kbias,
    hw,
    ww,
    cw,
    ow,
    xw,
    rw,
    kw,
    keep_out,
    send_out,
    grad,
    section_out,
    xf,
    cf,
    tall,
    canvas,
    valid,
    xhat,
    rstd,
    norm,
    rows_b,
    cols_b,
    norm_b,
    branch_h,
    branch_w,
    branch_c,
    mixed_b,
    xhat2,
    rstd2,
    norm2_b,
    hidden_b,
    slope,
    block,
    planes,
    taps,
    spread,
    gblock,
    gresid,
    gmixed,
    grows,
    gcols,
    gpre_b,
    sums,
    rows_out,
):
    shift = info[0]
    side = info[1]
    core = info[2]

    def vec(i):
        return vecs[i : i + 1, :]

    def put(row, value):
        count = value.shape[0]
        done = 0
        while done < count:
            chunk, inner = divmod(row + done, WROWS)
            size = min(count - done, WROWS - inner)
            slot = core if chunk % 2 == 0 else 1 - core
            rows_out[slot, chunk // 2, inner : inner + size, :] = value[done : done + size, :]
            done += size

    def total_of(row, value):
        sums[row : row + 1, :] = col_sum(value)

    cf[OUT:, :] = jnp.zeros((cf.shape[0] - OUT, cf.shape[1]), F32)
    for s in range(recv.shape[0]):
        piece = recv[s].astype(F32)
        for t in range(WIN):
            xf[4 * s : 4 * s + 4, t * LANES : (t + 1) * LANES] = piece[4 * t : 4 * t + 4, :]
        for j in range(OTILE):
            cf[10 * s : 10 * s + 10, j * LANES : (j + 1) * LANES] = piece[
                44 + 10 * j : 54 + 10 * j, :
            ]
    begin = pl.multiple_of(112 - shift, 16)
    for t in range(WIN):
        tall[pl.ds(begin + t * LANES, LANES), :] = xf[:, t * LANES : (t + 1) * LANES].T

    column = lax.broadcasted_iota(jnp.int32, (WIDE, CH), 0)
    for r in range(SIDE):
        keep = (column < side) & (r < side)
        canvas[r * WIDE : (r + 1) * WIDE, :] = jnp.where(
            keep, tall[112 + r * SIDE : 112 + r * SIDE + WIDE, :], 0.0
        )
        valid[r * WIDE : (r + 1) * WIDE, :] = jnp.where(keep, 1.0, 0.0)
    edge = jnp.zeros((GUARD, CH), F32)
    for ref in (norm, block, grows, gcols):
        ref[0:GUARD, :] = edge
        ref[GUARD + FLAT : FLAT + 2 * GUARD, :] = edge
    sums[...] = jnp.zeros_like(sums)

    def moved(ref, by):
        return ref[GUARD + by : GUARD + by + FLAT, :]

    x = canvas[...]
    center = x - lane_mean(x)
    scale = lax.rsqrt(lane_mean(center * center) + EPS)
    unit = center * scale
    xhat[...] = unit
    rstd[...] = jnp.broadcast_to(scale, unit.shape)
    value = jnp.where(valid[...] > 0, unit * vec(0) + vec(1), 0.0)
    norm[GUARD : GUARD + FLAT, :] = value.astype(BF16).astype(F32)

    by_row = vec(15)
    by_col = vec(16)
    plain = moved(norm, 0)
    rows_b[...] = jnp.where(
        by_row < 0, moved(norm, -WIDE), jnp.where(by_row > 0, moved(norm, WIDE), plain)
    ).astype(BF16)
    cols_b[...] = jnp.where(
        by_col < 0, moved(norm, -1), jnp.where(by_col > 0, moved(norm, 1), plain)
    ).astype(BF16)
    norm_b[...] = plain.astype(BF16)
    bh = nn(rows_b[...], hw[...]) + vec(2)
    bw = nn(cols_b[...], ww[...]) + vec(3)
    bc = nn(norm_b[...], cw[...])
    branch_h[...] = bh
    branch_w[...] = bw
    branch_c[...] = bc
    total = col_sum(valid[...] * (bh + bw + bc))

    index = lax.broadcasted_iota(jnp.int32, (1, OTILE * LANES), 1)
    lane_row = ((index.astype(F32) + 0.5) * (1.0 / HALF)).astype(jnp.int32)
    lane_col = index - lane_row * HALF
    out_keep = (2 * lane_row < side) & (2 * lane_col < side)
    cot = jnp.where(out_keep, cf[...], 0.0)
    cot_b = cot[0:OUT, :].astype(BF16)
    cot_t = cot.T.astype(BF16)[:, 0:OUT]
    kb_rows = jnp.sum(cot, axis=1, keepdims=True)
    spread[...] = nn(cot_t, kw[...])
    count = jnp.full((1, CH), side * side, jnp.int32).astype(F32)
    means = total / count
    inner_pre = jnp.sum(sqt[...] * means, axis=1, keepdims=True) + sqb[...]
    inner_cdf, inner_density = normal_parts(inner_pre)
    inner = inner_pre * inner_cdf
    inner_slope = inner_cdf + inner_density
    logit = [col_sum(exw[:, j * CH : (j + 1) * CH] * inner) + vec(12 + j) for j in range(3)]
    top = jnp.maximum(jnp.maximum(logit[0], logit[1]), logit[2])
    grown = [jnp.exp(v - top) for v in logit]
    whole = grown[0] + grown[1] + grown[2]
    mix = [v / whole for v in grown]

    mixed = mix[0] * branch_h[...] + mix[1] * branch_w[...] + mix[2] * branch_c[...]
    mixed_b[...] = mixed.astype(BF16)
    resid = canvas[...] + nn(mixed_b[...], ow[...]) + vec(4)
    center = resid - lane_mean(resid)
    scale = lax.rsqrt(lane_mean(center * center) + EPS)
    unit = center * scale
    xhat2[...] = unit
    rstd2[...] = jnp.broadcast_to(scale, unit.shape)
    norm2_b[...] = (unit * vec(5) + vec(6)).astype(BF16)
    used = 336
    row_id = lax.broadcasted_iota(jnp.int32, (used, CH), 0)
    row_of = ((row_id.astype(F32) + 0.5) * (1.0 / HALF)).astype(jnp.int32)
    out_column = row_id - row_of * HALF
    inside = out_column[0:OPIX, :] < HALF - 1

    def part(tap, ahead, masked):
        value = spread[ahead : ahead + OPIX, tap * CH : (tap + 1) * CH]
        return jnp.where(inside, value, 0.0) if masked else value

    found = (
        part(4, 0, False),
        part(5, 0, False) + part(3, 1, True),
        part(7, 0, False) + part(1, HALF, False),
        (part(8, 0, False) + part(6, 1, True)) + (part(2, HALF, False) + part(0, HALF + 1, True)),
    )
    for p in range(4):
        planes[p, 0:OPIX, :] = found[p]
        for i in range(HALF):
            at = (2 * i + p // 2) * WIDE + p % 2
            gblock[pl.ds(at, HALF, stride=2), :] = planes[p, i * HALF : (i + 1) * HALF, :]

    through = resid + vec(7)
    for j in range(FF // CH):
        lanes = slice(j * CH, (j + 1) * CH)
        pre = nn(norm2_b[...], xw[:, lanes]) + vec(8 + j)
        cdf, density = normal_parts(pre)
        hidden_b[:, lanes] = (pre * cdf).astype(BF16)
        slope[:, lanes] = cdf + density
    through = through + nn(hidden_b[...], rw[...])
    value = jnp.where(valid[...] > 0, through, 0.0)
    block[GUARD : GUARD + FLAT, :] = value.astype(BF16).astype(F32)

    top_rows = 24
    for p in range(4):
        planes[p, 0:top_rows, :] = jnp.zeros((top_rows, CH), F32)
        planes[p, top_rows + OPIX :, :] = jnp.zeros((planes.shape[1] - top_rows - OPIX, CH), F32)
        for i in range(HALF):
            at = GUARD + (2 * i + p // 2) * WIDE + p % 2
            row = top_rows + i * HALF
            planes[p, row : row + HALF, :] = block[pl.ds(at, HALF, stride=2), :]
    for a in range(3):
        for b in range(3):
            plane = 2 * ((a + 1) % 2) + (b + 1) % 2
            row = top_rows - HALF * (a == 0) - (b == 0)
            value = planes[plane, row : row + used, :]
            if b == 0:
                value = jnp.where(out_column > 0, value, 0.0)
            taps[0:used, (3 * a + b) * CH : (3 * a + b + 1) * CH] = value.astype(BF16)
    taps[used:, :] = jnp.zeros((taps.shape[0] - used, taps.shape[1]), BF16)
    gb = jnp.where(valid[...] > 0, gblock[...], 0.0)
    gred = gb.astype(BF16)
    total_of(7, gred.astype(F32))
    for j in range(FF // (2 * CH)):
        lanes = slice(2 * j * CH, 2 * (j + 1) * CH)
        gpre = (nt(gred, rw[lanes, :]) * slope[:, lanes]).astype(BF16)
        total_of(8 + 2 * j, gpre[:, 0:CH].astype(F32))
        total_of(9 + 2 * j, gpre[:, CH:].astype(F32))
        gpre_b[:, lanes] = gpre
    gn2 = nt(gpre_b[...], xw[...])
    conv = nn(cot_b, taps[...])
    for t in range(9):
        put(AT_CONV + t * OUT, conv[:, t * CH : (t + 1) * CH])
    unit = xhat2[...]
    total_of(5, gn2 * unit)
    total_of(6, gn2)
    gy = gn2 * vec(5)
    gr = gb + rstd2[...] * (gy - lane_mean(gy) - unit * lane_mean(gy * unit))
    gresid[...] = gr
    gproj = gr.astype(BF16)
    total_of(4, gproj.astype(F32))
    grown = tn(gred, hidden_b[...])
    for j in range(FF // CH):
        put(AT_REDUCE + j * CH, grown[:, j * CH : (j + 1) * CH].T)
    gm = nt(gproj, ow[...])
    gmixed[...] = gm
    section = nt(kw[...], taps[...]) + kbias[...]
    section_out[...] = jnp.where(out_keep, section, 0.0)
    gmix = [col_sum(gm * branch[...]) for branch in (branch_h, branch_w, branch_c)]
    put(AT_OUTPUT, tn(mixed_b[...], gproj))
    inner_dot = mix[0] * gmix[0] + mix[1] * gmix[1] + mix[2] * gmix[2]
    glogit = [mix[j] * (gmix[j] - inner_dot) for j in range(3)]
    ginner = jnp.zeros((RED, 1), F32)
    for j in range(3):
        ginner += jnp.sum(exw[:, j * CH : (j + 1) * CH] * glogit[j], axis=1, keepdims=True)
        put(AT_EXCITE + RED * j, inner * glogit[j])
        sums[12 + j : 13 + j, :] = glogit[j]
    ginner = ginner * inner_slope
    put(AT_SQUEEZE, ginner * means)
    put(AT_SQ_BIAS, jnp.broadcast_to(ginner, (RED, CH)))
    gmeans = col_sum(sqt[...] * ginner) / count

    gm = gmixed[...]
    level = valid[...] * gmeans
    gh = (mix[0] * gm + level).astype(BF16)
    gw = (mix[1] * gm + level).astype(BF16)
    gc = (mix[2] * gm + level).astype(BF16)
    total_of(2, gh.astype(F32))
    total_of(3, gw.astype(F32))
    grown = tn(norm2_b[...], gpre_b[...])
    for j in range(FF // CH):
        put(AT_EXPAND + j * CH, grown[:, j * CH : (j + 1) * CH])
    grows[GUARD : GUARD + FLAT, :] = nt(gh, hw[...])
    gcols[GUARD : GUARD + FLAT, :] = nt(gw, ww[...])
    value = nt(gc, cw[...])
    put(AT_HEIGHT, tn(rows_b[...], gh))
    put(AT_WIDTH, tn(cols_b[...], gw))
    put(AT_CHANNEL, tn(norm_b[...], gc))
    value = value + jnp.where(
        by_row < 0,
        moved(grows, WIDE),
        jnp.where(by_row > 0, moved(grows, -WIDE), moved(grows, 0)),
    )
    value = value + jnp.where(
        by_col < 0, moved(gcols, 1), jnp.where(by_col > 0, moved(gcols, -1), moved(gcols, 0))
    )
    keep = valid[...] > 0
    value = jnp.where(keep, value, 0.0)
    unit = xhat[...]
    total_of(0, value * unit)
    total_of(1, value)
    gy = value * vec(0)
    back = rstd[...] * (gy - lane_mean(gy) - unit * lane_mean(gy * unit))
    grad[...] = jnp.where(keep, gresid[...] + back, 0.0)

    same = lax.broadcasted_iota(jnp.int32, (LANES, LANES), 0) == lax.broadcasted_iota(
        jnp.int32, (LANES, LANES), 1
    )
    for j in range(OTILE):
        total_of(15 + j, jnp.where(same, kb_rows[j * LANES : (j + 1) * LANES, :], 0.0))
    put(AT_VECTOR, sums[...])
    keep_out[...] = rows_out[0]
    send_out[...] = rows_out[1].astype(BF16)


def send_kernel(info, grad, section, out, tall, turned, stage):
    begin = pl.multiple_of(112 - info[0], 16)
    tall[0:112, :] = jnp.zeros((112, CH), F32)
    tall[112 + PIX :, :] = jnp.zeros((tall.shape[0] - 112 - PIX, CH), F32)
    for r in range(SIDE):
        tall[112 + r * SIDE : 112 + (r + 1) * SIDE, :] = grad[r * WIDE : r * WIDE + SIDE, :]
    for t in range(WIN):
        turned[:, t * LANES : (t + 1) * LANES] = tall[pl.ds(begin + t * LANES, LANES), :].T
    for s in range(out.shape[0]):
        base = s * PIXROWS
        for t in range(WIN):
            stage[base + 4 * t : base + 4 * t + 4, :] = turned[
                4 * s : 4 * s + 4, t * LANES : (t + 1) * LANES
            ]
        for j in range(OTILE):
            stage[base + 44 + 10 * j : base + 54 + 10 * j, :] = section[
                10 * s : 10 * s + 10, j * LANES : (j + 1) * LANES
            ]
        out[s] = stage[base : base + PIXROWS, :].astype(BF16)


def pair_kernel(kept, met, out):
    out[...] = (kept[...] + met[...].astype(F32)).astype(BF16)


def add_kernel(recv, out):
    total = recv[0].astype(F32)
    for s in range(1, recv.shape[0]):
        total += recv[s].astype(F32)
    out[...] = total.astype(BF16)


def copies_kernel(mine, one, two, three, out):
    total = (mine[...].astype(F32) + two[...].astype(F32)) + (
        one[...].astype(F32) + three[...].astype(F32)
    )
    total = total.astype(BF16)
    for s in range(out.shape[0]):
        out[s] = total


def pixel_kernel(info, near, far, feat, section, stage, recv):
    core = info[2]
    for i in range(near.shape[0]):
        recv[2 * i + core] = near[i]
        recv[2 * i + 1 - core] = far[i]
    for k in range(recv.shape[0]):
        piece = recv[k].astype(F32)
        tile = first_tile(k)
        for t in range(WIN):
            lanes = slice((tile + t) * LANES, (tile + t + 1) * LANES)
            value = piece[4 * t : 4 * t + 4, :]
            if t == 0 and k % 8:
                feat[:, lanes] += value
            else:
                feat[:, lanes] = value
        for j in range(OTILE):
            width = min(LANES, OPIX - j * LANES)
            at = k * OPIX + j * LANES
            stage[:, at : at + width] = piece[44 + 10 * j : 54 + 10 * j, 0:width]
    section[...] = stage[...].astype(BF16)


def weight_kernel(info, own, other, *refs):
    outs = refs[:-1]
    both = refs[-1]
    core = info[2]
    for i in range(own.shape[0]):
        both[2 * i + core] = own[i]
        both[2 * i + 1 - core] = other[i]

    def rows(at, count):
        found = []
        done = 0
        while done < count:
            chunk, inner = divmod(at + done, WROWS)
            size = min(count - done, WROWS - inner)
            found.append(both[chunk, inner : inner + size, :])
            done += size
        return jnp.concatenate(found).astype(F32)

    conv, red, exp, height, width, chan, outw, squeeze, excite, sq_bias = outs[:10]
    for t in range(9):
        conv[t] = rows(AT_CONV + t * OUT, OUT)
    red[...] = rows(AT_REDUCE, FF)
    for j in range(FF // CH):
        exp[:, j * CH : (j + 1) * CH] = rows(AT_EXPAND + j * CH, CH)
    for at, ref in (
        (AT_HEIGHT, height),
        (AT_WIDTH, width),
        (AT_CHANNEL, chan),
        (AT_OUTPUT, outw),
    ):
        ref[...] = rows(at, CH)
    squeeze[...] = rows(AT_SQUEEZE, RED)
    for j in range(3):
        excite[:, j * CH : (j + 1) * CH] = rows(AT_EXCITE + j * RED, RED)
    same = lax.broadcasted_iota(jnp.int32, (RED, CH), 0) == lax.broadcasted_iota(
        jnp.int32, (RED, CH), 1
    )
    sq_bias[...] = jnp.sum(jnp.where(same, rows(AT_SQ_BIAS, RED), 0.0), axis=0)[0:RED]
    vectors = rows(AT_VECTOR, RED)
    for ref, row in zip(outs[10:], VECTOR_ROWS):
        size = ref.shape[0]
        for j in range(-(-size // CH)):
            width = min(CH, size - j * CH)
            ref[j * CH : j * CH + width] = vectors[row + j, 0:width]


def body(
    features,
    size_group,
    cycle_offsets,
    norm_gain,
    norm_bias,
    height_weight,
    height_bias,
    width_weight,
    width_bias,
    channel_weight,
    squeeze_weight,
    squeeze_bias,
    excite_weight,
    excite_bias,
    output_weight,
    output_bias,
    second_gain,
    second_bias,
    expand_weight,
    expand_bias,
    reduce_weight,
    reduce_bias,
    stride_weight,
    stride_bias,
    cotangent,
):
    shards = lax.axis_size("ch")
    rank = lax.axis_index("ch")
    side = SIDE - 4 * (2 - lax.dynamic_index_in_dim(size_group, rank, keepdims=False))
    info = jnp.stack([16 * (rank % 8), side, rank % 2]).astype(jnp.int32)
    vecs = jnp.concatenate(
        [
            v.astype(F32)
            for v in (
                norm_gain,
                norm_bias,
                height_bias,
                width_bias,
                output_bias,
                second_gain,
                second_bias,
                reduce_bias,
                expand_bias,
                excite_bias,
                cycle_offsets[0],
                cycle_offsets[1],
            )
        ]
    ).reshape(17, CH)

    whole = pl.BlockSpec(memory_space=pltpu.VMEM)
    chunks = pl.pallas_call(
        pack_kernel,
        cost_estimate=cost(2.5),
        out_shape=jax.ShapeDtypeStruct((shards, PIXROWS, LANES), BF16),
        in_specs=[pl.BlockSpec(memory_space=pltpu.HBM)] * 2,
        out_specs=whole,
        scratch_shapes=[
            pltpu.VMEM((shards * PIXROWS, LANES), F32),
            pltpu.VMEM(cotangent.shape, F32),
            pltpu.VMEM(features.shape, BF16),
            pltpu.VMEM(cotangent.shape, BF16),
            pltpu.SemaphoreType.DMA((2,)),
        ],
        compiler_params=params(56),
    )(features, cotangent)
    arrived = lax.all_to_all(chunks, "ch", split_axis=0, concat_axis=0, tiled=True)

    canvas = pltpu.VMEM((FLAT, CH), F32)
    guarded = pltpu.VMEM((FLAT + 2 * GUARD, CH), F32)
    narrow = pltpu.VMEM((FLAT, CH), BF16)
    kept, sent, grad, section_part = pl.pallas_call(
        main_kernel,
        cost_estimate=cost(22),
        out_shape=(
            jax.ShapeDtypeStruct((shards // 2, WROWS, LANES), F32),
            jax.ShapeDtypeStruct((shards // 2, WROWS, LANES), BF16),
            jax.ShapeDtypeStruct((FLAT, CH), F32),
            jax.ShapeDtypeStruct((OUT, OTILE * LANES), F32),
        ),
        in_specs=[pl.BlockSpec(memory_space=pltpu.SMEM)] + [whole] * 13,
        out_specs=(whole,) * 4,
        scratch_shapes=[
            pltpu.VMEM((CH, WIN * LANES), F32),
            pltpu.VMEM((3 * LANES, OTILE * LANES), F32),
            pltpu.VMEM((112 + WIN * LANES, CH), F32),
            canvas,
            canvas,
            canvas,
            canvas,
            guarded,
            narrow,
            narrow,
            narrow,
            canvas,
            canvas,
            canvas,
            narrow,
            canvas,
            canvas,
            narrow,
            pltpu.VMEM((FLAT, FF), BF16),
            pltpu.VMEM((FLAT, FF), F32),
            guarded,
            pltpu.VMEM((4, 360, CH), F32),
            pltpu.VMEM((OTILE * LANES, 9 * CH), BF16),
            pltpu.VMEM((OTILE * LANES, 9 * CH), F32),
            canvas,
            canvas,
            canvas,
            guarded,
            guarded,
            pltpu.VMEM((FLAT, FF), BF16),
            pltpu.VMEM((RED, CH), F32),
            pltpu.VMEM((2, shards // 2, WROWS, LANES), F32),
        ],
        compiler_params=params(42),
    )(
        info,
        arrived,
        vecs,
        squeeze_weight.astype(F32).T,
        squeeze_bias.astype(F32)[:, None],
        excite_weight.astype(F32),
        stride_bias.astype(F32)[:, None],
        height_weight,
        width_weight,
        channel_weight,
        output_weight,
        expand_weight,
        reduce_weight,
        stride_weight.reshape(OUT, 9 * CH),
    )
    other_core = [(i, i ^ 1) for i in range(shards)]
    same_core = [[2 * i + c for i in range(shards // 2)] for c in range(2)]
    met = lax.ppermute(sent, "ch", other_core)
    pixels = pl.pallas_call(
        send_kernel,
        cost_estimate=cost(2.5),
        out_shape=jax.ShapeDtypeStruct((shards, PIXROWS, LANES), BF16),
        in_specs=[pl.BlockSpec(memory_space=pltpu.SMEM)] + [whole] * 2,
        out_specs=whole,
        scratch_shapes=[
            pltpu.VMEM((112 + WIN * LANES, CH), F32),
            pltpu.VMEM((CH, WIN * LANES), F32),
            pltpu.VMEM((shards * PIXROWS, LANES), F32),
        ],
        compiler_params=params(8),
    )(info, grad, section_part)
    kept, pixels = lax.optimization_barrier((kept, pixels))
    partial = pl.pallas_call(
        pair_kernel,
        cost_estimate=cost(2.3),
        out_shape=jax.ShapeDtypeStruct(kept.shape, BF16),
        in_specs=[whole] * 2,
        out_specs=whole,
        compiler_params=params(3),
    )(kept, met)

    def exchange(v):
        return lax.all_to_all(
            v, "ch", split_axis=0, concat_axis=0, tiled=True, axis_index_groups=same_core
        )

    parts = exchange(partial)
    parts, pixels = lax.optimization_barrier((parts, pixels))
    back = exchange(pixels.reshape(shards // 2, 2, PIXROWS, LANES))

    mine = pl.pallas_call(
        add_kernel,
        cost_estimate=cost(1.7),
        out_shape=jax.ShapeDtypeStruct((WROWS, LANES), BF16),
        compiler_params=params(2),
    )(parts)
    groups = lax.axis_size("img")
    other = [
        lax.ppermute(mine, "img", [(i, (i + d) % groups) for i in range(groups)])
        for d in (1, 2, 3)
    ]
    copies = pl.pallas_call(
        copies_kernel,
        cost_estimate=cost(1.7),
        in_specs=[whole] * 4,
        out_specs=whole,
        out_shape=jax.ShapeDtypeStruct((shards // 2, WROWS, LANES), BF16),
        compiler_params=params(2),
    )(mine, *other)
    copies, back = lax.optimization_barrier((copies, back))
    own_half = exchange(copies)
    core = rank % 2
    near = lax.dynamic_index_in_dim(back, core, axis=1, keepdims=False)
    far = lax.dynamic_index_in_dim(back, 1 - core, axis=1, keepdims=False)
    far = lax.ppermute(far, "ch", other_core)

    features_grad, section = pl.pallas_call(
        pixel_kernel,
        cost_estimate=cost(2.5),
        out_shape=(
            jax.ShapeDtypeStruct(features.shape, F32),
            jax.ShapeDtypeStruct(cotangent.shape, BF16),
        ),
        in_specs=[pl.BlockSpec(memory_space=pltpu.SMEM)] + [whole] * 2,
        out_specs=(whole,) * 2,
        scratch_shapes=[
            pltpu.VMEM(cotangent.shape, F32),
            pltpu.VMEM((shards, PIXROWS, LANES), BF16),
        ],
        compiler_params=params(5),
    )(info, near, far)

    own_half, features_grad, section = lax.optimization_barrier((own_half, features_grad, section))
    other_half = lax.ppermute(own_half, "ch", other_core)

    def like(*shape):
        return jax.ShapeDtypeStruct(shape, F32)

    (
        conv_grad,
        reduce_grad,
        expand_grad,
        height_grad,
        width_grad,
        channel_grad,
        output_grad,
        squeeze_grad,
        excite_grad,
        squeeze_bias_grad,
        norm_gain_grad,
        norm_bias_grad,
        height_bias_grad,
        width_bias_grad,
        output_bias_grad,
        second_gain_grad,
        second_bias_grad,
        reduce_bias_grad,
        expand_bias_grad,
        excite_bias_grad,
        conv_bias_grad,
    ) = pl.pallas_call(
        weight_kernel,
        cost_estimate=cost(2.8),
        out_shape=(
            like(9, OUT, CH),
            like(FF, CH),
            like(CH, FF),
            like(CH, CH),
            like(CH, CH),
            like(CH, CH),
            like(CH, CH),
            like(RED, CH),
            like(RED, 3 * CH),
            like(RED),
        )
        + tuple(like(size) for size in VECTOR_SIZES),
        in_specs=[pl.BlockSpec(memory_space=pltpu.SMEM)] + [whole] * 2,
        out_specs=(whole,) * 21,
        scratch_shapes=[pltpu.VMEM((shards, WROWS, LANES), BF16)],
        compiler_params=params(6),
    )(info, own_half, other_half)
    return (
        section,
        features_grad,
        norm_gain_grad,
        norm_bias_grad,
        height_grad,
        height_bias_grad,
        width_grad,
        width_bias_grad,
        channel_grad,
        squeeze_grad.T,
        squeeze_bias_grad,
        excite_grad,
        excite_bias_grad,
        output_grad,
        output_bias_grad,
        second_gain_grad,
        second_bias_grad,
        expand_grad,
        expand_bias_grad,
        reduce_grad,
        reduce_bias_grad,
        jnp.transpose(conv_grad, (1, 0, 2)),
        conv_bias_grad,
    )


def solution(mesh):
    split = P("ch", "img")
    return jax.shard_map(
        body,
        mesh=mesh,
        in_specs=(split, P("img")) + (P(),) * 22 + (split,),
        out_specs=(split, split) + (P(),) * 21,
        check_vma=False,
    )
```

```python
import jax
import jax.numpy as jnp
from jax import lax
from jax.experimental import pallas as pl
from jax.experimental.pallas import tpu as pltpu
from jax.sharding import PartitionSpec as P

CH = 128
FF = 512
RED = 32
OUT = 320
SIDE = 36
PIX = SIDE * SIDE
HALF = SIDE // 2
OPIX = HALF * HALF
WIDE = 40
FLAT = SIDE * WIDE
GUARD = 48
EPS = 1e-05
LANES = 128
WIN = 11
OTILE = 3
PIXROWS = 80
WROWS = 144

F32 = jnp.float32
BF16 = jnp.bfloat16

AT_CONV = 0
AT_REDUCE = 2880
AT_EXPAND = 3392
AT_HEIGHT = 3904
AT_WIDTH = 4032
AT_CHANNEL = 4160
AT_OUTPUT = 4288
AT_SQUEEZE = 4416
AT_EXCITE = 4448
AT_SQ_BIAS = 4544
AT_VECTOR = 4576
VECTOR_ROWS = (0, 1, 2, 3, 4, 5, 6, 7, 8, 12, 15)
VECTOR_SIZES = (CH,) * 8 + (FF, 3 * CH, OUT)


def params(mebibytes):
    return pltpu.CompilerParams(vmem_limit_bytes=mebibytes * 1024 * 1024)


def cost(micros):
    return pl.CostEstimate(flops=0, bytes_accessed=int(micros * 3.69e6), transcendentals=0)


def first_tile(k):
    return 10 * k + k // 8


def nn(a, b):
    return lax.dot_general(a, b, (((1,), (0,)), ((), ())), preferred_element_type=F32)


def nt(a, b):
    return lax.dot_general(a, b, (((1,), (1,)), ((), ())), preferred_element_type=F32)


def tn(a, b):
    return lax.dot_general(a, b, (((0,), (0,)), ((), ())), preferred_element_type=F32)


def lane_mean(v):
    return jnp.sum(v, axis=1, keepdims=True) * (1.0 / CH)


def col_sum(v):
    return jnp.sum(v, axis=0, keepdims=True)


def normal_parts(x):
    cdf = 0.5 + 0.5 * lax.erf(x * 0.7071067811865476)
    return cdf, (x * 0.3989422804014327) * jnp.exp(x * (x * -0.5))


def pack_kernel(feat_hbm, cot_hbm, out, stage, cots, feat, cot, ready):
    images = out.shape[0]
    first = pltpu.make_async_copy(cot_hbm, cot, ready.at[0])
    second = pltpu.make_async_copy(feat_hbm, feat, ready.at[1])
    first.start()
    second.start()
    first.wait()
    cots[...] = cot[...].astype(F32)
    for k in range(images):
        base = k * PIXROWS
        for j in range(OTILE):
            width = min(LANES, OPIX - j * LANES)
            at = k * OPIX + j * LANES
            row = base + 44 + 10 * j
            stage[row : row + 10, 0:width] = cots[:, at : at + width]
    second.wait()
    for k in range(images):
        base = k * PIXROWS
        begin = first_tile(k) * LANES
        for t in range(WIN):
            stage[base + 4 * t : base + 4 * t + 4, :] = feat[
                :, begin + t * LANES : begin + (t + 1) * LANES
            ].astype(F32)
        out[k] = stage[base : base + PIXROWS, :].astype(BF16)


def main_kernel(
    info,
    recv,
    vecs,
    sqt,
    sqb,
    exw,
    kbias,
    hw,
    ww,
    cw,
    ow,
    xw,
    rw,
    kw,
    keep_out,
    send_out,
    grad,
    section_out,
    xf,
    cf,
    tall,
    canvas,
    valid,
    xhat,
    rstd,
    norm,
    rows_b,
    cols_b,
    norm_b,
    branch_h,
    branch_w,
    branch_c,
    mixed_b,
    xhat2,
    rstd2,
    norm2_b,
    hidden_b,
    slope,
    block,
    planes,
    taps,
    spread,
    gblock,
    gresid,
    gmixed,
    grows,
    gcols,
    gpre_b,
    sums,
    rows_out,
):
    shift = info[0]
    side = info[1]
    core = info[2]

    def vec(i):
        return vecs[i : i + 1, :]

    def put(row, value):
        count = value.shape[0]
        done = 0
        while done < count:
            chunk, inner = divmod(row + done, WROWS)
            size = min(count - done, WROWS - inner)
            slot = core if chunk % 2 == 0 else 1 - core
            rows_out[slot, chunk // 2, inner : inner + size, :] = value[done : done + size, :]
            done += size

    def total_of(row, value):
        sums[row : row + 1, :] = col_sum(value)

    cf[OUT:, :] = jnp.zeros((cf.shape[0] - OUT, cf.shape[1]), F32)
    for s in range(recv.shape[0]):
        piece = recv[s].astype(F32)
        for t in range(WIN):
            xf[4 * s : 4 * s + 4, t * LANES : (t + 1) * LANES] = piece[4 * t : 4 * t + 4, :]
        for j in range(OTILE):
            cf[10 * s : 10 * s + 10, j * LANES : (j + 1) * LANES] = piece[
                44 + 10 * j : 54 + 10 * j, :
            ]
    begin = pl.multiple_of(112 - shift, 16)
    for t in range(WIN):
        tall[pl.ds(begin + t * LANES, LANES), :] = xf[:, t * LANES : (t + 1) * LANES].T

    column = lax.broadcasted_iota(jnp.int32, (WIDE, CH), 0)
    for r in range(SIDE):
        keep = (column < side) & (r < side)
        canvas[r * WIDE : (r + 1) * WIDE, :] = jnp.where(
            keep, tall[112 + r * SIDE : 112 + r * SIDE + WIDE, :], 0.0
        )
        valid[r * WIDE : (r + 1) * WIDE, :] = jnp.where(keep, 1.0, 0.0)
    edge = jnp.zeros((GUARD, CH), F32)
    for ref in (norm, block, grows, gcols):
        ref[0:GUARD, :] = edge
        ref[GUARD + FLAT : FLAT + 2 * GUARD, :] = edge
    sums[...] = jnp.zeros_like(sums)

    def moved(ref, by):
        return ref[GUARD + by : GUARD + by + FLAT, :]

    x = canvas[...]
    center = x - lane_mean(x)
    scale = lax.rsqrt(lane_mean(center * center) + EPS)
    unit = center * scale
    xhat[...] = unit
    rstd[...] = jnp.broadcast_to(scale, unit.shape)
    value = jnp.where(valid[...] > 0, unit * vec(0) + vec(1), 0.0)
    norm[GUARD : GUARD + FLAT, :] = value.astype(BF16).astype(F32)

    by_row = vec(15)
    by_col = vec(16)
    plain = moved(norm, 0)
    rows_b[...] = jnp.where(
        by_row < 0, moved(norm, -WIDE), jnp.where(by_row > 0, moved(norm, WIDE), plain)
    ).astype(BF16)
    cols_b[...] = jnp.where(
        by_col < 0, moved(norm, -1), jnp.where(by_col > 0, moved(norm, 1), plain)
    ).astype(BF16)
    norm_b[...] = plain.astype(BF16)
    bh = nn(rows_b[...], hw[...]) + vec(2)
    bw = nn(cols_b[...], ww[...]) + vec(3)
    bc = nn(norm_b[...], cw[...])
    branch_h[...] = bh
    branch_w[...] = bw
    branch_c[...] = bc
    total = col_sum(valid[...] * (bh + bw + bc))

    index = lax.broadcasted_iota(jnp.int32, (1, OTILE * LANES), 1)
    lane_row = ((index.astype(F32) + 0.5) * (1.0 / HALF)).astype(jnp.int32)
    lane_col = index - lane_row * HALF
    out_keep = (2 * lane_row < side) & (2 * lane_col < side)
    cot = jnp.where(out_keep, cf[...], 0.0)
    cot_b = cot[0:OUT, :].astype(BF16)
    cot_t = cot.T.astype(BF16)[:, 0:OUT]
    kb_rows = jnp.sum(cot, axis=1, keepdims=True)
    spread[...] = nn(cot_t, kw[...])
    count = jnp.full((1, CH), side * side, jnp.int32).astype(F32)
    means = total / count
    inner_pre = jnp.sum(sqt[...] * means, axis=1, keepdims=True) + sqb[...]
    inner_cdf, inner_density = normal_parts(inner_pre)
    inner = inner_pre * inner_cdf
    inner_slope = inner_cdf + inner_density
    logit = [col_sum(exw[:, j * CH : (j + 1) * CH] * inner) + vec(12 + j) for j in range(3)]
    top = jnp.maximum(jnp.maximum(logit[0], logit[1]), logit[2])
    grown = [jnp.exp(v - top) for v in logit]
    whole = grown[0] + grown[1] + grown[2]
    mix = [v / whole for v in grown]

    mixed = mix[0] * branch_h[...] + mix[1] * branch_w[...] + mix[2] * branch_c[...]
    mixed_b[...] = mixed.astype(BF16)
    resid = canvas[...] + nn(mixed_b[...], ow[...]) + vec(4)
    center = resid - lane_mean(resid)
    scale = lax.rsqrt(lane_mean(center * center) + EPS)
    unit = center * scale
    xhat2[...] = unit
    rstd2[...] = jnp.broadcast_to(scale, unit.shape)
    norm2_b[...] = (unit * vec(5) + vec(6)).astype(BF16)
    used = 336
    row_id = lax.broadcasted_iota(jnp.int32, (used, CH), 0)
    row_of = ((row_id.astype(F32) + 0.5) * (1.0 / HALF)).astype(jnp.int32)
    out_column = row_id - row_of * HALF
    inside = out_column[0:OPIX, :] < HALF - 1

    def part(tap, ahead, masked):
        value = spread[ahead : ahead + OPIX, tap * CH : (tap + 1) * CH]
        return jnp.where(inside, value, 0.0) if masked else value

    found = (
        part(4, 0, False),
        part(5, 0, False) + part(3, 1, True),
        part(7, 0, False) + part(1, HALF, False),
        (part(8, 0, False) + part(6, 1, True)) + (part(2, HALF, False) + part(0, HALF + 1, True)),
    )
    for p in range(4):
        planes[p, 0:OPIX, :] = found[p]
        for i in range(HALF):
            at = (2 * i + p // 2) * WIDE + p % 2
            gblock[pl.ds(at, HALF, stride=2), :] = planes[p, i * HALF : (i + 1) * HALF, :]

    through = resid + vec(7)
    for j in range(FF // CH):
        lanes = slice(j * CH, (j + 1) * CH)
        pre = nn(norm2_b[...], xw[:, lanes]) + vec(8 + j)
        cdf, density = normal_parts(pre)
        hidden_b[:, lanes] = (pre * cdf).astype(BF16)
        slope[:, lanes] = cdf + density
    through = through + nn(hidden_b[...], rw[...])
    value = jnp.where(valid[...] > 0, through, 0.0)
    block[GUARD : GUARD + FLAT, :] = value.astype(BF16).astype(F32)

    top_rows = 24
    for p in range(4):
        planes[p, 0:top_rows, :] = jnp.zeros((top_rows, CH), F32)
        planes[p, top_rows + OPIX :, :] = jnp.zeros((planes.shape[1] - top_rows - OPIX, CH), F32)
        for i in range(HALF):
            at = GUARD + (2 * i + p // 2) * WIDE + p % 2
            row = top_rows + i * HALF
            planes[p, row : row + HALF, :] = block[pl.ds(at, HALF, stride=2), :]
    for a in range(3):
        for b in range(3):
            plane = 2 * ((a + 1) % 2) + (b + 1) % 2
            row = top_rows - HALF * (a == 0) - (b == 0)
            value = planes[plane, row : row + used, :]
            if b == 0:
                value = jnp.where(out_column > 0, value, 0.0)
            taps[0:used, (3 * a + b) * CH : (3 * a + b + 1) * CH] = value.astype(BF16)
    taps[used:, :] = jnp.zeros((taps.shape[0] - used, taps.shape[1]), BF16)
    gb = jnp.where(valid[...] > 0, gblock[...], 0.0)
    gred = gb.astype(BF16)
    total_of(7, gred.astype(F32))
    for j in range(FF // (2 * CH)):
        lanes = slice(2 * j * CH, 2 * (j + 1) * CH)
        gpre = (nt(gred, rw[lanes, :]) * slope[:, lanes]).astype(BF16)
        total_of(8 + 2 * j, gpre[:, 0:CH].astype(F32))
        total_of(9 + 2 * j, gpre[:, CH:].astype(F32))
        gpre_b[:, lanes] = gpre
    gn2 = nt(gpre_b[...], xw[...])
    conv = nn(cot_b, taps[...])
    for t in range(9):
        put(AT_CONV + t * OUT, conv[:, t * CH : (t + 1) * CH])
    unit = xhat2[...]
    total_of(5, gn2 * unit)
    total_of(6, gn2)
    gy = gn2 * vec(5)
    gr = gb + rstd2[...] * (gy - lane_mean(gy) - unit * lane_mean(gy * unit))
    gresid[...] = gr
    gproj = gr.astype(BF16)
    total_of(4, gproj.astype(F32))
    grown = tn(gred, hidden_b[...])
    for j in range(FF // CH):
        put(AT_REDUCE + j * CH, grown[:, j * CH : (j + 1) * CH].T)
    gm = nt(gproj, ow[...])
    gmixed[...] = gm
    section = nt(kw[...], taps[...]) + kbias[...]
    section_out[...] = jnp.where(out_keep, section, 0.0)
    gmix = [col_sum(gm * branch[...]) for branch in (branch_h, branch_w, branch_c)]
    put(AT_OUTPUT, tn(mixed_b[...], gproj))
    inner_dot = mix[0] * gmix[0] + mix[1] * gmix[1] + mix[2] * gmix[2]
    glogit = [mix[j] * (gmix[j] - inner_dot) for j in range(3)]
    ginner = jnp.zeros((RED, 1), F32)
    for j in range(3):
        ginner += jnp.sum(exw[:, j * CH : (j + 1) * CH] * glogit[j], axis=1, keepdims=True)
        put(AT_EXCITE + RED * j, inner * glogit[j])
        sums[12 + j : 13 + j, :] = glogit[j]
    ginner = ginner * inner_slope
    put(AT_SQUEEZE, ginner * means)
    put(AT_SQ_BIAS, jnp.broadcast_to(ginner, (RED, CH)))
    gmeans = col_sum(sqt[...] * ginner) / count

    gm = gmixed[...]
    level = valid[...] * gmeans
    gh = (mix[0] * gm + level).astype(BF16)
    gw = (mix[1] * gm + level).astype(BF16)
    gc = (mix[2] * gm + level).astype(BF16)
    total_of(2, gh.astype(F32))
    total_of(3, gw.astype(F32))
    grown = tn(norm2_b[...], gpre_b[...])
    for j in range(FF // CH):
        put(AT_EXPAND + j * CH, grown[:, j * CH : (j + 1) * CH])
    grows[GUARD : GUARD + FLAT, :] = nt(gh, hw[...])
    gcols[GUARD : GUARD + FLAT, :] = nt(gw, ww[...])
    value = nt(gc, cw[...])
    put(AT_HEIGHT, tn(rows_b[...], gh))
    put(AT_WIDTH, tn(cols_b[...], gw))
    put(AT_CHANNEL, tn(norm_b[...], gc))
    value = value + jnp.where(
        by_row < 0,
        moved(grows, WIDE),
        jnp.where(by_row > 0, moved(grows, -WIDE), moved(grows, 0)),
    )
    value = value + jnp.where(
        by_col < 0, moved(gcols, 1), jnp.where(by_col > 0, moved(gcols, -1), moved(gcols, 0))
    )
    keep = valid[...] > 0
    value = jnp.where(keep, value, 0.0)
    unit = xhat[...]
    total_of(0, value * unit)
    total_of(1, value)
    gy = value * vec(0)
    back = rstd[...] * (gy - lane_mean(gy) - unit * lane_mean(gy * unit))
    grad[...] = jnp.where(keep, gresid[...] + back, 0.0)

    same = lax.broadcasted_iota(jnp.int32, (LANES, LANES), 0) == lax.broadcasted_iota(
        jnp.int32, (LANES, LANES), 1
    )
    for j in range(OTILE):
        total_of(15 + j, jnp.where(same, kb_rows[j * LANES : (j + 1) * LANES, :], 0.0))
    put(AT_VECTOR, sums[...])
    keep_out[...] = rows_out[0]
    send_out[...] = rows_out[1].astype(BF16)


def send_kernel(info, grad, section, out, tall, turned, stage):
    begin = pl.multiple_of(112 - info[0], 16)
    tall[0:112, :] = jnp.zeros((112, CH), F32)
    tall[112 + PIX :, :] = jnp.zeros((tall.shape[0] - 112 - PIX, CH), F32)
    for r in range(SIDE):
        tall[112 + r * SIDE : 112 + (r + 1) * SIDE, :] = grad[r * WIDE : r * WIDE + SIDE, :]
    for t in range(WIN):
        turned[:, t * LANES : (t + 1) * LANES] = tall[pl.ds(begin + t * LANES, LANES), :].T
    for s in range(out.shape[0]):
        base = s * PIXROWS
        for t in range(WIN):
            stage[base + 4 * t : base + 4 * t + 4, :] = turned[
                4 * s : 4 * s + 4, t * LANES : (t + 1) * LANES
            ]
        for j in range(OTILE):
            stage[base + 44 + 10 * j : base + 54 + 10 * j, :] = section[
                10 * s : 10 * s + 10, j * LANES : (j + 1) * LANES
            ]
        out[s] = stage[base : base + PIXROWS, :].astype(BF16)


def pair_kernel(kept, met, out):
    out[...] = (kept[...] + met[...].astype(F32)).astype(BF16)


def add_kernel(recv, out):
    total = recv[0].astype(F32)
    for s in range(1, recv.shape[0]):
        total += recv[s].astype(F32)
    out[...] = total.astype(BF16)


def copies_kernel(mine, one, two, three, out):
    total = (mine[...].astype(F32) + two[...].astype(F32)) + (
        one[...].astype(F32) + three[...].astype(F32)
    )
    total = total.astype(BF16)
    for s in range(out.shape[0]):
        out[s] = total


def pixel_kernel(info, near, far, feat, section, stage, recv):
    core = info[2]
    for i in range(near.shape[0]):
        recv[2 * i + core] = near[i]
        recv[2 * i + 1 - core] = far[i]
    for k in range(recv.shape[0]):
        piece = recv[k].astype(F32)
        tile = first_tile(k)
        for t in range(WIN):
            lanes = slice((tile + t) * LANES, (tile + t + 1) * LANES)
            value = piece[4 * t : 4 * t + 4, :]
            if t == 0 and k % 8:
                feat[:, lanes] += value
            else:
                feat[:, lanes] = value
        for j in range(OTILE):
            width = min(LANES, OPIX - j * LANES)
            at = k * OPIX + j * LANES
            stage[:, at : at + width] = piece[44 + 10 * j : 54 + 10 * j, 0:width]
    section[...] = stage[...].astype(BF16)


def weight_kernel(info, own, other, *refs):
    outs = refs[:-1]
    both = refs[-1]
    core = info[2]
    for i in range(own.shape[0]):
        both[2 * i + core] = own[i]
        both[2 * i + 1 - core] = other[i]

    def rows(at, count):
        found = []
        done = 0
        while done < count:
            chunk, inner = divmod(at + done, WROWS)
            size = min(count - done, WROWS - inner)
            found.append(both[chunk, inner : inner + size, :])
            done += size
        return jnp.concatenate(found).astype(F32)

    conv, red, exp, height, width, chan, outw, squeeze, excite, sq_bias = outs[:10]
    for t in range(9):
        conv[t] = rows(AT_CONV + t * OUT, OUT)
    red[...] = rows(AT_REDUCE, FF)
    for j in range(FF // CH):
        exp[:, j * CH : (j + 1) * CH] = rows(AT_EXPAND + j * CH, CH)
    for at, ref in (
        (AT_HEIGHT, height),
        (AT_WIDTH, width),
        (AT_CHANNEL, chan),
        (AT_OUTPUT, outw),
    ):
        ref[...] = rows(at, CH)
    squeeze[...] = rows(AT_SQUEEZE, RED)
    for j in range(3):
        excite[:, j * CH : (j + 1) * CH] = rows(AT_EXCITE + j * RED, RED)
    same = lax.broadcasted_iota(jnp.int32, (RED, CH), 0) == lax.broadcasted_iota(
        jnp.int32, (RED, CH), 1
    )
    sq_bias[...] = jnp.sum(jnp.where(same, rows(AT_SQ_BIAS, RED), 0.0), axis=0)[0:RED]
    vectors = rows(AT_VECTOR, RED)
    for ref, row in zip(outs[10:], VECTOR_ROWS):
        size = ref.shape[0]
        for j in range(-(-size // CH)):
            width = min(CH, size - j * CH)
            ref[j * CH : j * CH + width] = vectors[row + j, 0:width]


def body(
    features,
    size_group,
    cycle_offsets,
    norm_gain,
    norm_bias,
    height_weight,
    height_bias,
    width_weight,
    width_bias,
    channel_weight,
    squeeze_weight,
    squeeze_bias,
    excite_weight,
    excite_bias,
    output_weight,
    output_bias,
    second_gain,
    second_bias,
    expand_weight,
    expand_bias,
    reduce_weight,
    reduce_bias,
    stride_weight,
    stride_bias,
    cotangent,
):
    shards = lax.axis_size("ch")
    rank = lax.axis_index("ch")
    side = SIDE - 4 * (2 - lax.dynamic_index_in_dim(size_group, rank, keepdims=False))
    info = jnp.stack([16 * (rank % 8), side, rank % 2]).astype(jnp.int32)
    vecs = jnp.concatenate(
        [
            v.astype(F32)
            for v in (
                norm_gain,
                norm_bias,
                height_bias,
                width_bias,
                output_bias,
                second_gain,
                second_bias,
                reduce_bias,
                expand_bias,
                excite_bias,
                cycle_offsets[0],
                cycle_offsets[1],
            )
        ]
    ).reshape(17, CH)

    whole = pl.BlockSpec(memory_space=pltpu.VMEM)
    chunks = pl.pallas_call(
        pack_kernel,
        cost_estimate=cost(2.5),
        out_shape=jax.ShapeDtypeStruct((shards, PIXROWS, LANES), BF16),
        in_specs=[pl.BlockSpec(memory_space=pltpu.HBM)] * 2,
        out_specs=whole,
        scratch_shapes=[
            pltpu.VMEM((shards * PIXROWS, LANES), F32),
            pltpu.VMEM(cotangent.shape, F32),
            pltpu.VMEM(features.shape, BF16),
            pltpu.VMEM(cotangent.shape, BF16),
            pltpu.SemaphoreType.DMA((2,)),
        ],
        compiler_params=params(56),
    )(features, cotangent)
    arrived = lax.all_to_all(chunks, "ch", split_axis=0, concat_axis=0, tiled=True)

    canvas = pltpu.VMEM((FLAT, CH), F32)
    guarded = pltpu.VMEM((FLAT + 2 * GUARD, CH), F32)
    narrow = pltpu.VMEM((FLAT, CH), BF16)
    kept, sent, grad, section_part = pl.pallas_call(
        main_kernel,
        cost_estimate=cost(22),
        out_shape=(
            jax.ShapeDtypeStruct((shards // 2, WROWS, LANES), F32),
            jax.ShapeDtypeStruct((shards // 2, WROWS, LANES), BF16),
            jax.ShapeDtypeStruct((FLAT, CH), F32),
            jax.ShapeDtypeStruct((OUT, OTILE * LANES), F32),
        ),
        in_specs=[pl.BlockSpec(memory_space=pltpu.SMEM)] + [whole] * 13,
        out_specs=(whole,) * 4,
        scratch_shapes=[
            pltpu.VMEM((CH, WIN * LANES), F32),
            pltpu.VMEM((3 * LANES, OTILE * LANES), F32),
            pltpu.VMEM((112 + WIN * LANES, CH), F32),
            canvas,
            canvas,
            canvas,
            canvas,
            guarded,
            narrow,
            narrow,
            narrow,
            canvas,
            canvas,
            canvas,
            narrow,
            canvas,
            canvas,
            narrow,
            pltpu.VMEM((FLAT, FF), BF16),
            pltpu.VMEM((FLAT, FF), F32),
            guarded,
            pltpu.VMEM((4, 360, CH), F32),
            pltpu.VMEM((OTILE * LANES, 9 * CH), BF16),
            pltpu.VMEM((OTILE * LANES, 9 * CH), F32),
            canvas,
            canvas,
            canvas,
            guarded,
            guarded,
            pltpu.VMEM((FLAT, FF), BF16),
            pltpu.VMEM((RED, CH), F32),
            pltpu.VMEM((2, shards // 2, WROWS, LANES), F32),
        ],
        compiler_params=params(42),
    )(
        info,
        arrived,
        vecs,
        squeeze_weight.astype(F32).T,
        squeeze_bias.astype(F32)[:, None],
        excite_weight.astype(F32),
        stride_bias.astype(F32)[:, None],
        height_weight,
        width_weight,
        channel_weight,
        output_weight,
        expand_weight,
        reduce_weight,
        stride_weight.reshape(OUT, 9 * CH),
    )
    other_core = [(i, i ^ 1) for i in range(shards)]
    same_core = [[2 * i + c for i in range(shards // 2)] for c in range(2)]
    met = lax.ppermute(sent, "ch", other_core)
    pixels = pl.pallas_call(
        send_kernel,
        cost_estimate=cost(2.5),
        out_shape=jax.ShapeDtypeStruct((shards, PIXROWS, LANES), BF16),
        in_specs=[pl.BlockSpec(memory_space=pltpu.SMEM)] + [whole] * 2,
        out_specs=whole,
        scratch_shapes=[
            pltpu.VMEM((112 + WIN * LANES, CH), F32),
            pltpu.VMEM((CH, WIN * LANES), F32),
            pltpu.VMEM((shards * PIXROWS, LANES), F32),
        ],
        compiler_params=params(8),
    )(info, grad, section_part)
    kept, pixels = lax.optimization_barrier((kept, pixels))
    partial = pl.pallas_call(
        pair_kernel,
        cost_estimate=cost(2.3),
        out_shape=jax.ShapeDtypeStruct(kept.shape, BF16),
        in_specs=[whole] * 2,
        out_specs=whole,
        compiler_params=params(3),
    )(kept, met)

    def exchange(v):
        return lax.all_to_all(
            v, "ch", split_axis=0, concat_axis=0, tiled=True, axis_index_groups=same_core
        )

    parts = exchange(partial)
    parts, pixels = lax.optimization_barrier((parts, pixels))
    back = exchange(pixels.reshape(shards // 2, 2, PIXROWS, LANES))

    mine = pl.pallas_call(
        add_kernel,
        cost_estimate=cost(1.7),
        out_shape=jax.ShapeDtypeStruct((WROWS, LANES), BF16),
        compiler_params=params(2),
    )(parts)
    groups = lax.axis_size("img")
    other = [
        lax.ppermute(mine, "img", [(i, (i + d) % groups) for i in range(groups)])
        for d in (1, 2, 3)
    ]
    copies = pl.pallas_call(
        copies_kernel,
        cost_estimate=cost(1.7),
        in_specs=[whole] * 4,
        out_specs=whole,
        out_shape=jax.ShapeDtypeStruct((shards // 2, WROWS, LANES), BF16),
        compiler_params=params(2),
    )(mine, *other)
    copies, back = lax.optimization_barrier((copies, back))
    own_half = exchange(copies)
    core = rank % 2
    near = lax.dynamic_index_in_dim(back, core, axis=1, keepdims=False)
    far = lax.dynamic_index_in_dim(back, 1 - core, axis=1, keepdims=False)
    far = lax.ppermute(far, "ch", other_core)

    features_grad, section = pl.pallas_call(
        pixel_kernel,
        cost_estimate=cost(2.5),
        out_shape=(
            jax.ShapeDtypeStruct(features.shape, F32),
            jax.ShapeDtypeStruct(cotangent.shape, BF16),
        ),
        in_specs=[pl.BlockSpec(memory_space=pltpu.SMEM)] + [whole] * 2,
        out_specs=(whole,) * 2,
        scratch_shapes=[
            pltpu.VMEM(cotangent.shape, F32),
            pltpu.VMEM((shards, PIXROWS, LANES), BF16),
        ],
        compiler_params=params(5),
    )(info, near, far)

    own_half, features_grad, section = lax.optimization_barrier((own_half, features_grad, section))
    other_half = lax.ppermute(own_half, "ch", other_core)

    def like(*shape):
        return jax.ShapeDtypeStruct(shape, F32)

    (
        conv_grad,
        reduce_grad,
        expand_grad,
        height_grad,
        width_grad,
        channel_grad,
        output_grad,
        squeeze_grad,
        excite_grad,
        squeeze_bias_grad,
        norm_gain_grad,
        norm_bias_grad,
        height_bias_grad,
        width_bias_grad,
        output_bias_grad,
        second_gain_grad,
        second_bias_grad,
        reduce_bias_grad,
        expand_bias_grad,
        excite_bias_grad,
        conv_bias_grad,
    ) = pl.pallas_call(
        weight_kernel,
        cost_estimate=cost(2.8),
        out_shape=(
            like(9, OUT, CH),
            like(FF, CH),
            like(CH, FF),
            like(CH, CH),
            like(CH, CH),
            like(CH, CH),
            like(CH, CH),
            like(RED, CH),
            like(RED, 3 * CH),
            like(RED),
        )
        + tuple(like(size) for size in VECTOR_SIZES),
        in_specs=[pl.BlockSpec(memory_space=pltpu.SMEM)] + [whole] * 2,
        out_specs=(whole,) * 21,
        scratch_shapes=[pltpu.VMEM((shards, WROWS, LANES), BF16)],
        compiler_params=params(6),
    )(info, own_half, other_half)
    return (
        section,
        features_grad,
        norm_gain_grad,
        norm_bias_grad,
        height_grad,
        height_bias_grad,
        width_grad,
        width_bias_grad,
        channel_grad,
        squeeze_grad.T,
        squeeze_bias_grad,
        excite_grad,
        excite_bias_grad,
        output_grad,
        output_bias_grad,
        second_gain_grad,
        second_bias_grad,
        expand_grad,
        expand_bias_grad,
        reduce_grad,
        reduce_bias_grad,
        jnp.transpose(conv_grad, (1, 0, 2)),
        conv_bias_grad,
    )


def solution(mesh):
    split = P("ch", "img")
    return jax.shard_map(
        body,
        mesh=mesh,
        in_specs=(split, P("img")) + (P(),) * 22 + (split,),
        out_specs=(split, split) + (P(),) * 21,
        check_vma=False,
    )
```

```python
import jax
import jax.numpy as jnp
from jax import lax
from jax.experimental import pallas as pl
from jax.experimental.pallas import tpu as pltpu
from jax.sharding import PartitionSpec as P

CH = 128
FF = 512
RED = 32
OUT = 320
SIDE = 36
PIX = SIDE * SIDE
HALF = SIDE // 2
OPIX = HALF * HALF
WIDE = 40
FLAT = SIDE * WIDE
GUARD = 48
EPS = 1e-05
LANES = 128
WIN = 11
OTILE = 3
PIXROWS = 80
WROWS = 144

F32 = jnp.float32
BF16 = jnp.bfloat16

CHIPS = (1, 6, 8, 9, 13, 4, 2, 14, 10, 7, 15, 11, 3, 0, 5, 12)

AT_CONV = 0
AT_REDUCE = 2880
AT_EXPAND = 3392
AT_HEIGHT = 3904
AT_WIDTH = 4032
AT_CHANNEL = 4160
AT_OUTPUT = 4288
AT_SQUEEZE = 4416
AT_EXCITE = 4448
AT_SQ_BIAS = 4544
AT_VECTOR = 4576
VECTOR_ROWS = (0, 1, 2, 3, 4, 5, 6, 7, 8, 12, 15)
VECTOR_SIZES = (CH,) * 8 + (FF, 3 * CH, OUT)


def params(mebibytes):
    return pltpu.CompilerParams(vmem_limit_bytes=mebibytes * 1024 * 1024)


def cost(micros):
    return pl.CostEstimate(flops=0, bytes_accessed=int(micros * 3.69e6), transcendentals=0)


def first_tile(k):
    return 10 * k + k // 8


def nn(a, b):
    return lax.dot_general(a, b, (((1,), (0,)), ((), ())), preferred_element_type=F32)


def nt(a, b):
    return lax.dot_general(a, b, (((1,), (1,)), ((), ())), preferred_element_type=F32)


def tn(a, b):
    return lax.dot_general(a, b, (((0,), (0,)), ((), ())), preferred_element_type=F32)


def lane_mean(v):
    return jnp.sum(v, axis=1, keepdims=True) * (1.0 / CH)


def col_sum(v):
    return jnp.sum(v, axis=0, keepdims=True)


def normal_parts(x):
    cdf = 0.5 + 0.5 * lax.erf(x * 0.7071067811865476)
    return cdf, (x * 0.3989422804014327) * jnp.exp(x * (x * -0.5))


def pack_kernel(feat_hbm, cot_hbm, out, stage, cots, feat, cot, ready):
    images = out.shape[0]
    first = pltpu.make_async_copy(feat_hbm, feat, ready.at[0])
    second = pltpu.make_async_copy(cot_hbm, cot, ready.at[1])
    first.start()
    second.start()
    first.wait()
    for k in range(images):
        base = k * PIXROWS
        begin = first_tile(k) * LANES
        for t in range(WIN):
            stage[base + 4 * t : base + 4 * t + 4, :] = feat[
                :, begin + t * LANES : begin + (t + 1) * LANES
            ].astype(F32)
    second.wait()
    cots[...] = cot[...].astype(F32)
    for k in range(images):
        base = k * PIXROWS
        for j in range(OTILE):
            width = min(LANES, OPIX - j * LANES)
            at = k * OPIX + j * LANES
            row = base + 44 + 10 * j
            stage[row : row + 10, 0:width] = cots[:, at : at + width]
        out[k] = stage[base : base + PIXROWS, :].astype(BF16)


def main_kernel(
    info,
    recv,
    vecs,
    sqt,
    sqb,
    exw,
    kbias,
    hw,
    ww,
    cw,
    ow,
    xw,
    rw,
    kw,
    keep_out,
    send_out,
    grad,
    section_out,
    xf,
    cf,
    tall,
    canvas,
    valid,
    xhat,
    rstd,
    norm,
    rows_b,
    cols_b,
    norm_b,
    branch_h,
    branch_w,
    branch_c,
    mixed_b,
    xhat2,
    rstd2,
    norm2_b,
    hidden_b,
    slope,
    block,
    planes,
    taps,
    spread,
    gblock,
    gresid,
    gmixed,
    grows,
    gcols,
    gpre_b,
    sums,
    rows_out,
):
    shift = info[0]
    side = info[1]
    core = info[2]

    def vec(i):
        return vecs[i : i + 1, :]

    def put(row, value):
        count = value.shape[0]
        done = 0
        while done < count:
            chunk, inner = divmod(row + done, WROWS)
            size = min(count - done, WROWS - inner)
            slot = core if chunk % 2 == 0 else 1 - core
            rows_out[slot, chunk // 2, inner : inner + size, :] = value[done : done + size, :]
            done += size

    def total_of(row, value):
        sums[row : row + 1, :] = col_sum(value)

    cf[OUT:, :] = jnp.zeros((cf.shape[0] - OUT, cf.shape[1]), F32)
    for s in range(recv.shape[0]):
        piece = recv[s].astype(F32)
        for t in range(WIN):
            xf[4 * s : 4 * s + 4, t * LANES : (t + 1) * LANES] = piece[4 * t : 4 * t + 4, :]
        for j in range(OTILE):
            cf[10 * s : 10 * s + 10, j * LANES : (j + 1) * LANES] = piece[
                44 + 10 * j : 54 + 10 * j, :
            ]
    begin = pl.multiple_of(112 - shift, 16)
    for t in range(WIN):
        tall[pl.ds(begin + t * LANES, LANES), :] = xf[:, t * LANES : (t + 1) * LANES].T

    column = lax.broadcasted_iota(jnp.int32, (WIDE, CH), 0)
    for r in range(SIDE):
        keep = (column < side) & (r < side)
        canvas[r * WIDE : (r + 1) * WIDE, :] = jnp.where(
            keep, tall[112 + r * SIDE : 112 + r * SIDE + WIDE, :], 0.0
        )
        valid[r * WIDE : (r + 1) * WIDE, :] = jnp.where(keep, 1.0, 0.0)
    edge = jnp.zeros((GUARD, CH), F32)
    for ref in (norm, block, grows, gcols):
        ref[0:GUARD, :] = edge
        ref[GUARD + FLAT : FLAT + 2 * GUARD, :] = edge
    sums[...] = jnp.zeros_like(sums)

    def moved(ref, by):
        return ref[GUARD + by : GUARD + by + FLAT, :]

    x = canvas[...]
    center = x - lane_mean(x)
    scale = lax.rsqrt(lane_mean(center * center) + EPS)
    unit = center * scale
    xhat[...] = unit
    rstd[...] = jnp.broadcast_to(scale, unit.shape)
    value = jnp.where(valid[...] > 0, unit * vec(0) + vec(1), 0.0)
    norm[GUARD : GUARD + FLAT, :] = value.astype(BF16).astype(F32)

    by_row = vec(15)
    by_col = vec(16)
    plain = moved(norm, 0)
    rows_b[...] = jnp.where(
        by_row < 0, moved(norm, -WIDE), jnp.where(by_row > 0, moved(norm, WIDE), plain)
    ).astype(BF16)
    cols_b[...] = jnp.where(
        by_col < 0, moved(norm, -1), jnp.where(by_col > 0, moved(norm, 1), plain)
    ).astype(BF16)
    norm_b[...] = plain.astype(BF16)
    bh = nn(rows_b[...], hw[...]) + vec(2)
    bw = nn(cols_b[...], ww[...]) + vec(3)
    bc = nn(norm_b[...], cw[...])
    branch_h[...] = bh
    branch_w[...] = bw
    branch_c[...] = bc
    total = col_sum(valid[...] * (bh + bw + bc))

    index = lax.broadcasted_iota(jnp.int32, (1, OTILE * LANES), 1)
    lane_row = ((index.astype(F32) + 0.5) * (1.0 / HALF)).astype(jnp.int32)
    lane_col = index - lane_row * HALF
    out_keep = (2 * lane_row < side) & (2 * lane_col < side)
    cot = jnp.where(out_keep, cf[...], 0.0)
    cot_b = cot[0:OUT, :].astype(BF16)
    cot_t = cot.T.astype(BF16)[:, 0:OUT]
    kb_rows = jnp.sum(cot, axis=1, keepdims=True)
    spread[...] = nn(cot_t, kw[...])
    count = jnp.full((1, CH), side * side, jnp.int32).astype(F32)
    means = total / count
    inner_pre = jnp.sum(sqt[...] * means, axis=1, keepdims=True) + sqb[...]
    inner_cdf, inner_density = normal_parts(inner_pre)
    inner = inner_pre * inner_cdf
    inner_slope = inner_cdf + inner_density
    logit = [col_sum(exw[:, j * CH : (j + 1) * CH] * inner) + vec(12 + j) for j in range(3)]
    top = jnp.maximum(jnp.maximum(logit[0], logit[1]), logit[2])
    grown = [jnp.exp(v - top) for v in logit]
    whole = grown[0] + grown[1] + grown[2]
    mix = [v / whole for v in grown]

    mixed = mix[0] * branch_h[...] + mix[1] * branch_w[...] + mix[2] * branch_c[...]
    mixed_b[...] = mixed.astype(BF16)
    resid = canvas[...] + nn(mixed_b[...], ow[...]) + vec(4)
    center = resid - lane_mean(resid)
    scale = lax.rsqrt(lane_mean(center * center) + EPS)
    unit = center * scale
    xhat2[...] = unit
    rstd2[...] = jnp.broadcast_to(scale, unit.shape)
    norm2_b[...] = (unit * vec(5) + vec(6)).astype(BF16)
    used = 336
    row_id = lax.broadcasted_iota(jnp.int32, (used, CH), 0)
    row_of = ((row_id.astype(F32) + 0.5) * (1.0 / HALF)).astype(jnp.int32)
    out_column = row_id - row_of * HALF
    inside = out_column[0:OPIX, :] < HALF - 1

    def part(tap, ahead, masked):
        value = spread[ahead : ahead + OPIX, tap * CH : (tap + 1) * CH]
        return jnp.where(inside, value, 0.0) if masked else value

    found = (
        part(4, 0, False),
        part(5, 0, False) + part(3, 1, True),
        part(7, 0, False) + part(1, HALF, False),
        (part(8, 0, False) + part(6, 1, True)) + (part(2, HALF, False) + part(0, HALF + 1, True)),
    )
    for p in range(4):
        planes[p, 0:OPIX, :] = found[p]
        for i in range(HALF):
            at = (2 * i + p // 2) * WIDE + p % 2
            gblock[pl.ds(at, HALF, stride=2), :] = planes[p, i * HALF : (i + 1) * HALF, :]

    through = resid + vec(7)
    for j in range(FF // CH):
        lanes = slice(j * CH, (j + 1) * CH)
        pre = nn(norm2_b[...], xw[:, lanes]) + vec(8 + j)
        cdf, density = normal_parts(pre)
        hidden_b[:, lanes] = (pre * cdf).astype(BF16)
        slope[:, lanes] = cdf + density
    through = through + nn(hidden_b[...], rw[...])
    value = jnp.where(valid[...] > 0, through, 0.0)
    block[GUARD : GUARD + FLAT, :] = value.astype(BF16).astype(F32)

    top_rows = 24
    for p in range(4):
        planes[p, 0:top_rows, :] = jnp.zeros((top_rows, CH), F32)
        planes[p, top_rows + OPIX :, :] = jnp.zeros((planes.shape[1] - top_rows - OPIX, CH), F32)
        for i in range(HALF):
            at = GUARD + (2 * i + p // 2) * WIDE + p % 2
            row = top_rows + i * HALF
            planes[p, row : row + HALF, :] = block[pl.ds(at, HALF, stride=2), :]
    for a in range(3):
        for b in range(3):
            plane = 2 * ((a + 1) % 2) + (b + 1) % 2
            row = top_rows - HALF * (a == 0) - (b == 0)
            value = planes[plane, row : row + used, :]
            if b == 0:
                value = jnp.where(out_column > 0, value, 0.0)
            taps[0:used, (3 * a + b) * CH : (3 * a + b + 1) * CH] = value.astype(BF16)
    taps[used:, :] = jnp.zeros((taps.shape[0] - used, taps.shape[1]), BF16)
    gb = jnp.where(valid[...] > 0, gblock[...], 0.0)
    gred = gb.astype(BF16)
    total_of(7, gred.astype(F32))
    for j in range(FF // (2 * CH)):
        lanes = slice(2 * j * CH, 2 * (j + 1) * CH)
        gpre = (nt(gred, rw[lanes, :]) * slope[:, lanes]).astype(BF16)
        total_of(8 + 2 * j, gpre[:, 0:CH].astype(F32))
        total_of(9 + 2 * j, gpre[:, CH:].astype(F32))
        gpre_b[:, lanes] = gpre
    gn2 = nt(gpre_b[...], xw[...])
    conv = nn(cot_b, taps[...])
    for t in range(9):
        put(AT_CONV + t * OUT, conv[:, t * CH : (t + 1) * CH])
    unit = xhat2[...]
    total_of(5, gn2 * unit)
    total_of(6, gn2)
    gy = gn2 * vec(5)
    gr = gb + rstd2[...] * (gy - lane_mean(gy) - unit * lane_mean(gy * unit))
    gresid[...] = gr
    gproj = gr.astype(BF16)
    total_of(4, gproj.astype(F32))
    grown = tn(gred, hidden_b[...])
    for j in range(FF // CH):
        put(AT_REDUCE + j * CH, grown[:, j * CH : (j + 1) * CH].T)
    gm = nt(gproj, ow[...])
    gmixed[...] = gm
    section = nt(kw[...], taps[...]) + kbias[...]
    section_out[...] = jnp.where(out_keep, section, 0.0)
    gmix = [col_sum(gm * branch[...]) for branch in (branch_h, branch_w, branch_c)]
    put(AT_OUTPUT, tn(mixed_b[...], gproj))
    inner_dot = mix[0] * gmix[0] + mix[1] * gmix[1] + mix[2] * gmix[2]
    glogit = [mix[j] * (gmix[j] - inner_dot) for j in range(3)]
    ginner = jnp.zeros((RED, 1), F32)
    for j in range(3):
        ginner += jnp.sum(exw[:, j * CH : (j + 1) * CH] * glogit[j], axis=1, keepdims=True)
        put(AT_EXCITE + RED * j, inner * glogit[j])
        sums[12 + j : 13 + j, :] = glogit[j]
    ginner = ginner * inner_slope
    put(AT_SQUEEZE, ginner * means)
    put(AT_SQ_BIAS, jnp.broadcast_to(ginner, (RED, CH)))
    gmeans = col_sum(sqt[...] * ginner) / count

    gm = gmixed[...]
    level = valid[...] * gmeans
    gh = (mix[0] * gm + level).astype(BF16)
    gw = (mix[1] * gm + level).astype(BF16)
    gc = (mix[2] * gm + level).astype(BF16)
    total_of(2, gh.astype(F32))
    total_of(3, gw.astype(F32))
    grown = tn(norm2_b[...], gpre_b[...])
    for j in range(FF // CH):
        put(AT_EXPAND + j * CH, grown[:, j * CH : (j + 1) * CH])
    grows[GUARD : GUARD + FLAT, :] = nt(gh, hw[...])
    gcols[GUARD : GUARD + FLAT, :] = nt(gw, ww[...])
    value = nt(gc, cw[...])
    put(AT_HEIGHT, tn(rows_b[...], gh))
    put(AT_WIDTH, tn(cols_b[...], gw))
    put(AT_CHANNEL, tn(norm_b[...], gc))
    value = value + jnp.where(
        by_row < 0,
        moved(grows, WIDE),
        jnp.where(by_row > 0, moved(grows, -WIDE), moved(grows, 0)),
    )
    value = value + jnp.where(
        by_col < 0, moved(gcols, 1), jnp.where(by_col > 0, moved(gcols, -1), moved(gcols, 0))
    )
    keep = valid[...] > 0
    value = jnp.where(keep, value, 0.0)
    unit = xhat[...]
    total_of(0, value * unit)
    total_of(1, value)
    gy = value * vec(0)
    back = rstd[...] * (gy - lane_mean(gy) - unit * lane_mean(gy * unit))
    grad[...] = jnp.where(keep, gresid[...] + back, 0.0)

    same = lax.broadcasted_iota(jnp.int32, (LANES, LANES), 0) == lax.broadcasted_iota(
        jnp.int32, (LANES, LANES), 1
    )
    for j in range(OTILE):
        total_of(15 + j, jnp.where(same, kb_rows[j * LANES : (j + 1) * LANES, :], 0.0))
    put(AT_VECTOR, sums[...])
    keep_out[...] = rows_out[0]
    send_out[...] = rows_out[1].astype(BF16)


def send_kernel(info, grad, section, out, tall, turned, stage):
    begin = pl.multiple_of(112 - info[0], 16)
    tall[0:112, :] = jnp.zeros((112, CH), F32)
    tall[112 + PIX :, :] = jnp.zeros((tall.shape[0] - 112 - PIX, CH), F32)
    for r in range(SIDE):
        tall[112 + r * SIDE : 112 + (r + 1) * SIDE, :] = grad[r * WIDE : r * WIDE + SIDE, :]
    for t in range(WIN):
        turned[:, t * LANES : (t + 1) * LANES] = tall[pl.ds(begin + t * LANES, LANES), :].T
    for s in range(out.shape[0]):
        base = s * PIXROWS
        for t in range(WIN):
            stage[base + 4 * t : base + 4 * t + 4, :] = turned[
                4 * s : 4 * s + 4, t * LANES : (t + 1) * LANES
            ]
        for j in range(OTILE):
            stage[base + 44 + 10 * j : base + 54 + 10 * j, :] = section[
                10 * s : 10 * s + 10, j * LANES : (j + 1) * LANES
            ]
        out[2 * CHIPS.index(s // 2) + s % 2] = stage[base : base + PIXROWS, :].astype(BF16)


def pair_kernel(kept, met, out):
    out[...] = (kept[...] + met[...].astype(F32)).astype(BF16)


def add_kernel(recv, out):
    total = recv[0].astype(F32)
    for s in range(1, recv.shape[0]):
        total += recv[s].astype(F32)
    out[...] = total.astype(BF16)


def copies_kernel(mine, one, two, three, out):
    total = (mine[...].astype(F32) + two[...].astype(F32)) + (
        one[...].astype(F32) + three[...].astype(F32)
    )
    total = total.astype(BF16)
    for s in range(out.shape[0]):
        out[s] = total


def pixel_kernel(info, near, far, feat, section, stage, recv):
    core = info[2]
    for i in range(near.shape[0]):
        recv[2 * CHIPS[i] + core] = near[i]
        recv[2 * CHIPS[i] + 1 - core] = far[i]
    for k in range(recv.shape[0]):
        piece = recv[k].astype(F32)
        tile = first_tile(k)
        for t in range(WIN):
            lanes = slice((tile + t) * LANES, (tile + t + 1) * LANES)
            value = piece[4 * t : 4 * t + 4, :]
            if t == 0 and k % 8:
                feat[:, lanes] += value
            else:
                feat[:, lanes] = value
        for j in range(OTILE):
            width = min(LANES, OPIX - j * LANES)
            at = k * OPIX + j * LANES
            stage[:, at : at + width] = piece[44 + 10 * j : 54 + 10 * j, 0:width]
    section[...] = stage[...].astype(BF16)


def weight_kernel(info, own, other, *refs):
    outs = refs[:-1]
    both = refs[-1]
    core = info[2]
    for i in range(own.shape[0]):
        both[2 * i + core] = own[i]
        both[2 * i + 1 - core] = other[i]

    def rows(at, count):
        found = []
        done = 0
        while done < count:
            chunk, inner = divmod(at + done, WROWS)
            size = min(count - done, WROWS - inner)
            found.append(both[chunk, inner : inner + size, :])
            done += size
        return jnp.concatenate(found).astype(F32)

    conv, red, exp, height, width, chan, outw, squeeze, excite, sq_bias = outs[:10]
    for t in range(9):
        conv[t] = rows(AT_CONV + t * OUT, OUT)
    red[...] = rows(AT_REDUCE, FF)
    for j in range(FF // CH):
        exp[:, j * CH : (j + 1) * CH] = rows(AT_EXPAND + j * CH, CH)
    for at, ref in (
        (AT_HEIGHT, height),
        (AT_WIDTH, width),
        (AT_CHANNEL, chan),
        (AT_OUTPUT, outw),
    ):
        ref[...] = rows(at, CH)
    squeeze[...] = rows(AT_SQUEEZE, RED)
    for j in range(3):
        excite[:, j * CH : (j + 1) * CH] = rows(AT_EXCITE + j * RED, RED)
    same = lax.broadcasted_iota(jnp.int32, (RED, CH), 0) == lax.broadcasted_iota(
        jnp.int32, (RED, CH), 1
    )
    sq_bias[...] = jnp.sum(jnp.where(same, rows(AT_SQ_BIAS, RED), 0.0), axis=0)[0:RED]
    vectors = rows(AT_VECTOR, RED)
    for ref, row in zip(outs[10:], VECTOR_ROWS):
        size = ref.shape[0]
        for j in range(-(-size // CH)):
            width = min(CH, size - j * CH)
            ref[j * CH : j * CH + width] = vectors[row + j, 0:width]


def body(
    features,
    size_group,
    cycle_offsets,
    norm_gain,
    norm_bias,
    height_weight,
    height_bias,
    width_weight,
    width_bias,
    channel_weight,
    squeeze_weight,
    squeeze_bias,
    excite_weight,
    excite_bias,
    output_weight,
    output_bias,
    second_gain,
    second_bias,
    expand_weight,
    expand_bias,
    reduce_weight,
    reduce_bias,
    stride_weight,
    stride_bias,
    cotangent,
):
    shards = lax.axis_size("ch")
    rank = lax.axis_index("ch")
    side = SIDE - 4 * (2 - lax.dynamic_index_in_dim(size_group, rank, keepdims=False))
    info = jnp.stack([16 * (rank % 8), side, rank % 2]).astype(jnp.int32)
    vecs = jnp.concatenate(
        [
            v.astype(F32)
            for v in (
                norm_gain,
                norm_bias,
                height_bias,
                width_bias,
                output_bias,
                second_gain,
                second_bias,
                reduce_bias,
                expand_bias,
                excite_bias,
                cycle_offsets[0],
                cycle_offsets[1],
            )
        ]
    ).reshape(17, CH)

    whole = pl.BlockSpec(memory_space=pltpu.VMEM)
    chunks = pl.pallas_call(
        pack_kernel,
        cost_estimate=cost(2.5),
        out_shape=jax.ShapeDtypeStruct((shards, PIXROWS, LANES), BF16),
        in_specs=[pl.BlockSpec(memory_space=pltpu.HBM)] * 2,
        out_specs=whole,
        scratch_shapes=[
            pltpu.VMEM((shards * PIXROWS, LANES), F32),
            pltpu.VMEM(cotangent.shape, F32),
            pltpu.VMEM(features.shape, BF16),
            pltpu.VMEM(cotangent.shape, BF16),
            pltpu.SemaphoreType.DMA((2,)),
        ],
        compiler_params=params(56),
    )(features, cotangent)
    arrived = lax.all_to_all(chunks, "ch", split_axis=0, concat_axis=0, tiled=True)

    canvas = pltpu.VMEM((FLAT, CH), F32)
    guarded = pltpu.VMEM((FLAT + 2 * GUARD, CH), F32)
    narrow = pltpu.VMEM((FLAT, CH), BF16)
    kept, sent, grad, section_part = pl.pallas_call(
        main_kernel,
        cost_estimate=cost(22),
        out_shape=(
            jax.ShapeDtypeStruct((shards // 2, WROWS, LANES), F32),
            jax.ShapeDtypeStruct((shards // 2, WROWS, LANES), BF16),
            jax.ShapeDtypeStruct((FLAT, CH), F32),
            jax.ShapeDtypeStruct((OUT, OTILE * LANES), F32),
        ),
        in_specs=[pl.BlockSpec(memory_space=pltpu.SMEM)] + [whole] * 13,
        out_specs=(whole,) * 4,
        scratch_shapes=[
            pltpu.VMEM((CH, WIN * LANES), F32),
            pltpu.VMEM((3 * LANES, OTILE * LANES), F32),
            pltpu.VMEM((112 + WIN * LANES, CH), F32),
            canvas,
            canvas,
            canvas,
            canvas,
            guarded,
            narrow,
            narrow,
            narrow,
            canvas,
            canvas,
            canvas,
            narrow,
            canvas,
            canvas,
            narrow,
            pltpu.VMEM((FLAT, FF), BF16),
            pltpu.VMEM((FLAT, FF), F32),
            guarded,
            pltpu.VMEM((4, 360, CH), F32),
            pltpu.VMEM((OTILE * LANES, 9 * CH), BF16),
            pltpu.VMEM((OTILE * LANES, 9 * CH), F32),
            canvas,
            canvas,
            canvas,
            guarded,
            guarded,
            pltpu.VMEM((FLAT, FF), BF16),
            pltpu.VMEM((RED, CH), F32),
            pltpu.VMEM((2, shards // 2, WROWS, LANES), F32),
        ],
        compiler_params=params(42),
    )(
        info,
        arrived,
        vecs,
        squeeze_weight.astype(F32).T,
        squeeze_bias.astype(F32)[:, None],
        excite_weight.astype(F32),
        stride_bias.astype(F32)[:, None],
        height_weight,
        width_weight,
        channel_weight,
        output_weight,
        expand_weight,
        reduce_weight,
        stride_weight.reshape(OUT, 9 * CH),
    )
    other_core = [(i, i ^ 1) for i in range(shards)]
    same_core = [[2 * i + c for i in CHIPS] for c in range(2)]
    met = lax.ppermute(sent, "ch", other_core)
    pixels = pl.pallas_call(
        send_kernel,
        cost_estimate=cost(2.5),
        out_shape=jax.ShapeDtypeStruct((shards, PIXROWS, LANES), BF16),
        in_specs=[pl.BlockSpec(memory_space=pltpu.SMEM)] + [whole] * 2,
        out_specs=whole,
        scratch_shapes=[
            pltpu.VMEM((112 + WIN * LANES, CH), F32),
            pltpu.VMEM((CH, WIN * LANES), F32),
            pltpu.VMEM((shards * PIXROWS, LANES), F32),
        ],
        compiler_params=params(8),
    )(info, grad, section_part)
    kept, pixels = lax.optimization_barrier((kept, pixels))
    partial = pl.pallas_call(
        pair_kernel,
        cost_estimate=cost(2.3),
        out_shape=jax.ShapeDtypeStruct(kept.shape, BF16),
        in_specs=[whole] * 2,
        out_specs=whole,
        compiler_params=params(3),
    )(kept, met)

    def exchange(v):
        return lax.all_to_all(
            v, "ch", split_axis=0, concat_axis=0, tiled=True, axis_index_groups=same_core
        )

    parts = exchange(partial)
    parts, pixels = lax.optimization_barrier((parts, pixels))
    back = exchange(pixels.reshape(shards // 2, 2, PIXROWS, LANES))

    mine = pl.pallas_call(
        add_kernel,
        cost_estimate=cost(1.7),
        out_shape=jax.ShapeDtypeStruct((WROWS, LANES), BF16),
        compiler_params=params(2),
    )(parts)
    groups = lax.axis_size("img")
    other = [
        lax.ppermute(mine, "img", [(i, (i + d) % groups) for i in range(groups)])
        for d in (1, 2, 3)
    ]
    copies = pl.pallas_call(
        copies_kernel,
        cost_estimate=cost(1.7),
        in_specs=[whole] * 4,
        out_specs=whole,
        out_shape=jax.ShapeDtypeStruct((shards // 2, WROWS, LANES), BF16),
        compiler_params=params(2),
    )(mine, *other)
    copies, back = lax.optimization_barrier((copies, back))
    own_half = exchange(copies)
    core = rank % 2
    near = lax.dynamic_index_in_dim(back, core, axis=1, keepdims=False)
    far = lax.dynamic_index_in_dim(back, 1 - core, axis=1, keepdims=False)
    far = lax.ppermute(far, "ch", other_core)

    features_grad, section = pl.pallas_call(
        pixel_kernel,
        cost_estimate=cost(2.5),
        out_shape=(
            jax.ShapeDtypeStruct(features.shape, F32),
            jax.ShapeDtypeStruct(cotangent.shape, BF16),
        ),
        in_specs=[pl.BlockSpec(memory_space=pltpu.SMEM)] + [whole] * 2,
        out_specs=(whole,) * 2,
        scratch_shapes=[
            pltpu.VMEM(cotangent.shape, F32),
            pltpu.VMEM((shards, PIXROWS, LANES), BF16),
        ],
        compiler_params=params(5),
    )(info, near, far)

    own_half, features_grad, section = lax.optimization_barrier((own_half, features_grad, section))
    other_half = lax.ppermute(own_half, "ch", other_core)

    def like(*shape):
        return jax.ShapeDtypeStruct(shape, F32)

    (
        conv_grad,
        reduce_grad,
        expand_grad,
        height_grad,
        width_grad,
        channel_grad,
        output_grad,
        squeeze_grad,
        excite_grad,
        squeeze_bias_grad,
        norm_gain_grad,
        norm_bias_grad,
        height_bias_grad,
        width_bias_grad,
        output_bias_grad,
        second_gain_grad,
        second_bias_grad,
        reduce_bias_grad,
        expand_bias_grad,
        excite_bias_grad,
        conv_bias_grad,
    ) = pl.pallas_call(
        weight_kernel,
        cost_estimate=cost(2.8),
        out_shape=(
            like(9, OUT, CH),
            like(FF, CH),
            like(CH, FF),
            like(CH, CH),
            like(CH, CH),
            like(CH, CH),
            like(CH, CH),
            like(RED, CH),
            like(RED, 3 * CH),
            like(RED),
        )
        + tuple(like(size) for size in VECTOR_SIZES),
        in_specs=[pl.BlockSpec(memory_space=pltpu.SMEM)] + [whole] * 2,
        out_specs=(whole,) * 21,
        scratch_shapes=[pltpu.VMEM((shards, WROWS, LANES), BF16)],
        compiler_params=params(6),
    )(info, own_half, other_half)
    return (
        section,
        features_grad,
        norm_gain_grad,
        norm_bias_grad,
        height_grad,
        height_bias_grad,
        width_grad,
        width_bias_grad,
        channel_grad,
        squeeze_grad.T,
        squeeze_bias_grad,
        excite_grad,
        excite_bias_grad,
        output_grad,
        output_bias_grad,
        second_gain_grad,
        second_bias_grad,
        expand_grad,
        expand_bias_grad,
        reduce_grad,
        reduce_bias_grad,
        jnp.transpose(conv_grad, (1, 0, 2)),
        conv_bias_grad,
    )


def solution(mesh):
    split = P("ch", "img")
    return jax.shard_map(
        body,
        mesh=mesh,
        in_specs=(split, P("img")) + (P(),) * 22 + (split,),
        out_specs=(split, split) + (P(),) * 21,
        check_vma=False,
    )
```
